256 devices in a mesh: leaf: 256 (over x, z, y, core).
Axes of the slice: x: 4, y: 4, z: 8, core: 2. Of those that a mesh axis runs over, the one named last changes fastest.
Arguments:
- cotangent: float32 [2, 64, 65536], P(None, None, 'leaf'), may hold values from -30 to 30
- nodal_mass: float32 [64, 65536], P(None, 'leaf'), may hold values from 0.5 to 2
- curvature: float32 [64, 65536], P(None, 'leaf'), may hold values from -1 to 2
- stiffness: float32 [64, 64], replicated, may hold values from -0.75 to 0.75
- levels: int32 [65536], P('leaf'), may hold values from 0 to 3
- neighbours: int32 [6, 65536], P(None, 'leaf'), may hold values from -1 to 65535, as said below
- mortars: int32 [6, 32768], P(None, 'leaf'), may hold values from -1 to 65535, as said below
Outputs:
- adjoint: float32 [2, 64, 65536], P(None, None, 'leaf')
The draws below stay inside these ranges and needn't reach their ends.
Inputs may be any that keep to these rules, and one draw needn't show every extreme that they name: For each a of 0, 1, 2: neighbours[2 a + 1, i] = j >= 0 exactly when neighbours[2 a, j] = i. Every neighbour belongs to the same, the previous or the next device's block of 256 leaves. `mortars`: on each device's 128 slots the used ones come first; an unused slot holds -1 in all six rows. A used slot has a face of 0 to 5, a coarse leaf of the same device and fine leaves of the same, the previous or the next device. On some device all 128 slots are used.
All inputs are finite; a program needn't handle non-finite values.
Results may differ from the reference program's by a relative error of at most 0.002.
Values sent between devices are 32-bit elements; how exact they have to be, the bound alone decides.
No kernel may reach another device: no remote copies, remote signals or barrier semaphores. Data moves between devices by JAX's collectives and lax.ppermute only.
A program may use at most 128 MiB of HBM per device.

```python
import math
import jax
import jax.numpy as jnp
import numpy as np
from jax import lax

FIELDS = 2
NODES = 64
LEAVES_DEV = 256
MORT_DEV = 128
LEAVES = 65536
MORTARS = 32768


def draw_neighbours(key, part):
    key = jax.random.fold_in(key, 11)
    devices_here = LEAVES // LEAVES_DEV
    every_leaf = jnp.arange(LEAVES, dtype=jnp.int32)
    length = (devices_here - 1) * LEAVES_DEV
    rows = []
    for axis_id in range(3):
        start_at = (axis_id + 1) * LEAVES_DEV // 4
        subkey = jax.random.fold_in(key, axis_id)
        blocked = every_leaf[start_at:start_at + length].reshape(devices_here - 1, LEAVES_DEV)
        shuffled = jax.random.permutation(jax.random.fold_in(subkey, 1), blocked, axis=1, independent=True).reshape(-1)
        keeping = jax.random.randint(jax.random.fold_in(subkey, 2), (length,), 0, 8) < 7
        sources = blocked.reshape(-1)
        upper = jnp.full((LEAVES,), -1, jnp.int32).at[sources].set(jnp.where(keeping, shuffled, -1))
        lower = jnp.full((LEAVES,), -1, jnp.int32).at[jnp.where(keeping, shuffled, LEAVES)].set(sources, mode='drop')
        rows.append(lower)
        rows.append(upper)
    return jnp.stack(rows).astype(jnp.int32)


def draw_mortars(key, part):
    key = jax.random.fold_in(key, 23)
    devices_here = LEAVES // LEAVES_DEV
    slot_ids = jnp.arange(MORTARS, dtype=jnp.int32)
    owner = slot_ids // MORT_DEV
    within = slot_ids % MORT_DEV
    busiest = jax.random.randint(jax.random.fold_in(key, 1), (), 0, devices_here)
    heavy = jax.random.randint(jax.random.fold_in(key, 2), (devices_here,), 0, 4) == 0
    partial_fill = jax.random.randint(jax.random.fold_in(key, 3), (devices_here,), max(1, MORT_DEV // 8), max(2, MORT_DEV // 2 + 1))
    used = jnp.where(heavy | (jnp.arange(devices_here) == busiest), MORT_DEV, partial_fill)
    alive = within < used[owner]
    coarse = owner * LEAVES_DEV + jax.random.randint(jax.random.fold_in(key, 4), (MORTARS,), 0, LEAVES_DEV)
    facet = jax.random.randint(jax.random.fold_in(key, 5), (MORTARS,), 0, 6)
    fines = owner[None, :] * LEAVES_DEV - LEAVES_DEV + jax.random.randint(jax.random.fold_in(key, 6), (4, MORTARS), 0, 3 * LEAVES_DEV)
    fines = jnp.clip(fines, 0, LEAVES - 1)
    table = jnp.concatenate([coarse[None, :], facet[None, :], fines], axis=0)
    return jnp.where(alive[None, :], table, -1).astype(jnp.int32)


def draw_cotangent(key, part):
    key = jax.random.fold_in(key, 31)
    leaf_scale = jnp.exp(jax.random.uniform(jax.random.fold_in(key, 1), (1, 1, LEAVES), minval=0.0, maxval=math.log(10.0)))
    node_scale = jnp.exp(jax.random.uniform(jax.random.fold_in(key, 2), (FIELDS, NODES, 1), minval=0.0, maxval=math.log(10.0)))
    base = jnp.clip(jax.random.normal(jax.random.fold_in(key, 3), (FIELDS, NODES, LEAVES)), -3.0, 3.0)
    return (0.1 * base * leaf_scale * node_scale).astype(jnp.float32)


def place_ends(entries, stream_key, smallest, high):
    spot = [jax.random.randint(jax.random.fold_in(stream_key, axis), (), 0, length) for axis, length in enumerate(entries.shape)]
    main_axis = entries.shape.index(max(entries.shape))
    neighbour = spot[:main_axis] + [(spot[main_axis] + 1) % entries.shape[main_axis]] + spot[main_axis + 1:]
    return entries.at[tuple(spot)].set(smallest).at[tuple(neighbour)].set(high)


def shard_levels(own_key, dims, shards, low, largest):
    def one(dim, shards_of):
        steps = jax.random.uniform(jax.random.fold_in(jax.random.fold_in(own_key, 6), dim), (shards_of,), jnp.float32, low / len(shards), largest / len(shards))
        return jnp.repeat(jnp.exp(steps), dims[dim] // shards_of).reshape((-1,) + (1,) * (len(dims) - dim - 1))

    factor_of = one(*shards[0])
    for cut in shards[1:]:
        factor_of = factor_of * one(*cut)
    return factor_of


def noise(stream_key, extent, width, bound, kind=jnp.bfloat16):
    return jnp.clip(width * jax.random.normal(stream_key, extent, jnp.float32), -bound, bound).astype(kind)


def setup_inputs(seed: int = 0) -> dict:
    arg_keys = jax.random.split(jax.random.key(seed), 8)
    return {
        "cotangent": draw_cotangent(jax.random.fold_in(arg_keys[7], 71), 0),
        "nodal_mass": jnp.clip(jnp.exp(math.log(2.0) - 1.3862944 * jax.random.uniform(arg_keys[1], (NODES, LEAVES), jnp.float32) ** shard_levels(arg_keys[1], (NODES, LEAVES), ((1, 256),), -0.2, 0.2)), 0.5, 2.0),
        "curvature": jnp.clip(-1.0 + 3.0 * jax.random.uniform(arg_keys[2], (NODES, LEAVES), jnp.float32) ** shard_levels(arg_keys[2], (NODES, LEAVES), ((1, 256),), -0.2, 0.2), -1.0, 2.0),
        "stiffness": noise(arg_keys[3], (NODES, NODES), NODES ** -0.5, 0.75, jnp.float32),
        "levels": place_ends(jax.random.randint(arg_keys[4], (LEAVES,), 0, 4), jax.random.fold_in(arg_keys[4], 1), 0, 3).astype(jnp.int32),
        "neighbours": draw_neighbours(jax.random.fold_in(arg_keys[7], 71), 0),
        "mortars": draw_mortars(jax.random.fold_in(arg_keys[7], 71), 0),
    }


TAU_WEIGHT = 0.15
EPS_WEIGHT = 0.1
FLIP_ORDER = [1, 0, 3, 2, 5, 4]

def face_tables():
    select = np.zeros((6, 16, 64))
    node_at = np.zeros((6, 16), dtype=np.int64)
    for face_id in range(6):
        axis_id = face_id // 2
        layer_at = 3 * (face_id % 2)
        for row_pos in range(4):
            for col_pos in range(4):
                coords = [row_pos, col_pos]
                coords.insert(axis_id, layer_at)
                node_id = 16 * coords[0] + 4 * coords[1] + coords[2]
                select[face_id, 4 * row_pos + col_pos, node_id] = 1.0
                node_at[face_id, 4 * row_pos + col_pos] = node_id
    across = np.zeros((6, 64, 64))
    for face_id in range(6):
        other_face = FLIP_ORDER[face_id]
        for place in range(16):
            across[face_id, node_at[face_id, place], node_at[other_face, place]] += 1.0
    counts = select.sum(axis=(0, 1))
    points = np.array([-1.0, -1.0 / np.sqrt(5.0), 1.0 / np.sqrt(5.0), 1.0])
    halves = np.zeros((2, 4, 4))
    for half_id in range(2):
        target = (points + 2.0 * half_id - 1.0) / 2.0
        for column in range(4):
            lagrange = np.ones(4)
            for other_id in range(4):
                if other_id != column:
                    lagrange = lagrange * (target - points[other_id]) / (points[column] - points[other_id])
            halves[half_id, :, column] = lagrange
    mortar = np.stack([np.kron(halves[quarter // 2], halves[quarter % 2]) for quarter in range(4)])
    return (jnp.asarray(select, jnp.float32), jnp.asarray(across, jnp.float32), jnp.asarray(counts, jnp.float32), jnp.asarray(mortar, jnp.float32))

def laplace(nodal_in, stiffness, level_scale, neighbours, mortars):
    select, across, counts, mortar = face_tables()
    highest = lax.Precision.HIGHEST
    result = jnp.einsum('nm,xmL->xnL', stiffness, nodal_in, precision=highest) + counts[:, None] * nodal_in
    result = level_scale * result
    for face_id in range(6):
        face_index = neighbours[face_id]
        values = jnp.take(nodal_in, jnp.clip(face_index, 0, LEAVES - 1), axis=2)
        moved_in = jnp.einsum('nm,xmL->xnL', across[face_id], values, precision=highest)
        result = result - jnp.where(face_index >= 0, level_scale, 0.0) * moved_in
    coarse = jnp.clip(mortars[0], 0, LEAVES - 1)
    facing = (mortars[1][None, :] == jnp.arange(6, dtype=jnp.int32)[:, None]).astype(jnp.float32)
    flipped = facing[jnp.array(FLIP_ORDER, dtype=jnp.int32)]
    coarse_trace = jnp.einsum('fpn,xnS,fS->xpS', select, jnp.take(nodal_in, coarse, axis=2), facing, precision=highest)
    coarse_sum = jnp.zeros_like(coarse_trace)
    for quarter in range(4):
        fine_idx = jnp.clip(mortars[2 + quarter], 0, LEAVES - 1)
        fine_trace = jnp.einsum('fpn,xnS,fS->xpS', select, jnp.take(nodal_in, fine_idx, axis=2), flipped, precision=highest)
        mismatch = jnp.einsum('pr,xrS->xpS', mortar[quarter], coarse_trace, precision=highest) - fine_trace
        coarse_sum = coarse_sum + jnp.einsum('rp,xrS->xpS', mortar[quarter], mismatch, precision=highest)
        spread = jnp.einsum('fpn,xpS,fS->xnS', select, mismatch, flipped, precision=highest)
        result = result.at[:, :, fine_idx].add(-level_scale[fine_idx] * spread)
    spread = jnp.einsum('fpn,xpS,fS->xnS', select, coarse_sum, facing, precision=highest)
    return result.at[:, :, coarse].add(level_scale[coarse] * spread)

def forward(state, nodal_mass, curvature, stiffness, level_scale, neighbours, mortars):
    lapped = laplace(jnp.stack([state[1], state[0]]), stiffness, level_scale, neighbours, mortars)
    return jnp.stack([nodal_mass * state[0] + TAU_WEIGHT * lapped[0], nodal_mass * state[1] - curvature * state[0] - EPS_WEIGHT * lapped[1]])

def least_squares(rhs_norm, first_diag, first_below, upper_right, second_diag, second_below):
    first_len = jnp.sqrt(first_diag * first_diag + first_below * first_below)
    cos_one = first_diag / first_len
    sin_one = first_below / first_len
    rotated_top = cos_one * upper_right + sin_one * second_diag
    rotated_low = cos_one * second_diag - sin_one * upper_right
    second_len = jnp.sqrt(rotated_low * rotated_low + second_below * second_below)
    cos_two = rotated_low / second_len
    y_two = cos_two * (-sin_one * rhs_norm) / second_len
    y_one = (cos_one * rhs_norm - rotated_top * y_two) / first_len
    return (y_one, y_two)

def total(left, right):
    return jnp.sum(left * right)

def reference(cotangent, nodal_mass, curvature, stiffness, levels, neighbours, mortars):
    level_scale = jnp.left_shift(jnp.ones_like(levels), levels).astype(jnp.float32)

    def linear(probe):
        return forward(probe, nodal_mass, curvature, stiffness, level_scale, neighbours, mortars)

    def apply_t(vector):
        unused, pullback = jax.vjp(linear, jnp.zeros_like(vector))
        return pullback(vector)[0]
    rhs_norm = jnp.sqrt(total(cotangent, cotangent))
    basis_one = cotangent / rhs_norm
    image = apply_t(basis_one)
    first_diag = total(image, basis_one)
    image = image - first_diag * basis_one
    first_below = jnp.sqrt(total(image, image))
    basis_two = image / first_below
    image = apply_t(basis_two)
    upper_right = total(image, basis_one)
    second_diag = total(image, basis_two)
    image = image - upper_right * basis_one - second_diag * basis_two
    second_below = jnp.sqrt(total(image, image))
    y_one, y_two = least_squares(rhs_norm, first_diag, first_below, upper_right, second_diag, second_below)
    return y_one * basis_one + y_two * basis_two
```

```python
import jax
import jax.numpy as jnp
import ml_dtypes
import numpy as np
from jax import lax
from jax.experimental import pallas as pl
from jax.experimental.pallas import tpu as pltpu
from jax.sharding import PartitionSpec as P

TAU_WEIGHT = 0.15
EPS_WEIGHT = 0.1
FACES = 6
NODES = 64
LANES = 128
TRACE = 256
F32 = jnp.float32
BF16 = jnp.bfloat16


def face_tables():
    node_at = np.zeros((6, 16), dtype=np.int64)
    for face_id in range(6):
        for row_pos in range(4):
            for col_pos in range(4):
                coords = [row_pos, col_pos]
                coords.insert(face_id // 2, 3 * (face_id % 2))
                node_at[face_id, 4 * row_pos + col_pos] = (
                    16 * coords[0] + 4 * coords[1] + coords[2]
                )
    counts = np.zeros(64)
    for face_id in range(6):
        counts[node_at[face_id]] += 1.0
    points = np.array([-1.0, -1.0 / np.sqrt(5.0), 1.0 / np.sqrt(5.0), 1.0])
    halves = np.zeros((2, 4, 4))
    for half_id in range(2):
        target = (points + 2.0 * half_id - 1.0) / 2.0
        for column in range(4):
            lagrange = np.ones(4)
            for other_id in range(4):
                if other_id != column:
                    lagrange = (
                        lagrange * (target - points[other_id]) / (points[column] - points[other_id])
                    )
            halves[half_id, :, column] = lagrange
    mortar = np.stack([np.kron(halves[quarter // 2], halves[quarter % 2]) for quarter in range(4)])
    return node_at, counts, mortar


def matrices():
    node_at, counts, mortar = face_tables()
    traces = np.zeros((2 * LANES, TRACE))
    across = np.zeros((FACES * 2 * LANES, LANES))
    spread = np.zeros((TRACE, LANES))
    prolong = np.zeros((TRACE, 4 * TRACE))
    for face in range(FACES):
        other = face ^ 1
        for field in range(2):
            base = 32 * face + 16 * field
            lifted = 32 * other + 16 * field
            for place in range(16):
                node = 64 * field + node_at[face, place]
                facing = 64 * field + node_at[other, place]
                spread[base + place, node] = 1.0
                for part in range(2):
                    traces[part * LANES + node, base + place] = 1.0
                    across[(2 * face + part) * LANES + facing, node] = 1.0
            for quarter in range(4):
                start = quarter * TRACE + lifted
                prolong[base : base + 16, start : start + 16] = mortar[quarter].T
    count_row = np.tile(np.concatenate([counts, counts])[None, :], (8, 1))
    return traces, across, spread, prolong, count_row


def two_parts(table):
    high = table.astype(np.float32).astype(ml_dtypes.bfloat16)
    low = (table - high.astype(np.float64)).astype(np.float32).astype(ml_dtypes.bfloat16)
    return high, low


def split(values):
    high = values.astype(BF16)
    low = (values - high.astype(F32)).astype(BF16)
    return high, low


def dot(left, right):
    return jnp.dot(left, right, preferred_element_type=F32)


def dot3(values, high, low):
    v_high, v_low = split(values)
    return dot(v_high, high) + dot(v_low, high) + dot(v_high, low)


def pick(index, shape, dim):
    return jnp.where(index == lax.broadcasted_iota(jnp.int32, shape, dim), 1.0, 0.0).astype(BF16)


def prep_kernel(cot_ref, levels_ref, mortars_ref, pack_ref):
    leaves = cot_ref.shape[1]
    scale = jnp.left_shift(jnp.ones_like(levels_ref[...]), levels_ref[...]).astype(F32)
    pack_ref[0:leaves, :] = (cot_ref[...] * scale).T
    table = mortars_ref[...].astype(F32) + 1.0
    pack_ref[leaves : leaves + 8, :] = jnp.concatenate(
        [table, jnp.zeros((2, table.shape[1]), F32)], axis=0
    )


def laplace(blocks, tables, neighbours, stiffness, offset, consts):
    traces_ref, across_ref, spread_ref, pro_hi, pro_lo, res_hi, res_lo, count_ref = consts
    leaves = blocks[1].shape[0]
    slots = tables[1].shape[1]
    own = blocks[1]
    values = jnp.concatenate(blocks, axis=0)
    halves = jnp.concatenate(split(values), axis=1)
    near = jnp.where(neighbours >= 0, neighbours - offset + leaves, -1)
    near = jnp.concatenate([near, jnp.full((2, leaves), -1, jnp.int32)], axis=0)
    near = near.astype(F32).T.astype(jnp.int32)
    moved = jnp.zeros((leaves, LANES), F32)
    for face in range(FACES):
        chosen = dot(pick(near[:, face : face + 1], (leaves, 3 * leaves), 1), halves)
        moved = moved + dot(
            chosen.astype(BF16), across_ref[2 * LANES * face : 2 * LANES * (face + 1), :]
        )
    wide = jnp.concatenate([stiffness, stiffness], axis=1)
    wide = jnp.concatenate([wide, wide], axis=0)
    same = (lax.broadcasted_iota(jnp.int32, wide.shape, 0) < NODES) == (
        lax.broadcasted_iota(jnp.int32, wide.shape, 1) < NODES
    )
    result = count_ref[0:1, :] * own - moved + dot3(own, *split(jnp.where(same, wide, 0.0)))

    rows = [table.astype(jnp.int32) - 1 for table in tables]
    columns = [table.T.astype(jnp.int32) - 1 for table in tables]
    lane_face = lax.broadcasted_iota(jnp.int32, (slots, TRACE), 1) // 32
    coarse = []
    for place in range(3):
        local = columns[place][:, 0:1] - offset - (place - 1) * leaves
        block = halves[place * leaves : (place + 1) * leaves, :]
        chosen = dot(pick(local, (slots, leaves), 1), block).astype(BF16)
        trace = dot(chosen, traces_ref[...])
        coarse.append(jnp.where(lane_face == columns[place][:, 1:2], trace, 0.0))
    lifted = dot3(jnp.concatenate(coarse, axis=0), pro_hi[...], pro_lo[...])
    coarse_sum = jnp.zeros((slots, TRACE), F32)
    gathered = jnp.zeros((leaves, TRACE), F32)
    for quarter in range(4):
        fine = []
        for place in range(3):
            local = columns[place][:, 2 + quarter : 3 + quarter] - offset
            if place == 1:
                chosen = dot(pick(local + leaves, (slots, 3 * leaves), 1), halves)
            else:
                chosen = dot(
                    pick(local, (slots, leaves), 1), halves[leaves : 2 * leaves, :]
                )
            trace = dot(chosen.astype(BF16), traces_ref[...])
            face = columns[place][:, 1:2]
            other = jnp.where(face >= 0, face ^ 1, -1)
            fine.append(jnp.where(lane_face == other, trace, 0.0))
        jump = lifted[:, quarter * TRACE : (quarter + 1) * TRACE] - jnp.concatenate(fine, axis=0)
        high, low = split(jump)
        index = jnp.concatenate(
            [row[2 + quarter : 3 + quarter, :] - offset for row in rows], axis=1
        )
        back = pick(index, (leaves, 3 * slots), 0)
        gathered = gathered - (dot(back, high) + dot(back, low))
        part = slice(quarter * TRACE, (quarter + 1) * TRACE)
        coarse_sum = coarse_sum + dot3(
            jump[slots : 2 * slots, :], res_hi[part, :], res_lo[part, :]
        )
    high, low = split(coarse_sum)
    back = pick(rows[1][0:1, :] - offset, (leaves, slots), 0)
    gathered = gathered + (dot(back, high) + dot(back, low))
    high, low = split(gathered)
    return result + (dot(high, spread_ref[...]) + dot(low, spread_ref[...]))


def apply_t(vector, lapped, mass_ref, curve_ref):
    first = lax.broadcasted_iota(jnp.int32, vector.shape, 1) < NODES
    mass = jnp.concatenate([mass_ref[...], mass_ref[...]], axis=0).T
    curve = jnp.concatenate([curve_ref[...], curve_ref[...]], axis=0).T
    turned = pltpu.roll(lapped, NODES, 1)
    swapped = pltpu.roll(vector, NODES, 1)
    return mass * vector + jnp.where(
        first, -curve * swapped - EPS_WEIGHT * turned, TAU_WEIGHT * turned
    )


def columns_scale(levels):
    scale = jnp.left_shift(jnp.ones_like(levels), levels).astype(F32)
    return jnp.broadcast_to(scale, (LANES, levels.shape[1])).T


def first_kernel(
    offset_ref, own_ref, prev_ref, next_ref, levels_ref, neighbours_ref, mass_ref, curve_ref,
    stiffness_ref, *rest
):
    consts, (image_ref, send_ref) = rest[:-2], rest[-2:]
    leaves = levels_ref.shape[1]
    refs = (prev_ref, own_ref, next_ref)
    blocks = [ref[0:leaves, :] for ref in refs]
    tables = [ref[leaves : leaves + 8, :] for ref in refs]
    lapped = laplace(
        blocks, tables, neighbours_ref[...], stiffness_ref[...], offset_ref[0], consts
    )
    scale = columns_scale(levels_ref[...])
    image = apply_t(blocks[1] / scale, lapped, mass_ref, curve_ref)
    image_ref[...] = image
    send_ref[...] = image * scale


def over(top, bottom):
    return jnp.where(bottom > 0.0, top / jnp.where(bottom > 0.0, bottom, 1.0), 0.0)


def total(values):
    return jnp.sum(values, keepdims=True)


def second_kernel(
    offset_ref, own_ref, prev_ref, next_ref, levels_ref, neighbours_ref, mass_ref, curve_ref,
    stiffness_ref, pack_ref, pack_prev_ref, pack_next_ref, image_ref, *rest
):
    consts, stats_ref = rest[:-1], rest[-1]
    leaves = levels_ref.shape[1]
    blocks = [prev_ref[...], own_ref[...], next_ref[...]]
    tables = [ref[leaves : leaves + 8, :] for ref in (pack_prev_ref, pack_ref, pack_next_ref)]
    lapped = laplace(
        blocks, tables, neighbours_ref[...], stiffness_ref[...], offset_ref[0], consts
    )
    one = image_ref[...]
    two = apply_t(one, lapped, mass_ref, curve_ref)
    base = pack_ref[0:leaves, :] / columns_scale(levels_ref[...])
    r00 = jnp.sqrt(total(base * base))
    r01 = over(total(base * one), r00)
    r02 = over(total(base * two), r00)
    one = one - over(r01, r00) * base
    two = two - over(r02, r00) * base
    r11 = jnp.sqrt(total(one * one))
    r12 = over(total(one * two), r11)
    two = two - over(r12, r11) * one
    r22 = jnp.sqrt(total(two * two))
    lane = lax.broadcasted_iota(jnp.int32, stats_ref.shape, 1)
    row = jnp.zeros(stats_ref.shape, F32)
    for at, value in enumerate((r00, r01, r02, r11, r12, r22)):
        row = jnp.where(lane == at, value, row)
    stats_ref[...] = row


def final_kernel(stats_ref, cot_ref, image_ref, out_ref):
    table = stats_ref[...].T
    a0, a1, a2, b1, b2, c2 = [table[at : at + 1, :] for at in range(6)]
    r00_sq = total(a0 * a0)
    r00 = jnp.sqrt(r00_sq)
    f01 = total(a0 * a1) / r00_sq
    f02 = total(a0 * a2) / r00_sq
    a1 = a1 - f01 * a0
    a2 = a2 - f02 * a0
    r11_sq = total(a1 * a1) + total(b1 * b1)
    r11 = jnp.sqrt(r11_sq)
    f12 = (total(a1 * a2) + total(b1 * b2)) / r11_sq
    a2 = a2 - f12 * a1
    b2 = b2 - f12 * b1
    r22 = jnp.sqrt(total(a2 * a2) + total(b2 * b2) + total(c2 * c2))
    rhs_norm = r00
    first_diag = f01
    first_below = r11 / r00
    upper_right = (f02 - first_diag * f01) / first_below
    second_diag = f12 - first_diag
    second_below = r22 / r11
    first_len = jnp.sqrt(first_diag * first_diag + first_below * first_below)
    cos_one = first_diag / first_len
    sin_one = first_below / first_len
    rotated_top = cos_one * upper_right + sin_one * second_diag
    rotated_low = cos_one * second_diag - sin_one * upper_right
    second_len = jnp.sqrt(rotated_low * rotated_low + second_below * second_below)
    cos_two = rotated_low / second_len
    y_two = cos_two * (-sin_one * rhs_norm) / second_len
    y_one = (cos_one * rhs_norm - rotated_top * y_two) / first_len
    on_one = y_two / r11
    on_base = y_one / r00 - on_one * f01
    out_ref[...] = on_base * cot_ref[...] + on_one * image_ref[...].T


def on_device(cotangent, nodal_mass, curvature, stiffness, levels, neighbours, mortars):
    fields, nodes, leaves = cotangent.shape
    count = lax.axis_size("leaf")
    flat = cotangent.reshape(fields * nodes, leaves)
    levels = levels.reshape(1, leaves)
    offset = (lax.axis_index("leaf") * leaves).astype(jnp.int32).reshape(1)
    traces, across, spread, prolong, count_row = matrices()
    pro_hi, pro_lo = two_parts(prolong)
    res_hi, res_lo = two_parts(np.ascontiguousarray(prolong.T))
    small = ml_dtypes.bfloat16
    consts = [
        jnp.asarray(table)
        for table in (
            traces.astype(small), across.astype(small), spread.astype(small),
            pro_hi, pro_lo, res_hi, res_lo, count_row.astype(np.float32),
        )
    ]
    forward = [(i, i + 1) for i in range(count - 1)]
    backward = [(i + 1, i) for i in range(count - 1)]
    vmem = pl.BlockSpec(memory_space=pltpu.VMEM)
    smem = pl.BlockSpec(memory_space=pltpu.SMEM)
    params = pltpu.CompilerParams(vmem_limit_bytes=48 * 1024 * 1024)

    def call(kernel, outs, *operands, scalars=0):
        return pl.pallas_call(
            kernel,
            out_shape=outs,
            in_specs=[smem] * scalars + [vmem] * (len(operands) - scalars),
            out_specs=jax.tree.map(lambda _: vmem, outs),
            compiler_params=params,
        )(*operands)

    rows = jax.ShapeDtypeStruct((leaves, LANES), F32)
    pack = call(
        prep_kernel, jax.ShapeDtypeStruct((leaves + 8, LANES), F32), flat, levels, mortars
    )
    pack_prev = lax.ppermute(pack, "leaf", forward)
    pack_next = lax.ppermute(pack, "leaf", backward)
    local = (levels, neighbours, nodal_mass, curvature, stiffness)
    image, send = call(
        first_kernel, (rows, rows), offset, pack, pack_prev, pack_next, *local, *consts, scalars=1
    )
    send_prev = lax.ppermute(send, "leaf", forward)
    send_next = lax.ppermute(send, "leaf", backward)
    stats = call(
        second_kernel, jax.ShapeDtypeStruct((1, LANES), F32), offset, send, send_prev, send_next,
        *local, pack, pack_prev, pack_next, image, *consts, scalars=1
    )
    gathered = lax.all_to_all(
        jnp.broadcast_to(stats, (count, LANES)), "leaf", 0, 0, tiled=True
    )
    out = call(final_kernel, jax.ShapeDtypeStruct(flat.shape, F32), gathered, flat, image)
    return out.reshape(cotangent.shape)


def solution(mesh):
    placed = (
        P(None, None, "leaf"),
        P(None, "leaf"),
        P(None, "leaf"),
        P(),
        P("leaf"),
        P(None, "leaf"),
        P(None, "leaf"),
    )
    return jax.shard_map(
        on_device, mesh=mesh, in_specs=placed, out_specs=P(None, None, "leaf"), check_vma=False
    )
```

```python
import jax
import jax.numpy as jnp
import ml_dtypes
import numpy as np
from jax import lax
from jax.experimental import pallas as pl
from jax.experimental.pallas import tpu as pltpu
from jax.sharding import PartitionSpec as P

TAU_WEIGHT = 0.15
EPS_WEIGHT = 0.1
FACES = 6
NODES = 64
LANES = 128
TRACE = 256
F32 = jnp.float32
BF16 = jnp.bfloat16


def face_tables():
    node_at = np.zeros((6, 16), dtype=np.int64)
    for face_id in range(6):
        for row_pos in range(4):
            for col_pos in range(4):
                coords = [row_pos, col_pos]
                coords.insert(face_id // 2, 3 * (face_id % 2))
                node_at[face_id, 4 * row_pos + col_pos] = (
                    16 * coords[0] + 4 * coords[1] + coords[2]
                )
    counts = np.zeros(64)
    for face_id in range(6):
        counts[node_at[face_id]] += 1.0
    points = np.array([-1.0, -1.0 / np.sqrt(5.0), 1.0 / np.sqrt(5.0), 1.0])
    halves = np.zeros((2, 4, 4))
    for half_id in range(2):
        target = (points + 2.0 * half_id - 1.0) / 2.0
        for column in range(4):
            lagrange = np.ones(4)
            for other_id in range(4):
                if other_id != column:
                    lagrange = (
                        lagrange * (target - points[other_id]) / (points[column] - points[other_id])
                    )
            halves[half_id, :, column] = lagrange
    mortar = np.stack([np.kron(halves[quarter // 2], halves[quarter % 2]) for quarter in range(4)])
    return node_at, counts, mortar


def two_parts(table):
    high = table.astype(np.float32).astype(ml_dtypes.bfloat16)
    low = (table - high.astype(np.float64)).astype(np.float32).astype(ml_dtypes.bfloat16)
    return np.concatenate([high, low], axis=-1)


def matrices():
    node_at, counts, mortar = face_tables()
    traces = np.zeros((2 * LANES, TRACE))
    across = np.zeros((FACES * 2 * LANES, LANES))
    spread = np.zeros((TRACE, LANES))
    to_fine = np.zeros((4, TRACE, LANES))
    to_coarse = np.zeros((4, TRACE, LANES))
    stay = np.zeros((TRACE, LANES))
    square = sum(mortar[quarter].T @ mortar[quarter] for quarter in range(4))
    for face in range(FACES):
        other = face ^ 1
        for field in range(2):
            base = 32 * face + 16 * field
            lifted = 32 * other + 16 * field
            nodes = 64 * field + node_at[face]
            facing = 64 * field + node_at[other]
            for place in range(16):
                spread[base + place, nodes[place]] = 1.0
                for part in range(2):
                    traces[part * LANES + nodes[place], base + place] = 1.0
                    across[(2 * face + part) * LANES + facing[place], nodes[place]] = 1.0
                stay[base + place, nodes] = square[:, place]
                for quarter in range(4):
                    to_fine[quarter, base + place, facing] = mortar[quarter][:, place]
                    to_coarse[quarter, lifted + place, nodes] = mortar[quarter][place, :]
    small = ml_dtypes.bfloat16
    counts = np.tile(np.concatenate([counts, counts])[None, :], (8, 1)).astype(np.float32)
    return (
        traces.astype(small),
        across.astype(small),
        spread.astype(small),
        np.concatenate(list(two_parts(to_fine)), axis=-1),
        np.concatenate(list(two_parts(to_coarse)), axis=0),
        two_parts(stay),
        counts,
    )


def split(values, axis=1):
    high = values.astype(BF16)
    return jnp.concatenate([high, (values - high.astype(F32)).astype(BF16)], axis=axis)


def dot(left, right):
    return jnp.dot(left, right, preferred_element_type=F32)


def fold(values):
    return values[:, :LANES] + values[:, LANES:]


def dot_parts(values, table):
    high = values.astype(BF16)
    low = (values - high.astype(F32)).astype(BF16)
    return dot(high, table) + dot(low, table)


def pick(index, shape, dim):
    return jnp.where(index == lax.broadcasted_iota(jnp.int32, shape, dim), 1.0, 0.0).astype(BF16)


def on_face(face, slots):
    return lax.broadcasted_iota(jnp.int32, (slots, TRACE), 1) // 32 == face


def opposite(face):
    return jnp.where(face >= 0, face ^ 1, -1)


def level_rows(levels):
    scale = jnp.left_shift(jnp.ones_like(levels), levels).astype(F32)
    return jnp.broadcast_to(scale, (LANES, levels.shape[1])).T


def fetch(pairs, sems):
    copies = [
        pltpu.make_async_copy(source, target, sems.at[at])
        for at, (source, target) in enumerate(pairs)
    ]
    for copy in copies:
        copy.start()
    return copies


def prep_kernel(cot_hbm, levels_hbm, mortars_hbm, pack_ref, cot_ref, levels_ref, mortars_ref, sems):
    for copy in fetch(
        ((cot_hbm, cot_ref), (levels_hbm, levels_ref), (mortars_hbm, mortars_ref)), sems
    ):
        copy.wait()
    leaves = cot_ref.shape[1]
    scale = jnp.left_shift(jnp.ones_like(levels_ref[...]), levels_ref[...]).astype(F32)
    pack_ref[0:leaves, :] = (cot_ref[...] * scale).T
    table = mortars_ref[...].astype(F32) + 1.0
    pack_ref[leaves : leaves + 8, :] = jnp.concatenate(
        [table, jnp.zeros((2, table.shape[1]), F32)], axis=0
    )


TABLES = ("traces", "across", "to_fine", "to_coarse", "stay")
KEPT = (
    "oh_own", "oh_near", "coarse_pick", "fine_own", "fine_near", "fine_back", "coarse_back",
    "coarse_count", "diagonal", "stiff", "mass", "curve", "scale",
) + TABLES


def own_part(rows, kept):
    slots = kept["coarse_pick"].shape[0]
    parts = split(rows)
    chosen = dot(kept["oh_own"][...], parts).astype(BF16)
    leaves = rows.shape[0]
    moved = jnp.zeros(rows.shape, F32)
    for face in range(FACES):
        moved = moved + dot(
            chosen[leaves * face : leaves * (face + 1), :],
            kept["across"][2 * LANES * face : 2 * LANES * (face + 1), :],
        )
    result = kept["diagonal"][...] * rows - moved + fold(dot(parts, kept["stiff"][...]))
    here = dot(parts, kept["traces"][...]) * kept["coarse_count"][...]
    result = result + fold(dot_parts(here, kept["stay"][...]))
    face = kept["face"][...]
    trace = dot(dot(kept["coarse_pick"][...], parts).astype(BF16), kept["traces"][...])
    trace = jnp.where(on_face(face, slots), trace, 0.0)
    lifted = dot_parts(trace, kept["to_fine"][...])
    lifted = jnp.concatenate(
        [split(fold(lifted[:, TRACE * q : TRACE * (q + 1)])) for q in range(4)], axis=0
    )
    result = result - fold(dot(kept["fine_back"][...], lifted))
    return result - from_fine(kept["fine_own"], parts, kept)


def from_fine(picks, parts, kept):
    slots = kept["coarse_back"].shape[1]
    trace = dot(dot(picks[...], parts).astype(BF16), kept["traces"][...])
    other = on_face(opposite(kept["face"][...]), slots)
    sent = jnp.zeros((slots, 2 * LANES), F32)
    for quarter in range(4):
        part = jnp.where(other, trace[slots * quarter : slots * (quarter + 1), :], 0.0)
        sent = sent + dot_parts(part, kept["to_coarse"][TRACE * quarter : TRACE * (quarter + 1), :])
    return fold(dot(kept["coarse_back"][...], split(fold(sent))))


def fine_count(back, other, spread):
    weights = jnp.where(other, 1.0, 0.0).astype(BF16)
    times = dot(back, jnp.concatenate([weights] * 4, axis=0))
    return dot_parts(times, spread)


def near_index(index, offset, first, leaves):
    local = index - offset
    here = jnp.where(local < 0, local + leaves, local - leaves)
    is_first = (local < 0) == (first < 0)
    outside = (local >= 0) & (local < leaves)
    return jnp.where(outside | (index < 0), -1, jnp.where(is_first, here, here + leaves))


def own_index(index, offset):
    return jnp.where(index < 0, -1, index - offset)


def to_columns(table):
    return table.astype(F32).T.astype(jnp.int32)


def near_kernel(place_ref, pack_ref, *refs):
    names = ("neighbours", "mass", "curve", "stiffness", "levels", "spread", "counts") + TABLES
    sources = dict(zip(names, refs))
    refs = refs[len(names) :]
    kept = dict(zip(KEPT + ("face", "partial"), refs))
    refs = refs[len(KEPT) + 2 :]
    local = dict(zip(names[: -len(TABLES)], refs))
    sems = refs[-1]
    targets = [local[name] if name in local else kept[name] for name in names]
    copies = fetch(tuple(zip((sources[name] for name in names), targets)), sems)
    leaves = pack_ref.shape[0] - 8
    offset, first = place_ref[0], place_ref[1]
    table = pack_ref[leaves : leaves + 8, :].astype(jnp.int32) - 1
    columns = to_columns(pack_ref[leaves : leaves + 8, :]) - 1
    slots = table.shape[1]
    face = columns[:, 1:2]
    kept["face"][...] = face
    copies[0].wait()
    neighbours = jnp.concatenate(
        [local["neighbours"][...], jnp.full((2, leaves), -1, jnp.int32)], axis=0
    )
    own = to_columns(own_index(neighbours, offset))
    near = to_columns(near_index(neighbours, offset, first, leaves))
    for f in range(FACES):
        rows = slice(leaves * f, leaves * (f + 1))
        kept["oh_own"][rows, :] = pick(own[:, f : f + 1], (leaves, leaves), 1)
        kept["oh_near"][rows, :] = pick(near[:, f : f + 1], (leaves, 2 * leaves), 1)
    kept["coarse_pick"][...] = pick(columns[:, 0:1] - offset, (slots, leaves), 1)
    coarse_back = pick(table[0:1, :] - offset, (leaves, slots), 0)
    kept["coarse_back"][...] = coarse_back
    fine_own = own_index(columns, offset)
    fine_near = near_index(columns, offset, first, leaves)
    fine_rows = own_index(table, offset)
    for q in range(4):
        rows = slice(slots * q, slots * (q + 1))
        kept["fine_own"][rows, :] = pick(fine_own[:, 2 + q : 3 + q], (slots, leaves), 1)
        kept["fine_near"][rows, :] = pick(fine_near[:, 2 + q : 3 + q], (slots, 2 * leaves), 1)
        kept["fine_back"][:, rows] = pick(fine_rows[2 + q : 3 + q, :], (leaves, slots), 0)
    for copy in copies[1:]:
        copy.wait()
    weights = jnp.where(on_face(face, slots), 1.0, 0.0).astype(BF16)
    kept["coarse_count"][...] = dot(coarse_back, weights)
    kept["diagonal"][...] = local["counts"][0:1, :] + fine_count(
        kept["fine_back"][...], on_face(opposite(face), slots), local["spread"][...]
    )
    wide = jnp.concatenate([local["stiffness"][...]] * 2, axis=1)
    wide = jnp.concatenate([wide, wide], axis=0)
    same = (lax.broadcasted_iota(jnp.int32, wide.shape, 0) < NODES) == (
        lax.broadcasted_iota(jnp.int32, wide.shape, 1) < NODES
    )
    wide = split(jnp.where(same, wide, 0.0))
    kept["stiff"][...] = jnp.concatenate([wide, wide], axis=0)
    kept["mass"][...] = jnp.concatenate([local["mass"][...]] * 2, axis=0).T
    curve = local["curve"][...]
    kept["curve"][...] = jnp.concatenate([-curve, jnp.zeros_like(curve)], axis=0).T
    kept["scale"][...] = level_rows(local["levels"][...])
    kept["partial"][...] = own_part(pack_ref[0:leaves, :], kept)


def near_part(rows, kept, picks, backs, faces):
    leaves = rows.shape[0] // 2
    slots = picks.shape[0] // 2
    parts = split(rows)
    chosen = dot(kept["oh_near"][...], parts).astype(BF16)
    moved = jnp.zeros((leaves, LANES), F32)
    for face in range(FACES):
        moved = moved + dot(
            chosen[leaves * face : leaves * (face + 1), :],
            kept["across"][2 * LANES * face : 2 * LANES * (face + 1), :],
        )
    trace = jnp.concatenate(
        [
            dot(picks[slots * k : slots * (k + 1), :], parts[leaves * k : leaves * (k + 1), :])
            for k in range(2)
        ],
        axis=0,
    )
    trace = dot(trace.astype(BF16), kept["traces"][...])
    trace = jnp.where(on_face(faces, 2 * slots), trace, 0.0)
    lifted = dot_parts(trace, kept["to_fine"][...])
    lifted = jnp.concatenate(
        [split(fold(lifted[:, TRACE * q : TRACE * (q + 1)])) for q in range(4)], axis=0
    )
    return -moved - fold(dot(backs, lifted)) - from_fine(kept["fine_near"], parts, kept)


def apply_t(vector, lapped, kept):
    first = lax.broadcasted_iota(jnp.int32, vector.shape, 1) < NODES
    turned = pltpu.roll(lapped, NODES, 1)
    swapped = pltpu.roll(vector, NODES, 1)
    weight = jnp.where(first, -EPS_WEIGHT, TAU_WEIGHT)
    return kept["mass"][...] * vector + kept["curve"][...] * swapped + weight * turned


KEPT_FIRST = ("oh_near", "fine_near", "coarse_back", "mass", "curve", "scale") + TABLES[:4] + ("face",)
KEPT_AGAIN = (
    "oh_own", "coarse_pick", "fine_own", "fine_back", "coarse_back", "coarse_count", "diagonal",
    "stiff", "face",
) + TABLES


def first_kernel(place_ref, pack_ref, one_ref, two_ref, spread_ref, partial_ref, *refs):
    kept = dict(zip(KEPT_FIRST, refs))
    image_ref, send_ref, picks_ref, backs_ref, faces_ref, extra_ref = refs[len(KEPT_FIRST) :]
    leaves = pack_ref.shape[0] - 8
    offset, first = place_ref[0], place_ref[1]
    tables, columns = [], []
    for ref in (one_ref, two_ref):
        table = ref[leaves : leaves + 8, :]
        tables.append(table.astype(jnp.int32) - 1)
        columns.append(to_columns(table) - 1)
    slots = tables[0].shape[1]
    starts = (offset + first, offset - first)
    picks_ref[...] = jnp.concatenate(
        [pick(columns[k][:, 0:1] - starts[k], (slots, leaves), 1) for k in range(2)], axis=0
    )
    faces = jnp.concatenate([column[:, 1:2] for column in columns], axis=0)
    faces_ref[...] = faces
    index = jnp.concatenate([own_index(table, offset) for table in tables], axis=1)
    for q in range(4):
        backs_ref[:, 2 * slots * q : 2 * slots * (q + 1)] = pick(
            index[2 + q : 3 + q, :], (leaves, 2 * slots), 0
        )
    extra = fine_count(backs_ref[...], on_face(opposite(faces), 2 * slots), spread_ref[...])
    extra_ref[...] = extra
    own = pack_ref[0:leaves, :]
    rows = jnp.concatenate([one_ref[0:leaves, :], two_ref[0:leaves, :]], axis=0)
    lapped = partial_ref[...] + extra * own + near_part(
        rows, kept, picks_ref[...], backs_ref[...], faces
    )
    scale = kept["scale"][...]
    image = apply_t(own / scale, lapped, kept)
    image_ref[...] = image
    send_ref[...] = image * scale


def again_kernel(send_ref, extra_ref, *refs):
    kept = dict(zip(KEPT_AGAIN, refs))
    partial_ref = refs[len(KEPT_AGAIN)]
    rows = send_ref[...]
    partial_ref[...] = own_part(rows, kept) + extra_ref[...] * rows


def over(top, bottom):
    return jnp.where(bottom > 0.0, top / jnp.where(bottom > 0.0, bottom, 1.0), 0.0)


def total(values):
    return jnp.sum(values, keepdims=True)


def second_kernel(
    pack_ref, one_ref, two_ref, partial_ref, image_ref, picks_ref, backs_ref, faces_ref, *refs
):
    kept = dict(zip(KEPT_FIRST, refs))
    stats_ref = refs[len(KEPT_FIRST)]
    leaves = pack_ref.shape[0] - 8
    rows = jnp.concatenate([one_ref[...], two_ref[...]], axis=0)
    lapped = partial_ref[...] + near_part(
        rows, kept, picks_ref[...], backs_ref[...], faces_ref[...]
    )
    one = image_ref[...]
    two = apply_t(one, lapped, kept)
    base = pack_ref[0:leaves, :] / kept["scale"][...]
    r00 = jnp.sqrt(total(base * base))
    r01 = over(total(base * one), r00)
    r02 = over(total(base * two), r00)
    one = one - over(r01, r00) * base
    two = two - over(r02, r00) * base
    r11 = jnp.sqrt(total(one * one))
    r12 = over(total(one * two), r11)
    two = two - over(r12, r11) * one
    r22 = jnp.sqrt(total(two * two))
    lane = lax.broadcasted_iota(jnp.int32, stats_ref.shape, 1)
    row = jnp.zeros(stats_ref.shape, F32)
    for at, value in enumerate((r00, r01, r02, r11, r12, r22)):
        row = jnp.where(lane == at, value, row)
    stats_ref[...] = row


def final_kernel(stats_ref, cot_ref, image_ref, out_ref):
    table = stats_ref[...].T
    a0, a1, a2, b1, b2, c2 = [table[at : at + 1, :] for at in range(6)]
    r00_sq = total(a0 * a0)
    r00 = jnp.sqrt(r00_sq)
    f01 = total(a0 * a1) / r00_sq
    f02 = total(a0 * a2) / r00_sq
    a1 = a1 - f01 * a0
    a2 = a2 - f02 * a0
    r11_sq = total(a1 * a1) + total(b1 * b1)
    r11 = jnp.sqrt(r11_sq)
    f12 = (total(a1 * a2) + total(b1 * b2)) / r11_sq
    a2 = a2 - f12 * a1
    b2 = b2 - f12 * b1
    r22 = jnp.sqrt(total(a2 * a2) + total(b2 * b2) + total(c2 * c2))
    rhs_norm = r00
    first_diag = f01
    first_below = r11 / r00
    upper_right = (f02 - first_diag * f01) / first_below
    second_diag = f12 - first_diag
    second_below = r22 / r11
    first_len = jnp.sqrt(first_diag * first_diag + first_below * first_below)
    cos_one = first_diag / first_len
    sin_one = first_below / first_len
    rotated_top = cos_one * upper_right + sin_one * second_diag
    rotated_low = cos_one * second_diag - sin_one * upper_right
    second_len = jnp.sqrt(rotated_low * rotated_low + second_below * second_below)
    cos_two = rotated_low / second_len
    y_two = cos_two * (-sin_one * rhs_norm) / second_len
    y_one = (cos_one * rhs_norm - rotated_top * y_two) / first_len
    on_one = y_two / r11
    on_base = y_one / r00 - on_one * f01
    out_ref[...] = on_base * cot_ref[...] + on_one * image_ref[...].T


def on_device(cotangent, nodal_mass, curvature, stiffness, levels, neighbours, mortars):
    fields, nodes, leaves = cotangent.shape
    slots = mortars.shape[1]
    count = lax.axis_size("leaf")
    flat = cotangent.reshape(fields * nodes, leaves)
    levels = levels.reshape(1, leaves)
    me = lax.axis_index("leaf").astype(jnp.int32)
    place = jnp.stack([me * leaves, leaves - 2 * leaves * (me % 2)])
    traces, across, spread, to_fine, to_coarse, stay, counts = [
        jnp.asarray(table) for table in matrices()
    ]
    vmem = pl.BlockSpec(memory_space=pltpu.VMEM)
    smem = pl.BlockSpec(memory_space=pltpu.SMEM)
    hbm = pl.BlockSpec(memory_space=pltpu.HBM)

    def call(kernel, outs, specs, operands, scratch=(), flops=0, moved=0, mib=40):
        return pl.pallas_call(
            kernel,
            out_shape=outs,
            in_specs=specs,
            out_specs=jax.tree.map(lambda _: vmem, outs),
            scratch_shapes=scratch,
            compiler_params=pltpu.CompilerParams(vmem_limit_bytes=mib * 1024 * 1024),
            cost_estimate=pl.CostEstimate(flops=flops, bytes_accessed=moved, transcendentals=0),
        )(*operands)

    def shape(*dims, dtype=F32):
        return jax.ShapeDtypeStruct(dims, dtype)

    def exchange(values):
        pairs = [(i, i ^ 1) for i in range(count) if i ^ 1 < count]
        across_pairs = [(i, i + 1) for i in range(1, count - 1, 2)]
        across_pairs = across_pairs + [(j, i) for i, j in across_pairs]
        second = lax.ppermute(values, "leaf", across_pairs)
        return lax.ppermute(values, "leaf", pairs), second

    wide = 2 * LANES
    kept_shapes = dict(
        oh_own=shape(FACES * leaves, leaves, dtype=BF16),
        oh_near=shape(FACES * leaves, 2 * leaves, dtype=BF16),
        coarse_pick=shape(slots, leaves, dtype=BF16),
        fine_own=shape(4 * slots, leaves, dtype=BF16),
        fine_near=shape(4 * slots, 2 * leaves, dtype=BF16),
        fine_back=shape(leaves, 4 * slots, dtype=BF16),
        coarse_back=shape(leaves, slots, dtype=BF16),
        coarse_count=shape(leaves, TRACE),
        diagonal=shape(leaves, LANES),
        stiff=shape(wide, wide, dtype=BF16),
        mass=shape(leaves, LANES),
        curve=shape(leaves, LANES),
        scale=shape(leaves, LANES),
        traces=shape(*traces.shape, dtype=BF16),
        across=shape(*across.shape, dtype=BF16),
        to_fine=shape(*to_fine.shape, dtype=BF16),
        to_coarse=shape(*to_coarse.shape, dtype=BF16),
        stay=shape(*stay.shape, dtype=BF16),
        face=shape(slots, 1, dtype=jnp.int32),
        partial=shape(leaves, LANES),
    )
    rows = shape(leaves, LANES)
    pack = call(
        prep_kernel,
        shape(leaves + 8, LANES),
        [hbm] * 3,
        (flat, levels, mortars),
        scratch=[
            pltpu.VMEM(flat.shape, F32),
            pltpu.VMEM(levels.shape, jnp.int32),
            pltpu.VMEM(mortars.shape, jnp.int32),
            pltpu.SemaphoreType.DMA((3,)),
        ],
    )
    one, two = exchange(pack)
    sources = (neighbours, nodal_mass, curvature, stiffness, levels, spread, counts)
    loaded = sources + (traces, across, to_fine, to_coarse, stay)
    names = KEPT + ("face", "partial")
    kept = call(
        near_kernel,
        [kept_shapes[name] for name in names],
        [smem, vmem] + [hbm] * len(loaded),
        (place, pack) + loaded,
        scratch=[pltpu.VMEM(source.shape, source.dtype) for source in sources]
        + [pltpu.SemaphoreType.DMA((len(loaded),))],
        flops=2_000_000_000,
        moved=4_000_000,
    )
    kept = dict(zip(names, kept))
    first_kept = [kept[name] for name in KEPT_FIRST]
    image, send, picks, backs, faces, extra = call(
        first_kernel,
        [
            rows, rows, shape(2 * slots, leaves, dtype=BF16),
            shape(leaves, 8 * slots, dtype=BF16), shape(2 * slots, 1, dtype=jnp.int32), rows,
        ],
        [smem] + [vmem] * (5 + len(first_kept)),
        [place, pack, one, two, spread, kept["partial"]] + first_kept,
    )
    one, two = exchange(send)
    partial = call(
        again_kernel,
        rows,
        [vmem] * (2 + len(KEPT_AGAIN)),
        [send, extra] + [kept[name] for name in KEPT_AGAIN],
        flops=2_000_000_000,
        moved=4_000_000,
    )
    stats = call(
        second_kernel,
        shape(1, LANES),
        [vmem] * (8 + len(first_kept)),
        [pack, one, two, partial, image, picks, backs, faces] + first_kept,
    )
    gathered = lax.all_to_all(
        jnp.broadcast_to(stats, (count, LANES)), "leaf", 0, 0, tiled=True
    )
    out = call(final_kernel, shape(*flat.shape), [vmem] * 3, (gathered, flat, image))
    return out.reshape(cotangent.shape)


def solution(mesh):
    placed = (
        P(None, None, "leaf"),
        P(None, "leaf"),
        P(None, "leaf"),
        P(),
        P("leaf"),
        P(None, "leaf"),
        P(None, "leaf"),
    )
    return jax.shard_map(
        on_device, mesh=mesh, in_specs=placed, out_specs=P(None, None, "leaf"), check_vma=False
    )
```

```python
import jax
import jax.numpy as jnp
import ml_dtypes
import numpy as np
from jax import lax
from jax.experimental import pallas as pl
from jax.experimental.pallas import tpu as pltpu
from jax.sharding import PartitionSpec as P

TAU_WEIGHT = 0.15
EPS_WEIGHT = 0.1
FACES = 6
NODES = 64
LANES = 128
TRACE = 256
F32 = jnp.float32
BF16 = jnp.bfloat16


def face_tables():
    node_at = np.zeros((6, 16), dtype=np.int64)
    for face_id in range(6):
        for row_pos in range(4):
            for col_pos in range(4):
                coords = [row_pos, col_pos]
                coords.insert(face_id // 2, 3 * (face_id % 2))
                node_at[face_id, 4 * row_pos + col_pos] = (
                    16 * coords[0] + 4 * coords[1] + coords[2]
                )
    counts = np.zeros(64)
    for face_id in range(6):
        counts[node_at[face_id]] += 1.0
    points = np.array([-1.0, -1.0 / np.sqrt(5.0), 1.0 / np.sqrt(5.0), 1.0])
    halves = np.zeros((2, 4, 4))
    for half_id in range(2):
        target = (points + 2.0 * half_id - 1.0) / 2.0
        for column in range(4):
            lagrange = np.ones(4)
            for other_id in range(4):
                if other_id != column:
                    lagrange = (
                        lagrange * (target - points[other_id]) / (points[column] - points[other_id])
                    )
            halves[half_id, :, column] = lagrange
    mortar = np.stack([np.kron(halves[quarter // 2], halves[quarter % 2]) for quarter in range(4)])
    return node_at, counts, mortar


def two_parts(table):
    high = table.astype(np.float32).astype(ml_dtypes.bfloat16)
    low = (table - high.astype(np.float64)).astype(np.float32).astype(ml_dtypes.bfloat16)
    return np.concatenate([high, low], axis=-1)


def matrices():
    node_at, counts, mortar = face_tables()
    traces = np.zeros((2 * LANES, TRACE))
    across = np.zeros((FACES * 2 * LANES, LANES))
    spread = np.zeros((TRACE, LANES))
    to_fine = np.zeros((4, TRACE, LANES))
    to_coarse = np.zeros((4, TRACE, LANES))
    stay = np.zeros((TRACE, LANES))
    square = sum(mortar[quarter].T @ mortar[quarter] for quarter in range(4))
    for face in range(FACES):
        other = face ^ 1
        for field in range(2):
            base = 32 * face + 16 * field
            lifted = 32 * other + 16 * field
            nodes = 64 * field + node_at[face]
            facing = 64 * field + node_at[other]
            for place in range(16):
                spread[base + place, nodes[place]] = 1.0
                for part in range(2):
                    traces[part * LANES + nodes[place], base + place] = 1.0
                    across[(2 * face + part) * LANES + facing[place], nodes[place]] = 1.0
                stay[base + place, nodes] = square[:, place]
                for quarter in range(4):
                    to_fine[quarter, base + place, facing] = mortar[quarter][:, place]
                    to_coarse[quarter, lifted + place, nodes] = mortar[quarter][place, :]
    small = ml_dtypes.bfloat16
    counts = np.tile(np.concatenate([counts, counts])[None, :], (8, 1)).astype(np.float32)
    return (
        traces.astype(small),
        across.astype(small),
        spread.astype(small),
        np.concatenate(list(two_parts(to_fine)), axis=-1),
        np.concatenate(list(two_parts(to_coarse)), axis=0),
        two_parts(stay),
        counts,
    )


def split(values, axis=1):
    high = values.astype(BF16)
    return jnp.concatenate([high, (values - high.astype(F32)).astype(BF16)], axis=axis)


def dot(left, right):
    return jnp.dot(left, right, preferred_element_type=F32)


def fold(values):
    return values[:, :LANES] + values[:, LANES:]


def dot_parts(values, table):
    high = values.astype(BF16)
    low = (values - high.astype(F32)).astype(BF16)
    return dot(high, table) + dot(low, table)


def pick(index, shape, dim):
    places = lax.broadcasted_iota(jnp.int32, shape, dim).astype(F32).astype(BF16)
    index = jnp.broadcast_to(index.astype(F32), shape).astype(BF16)
    return jnp.where(index == places, jnp.ones(shape, BF16), jnp.zeros(shape, BF16))


def on_face(face, slots):
    return lax.broadcasted_iota(jnp.int32, (slots, TRACE), 1) // 32 == face


def opposite(face):
    return jnp.where(face >= 0, face ^ 1, -1)


def level_rows(levels):
    scale = jnp.left_shift(jnp.ones_like(levels), levels).astype(F32)
    return jnp.broadcast_to(scale, (LANES, levels.shape[1])).T


def fetch(pairs, sems):
    copies = [
        pltpu.make_async_copy(source, target, sems.at[at])
        for at, (source, target) in enumerate(pairs)
    ]
    for copy in copies:
        copy.start()
    return copies


def prep_kernel(cot_hbm, levels_hbm, mortars_hbm, pack_ref, cot_ref, levels_ref, mortars_ref, sems):
    for copy in fetch(
        ((cot_hbm, cot_ref), (levels_hbm, levels_ref), (mortars_hbm, mortars_ref)), sems
    ):
        copy.wait()
    leaves = cot_ref.shape[1]
    scale = jnp.left_shift(jnp.ones_like(levels_ref[...]), levels_ref[...]).astype(F32)
    pack_ref[0:leaves, :] = (cot_ref[...] * scale).T
    table = mortars_ref[...].astype(F32) + 1.0
    pack_ref[leaves : leaves + 8, :] = jnp.concatenate(
        [table, jnp.zeros((2, table.shape[1]), F32)], axis=0
    )


TABLES = ("traces", "across", "to_fine", "to_coarse", "stay")
KEPT = (
    "oh_own", "oh_near", "coarse_pick", "fine_own", "fine_near", "fine_back", "coarse_back",
    "coarse_count", "diagonal", "stiff", "mass", "curve", "scale",
) + TABLES


def own_part(rows, kept):
    slots = kept["coarse_pick"].shape[0]
    parts = split(rows)
    chosen = dot(kept["oh_own"][...], parts).astype(BF16)
    leaves = rows.shape[0]
    moved = jnp.zeros(rows.shape, F32)
    for face in range(FACES):
        moved = moved + dot(
            chosen[leaves * face : leaves * (face + 1), :],
            kept["across"][2 * LANES * face : 2 * LANES * (face + 1), :],
        )
    result = kept["diagonal"][...] * rows - moved + fold(dot(parts, kept["stiff"][...]))
    here = dot(parts, kept["traces"][...]) * kept["coarse_count"][...]
    result = result + fold(dot_parts(here, kept["stay"][...]))
    face = kept["face"][...]
    trace = dot(dot(kept["coarse_pick"][...], parts).astype(BF16), kept["traces"][...])
    trace = jnp.where(on_face(face, slots), trace, 0.0)
    lifted = dot_parts(trace, kept["to_fine"][...])
    lifted = jnp.concatenate(
        [split(fold(lifted[:, TRACE * q : TRACE * (q + 1)])) for q in range(4)], axis=0
    )
    result = result - fold(dot(kept["fine_back"][...], lifted))
    return result - from_fine(kept["fine_own"], parts, kept)


def from_fine(picks, parts, kept):
    slots = kept["coarse_back"].shape[1]
    trace = dot(dot(picks[...], parts).astype(BF16), kept["traces"][...])
    other = on_face(opposite(kept["face"][...]), slots)
    sent = jnp.zeros((slots, 2 * LANES), F32)
    for quarter in range(4):
        part = jnp.where(other, trace[slots * quarter : slots * (quarter + 1), :], 0.0)
        sent = sent + dot_parts(part, kept["to_coarse"][TRACE * quarter : TRACE * (quarter + 1), :])
    return fold(dot(kept["coarse_back"][...], split(fold(sent))))


def fine_count(back, other, spread):
    weights = jnp.where(other, 1.0, 0.0).astype(BF16)
    times = dot(back, jnp.concatenate([weights] * 4, axis=0))
    return dot_parts(times, spread)


def own_index(index, offset):
    return jnp.where(index < 0, -1, index - offset)


def pick_near(first_index, second_index, shape):
    return jnp.concatenate([pick(first_index, shape, 1), pick(second_index, shape, 1)], axis=1)


def to_columns(table):
    return table.astype(F32).T.astype(jnp.int32)


def near_kernel(place_ref, pack_ref, *refs):
    names = ("neighbours", "mass", "curve", "stiffness", "levels", "spread", "counts") + TABLES
    sources = dict(zip(names, refs))
    refs = refs[len(names) :]
    kept = dict(zip(KEPT + ("face", "partial"), refs))
    refs = refs[len(KEPT) + 2 :]
    local = dict(zip(names[: -len(TABLES)], refs))
    sems = refs[-1]
    targets = [local[name] if name in local else kept[name] for name in names]
    copies = fetch(tuple(zip((sources[name] for name in names), targets)), sems)
    leaves = pack_ref.shape[0] - 8
    offset, first = place_ref[0], place_ref[1]
    table = pack_ref[leaves : leaves + 8, :].astype(jnp.int32) - 1
    columns = to_columns(pack_ref[leaves : leaves + 8, :]) - 1
    slots = table.shape[1]
    face = columns[:, 1:2]
    kept["face"][...] = face
    copies[0].wait()
    neighbours = jnp.concatenate(
        [local["neighbours"][...], jnp.full((2, leaves), -1, jnp.int32)], axis=0
    )
    own = to_columns(own_index(neighbours, offset))
    near_one = to_columns(own_index(neighbours, offset + first))
    near_two = to_columns(own_index(neighbours, offset - first))
    for f in range(FACES):
        rows = slice(leaves * f, leaves * (f + 1))
        kept["oh_own"][rows, :] = pick(own[:, f : f + 1], (leaves, leaves), 1)
        kept["oh_near"][rows, :] = pick_near(
            near_one[:, f : f + 1], near_two[:, f : f + 1], (leaves, leaves)
        )
    kept["coarse_pick"][...] = pick(columns[:, 0:1] - offset, (slots, leaves), 1)
    coarse_back = pick(table[0:1, :] - offset, (leaves, slots), 0)
    kept["coarse_back"][...] = coarse_back
    fine_own = own_index(columns, offset)
    fine_one = own_index(columns, offset + first)
    fine_two = own_index(columns, offset - first)
    fine_rows = own_index(table, offset)
    for q in range(4):
        rows = slice(slots * q, slots * (q + 1))
        kept["fine_own"][rows, :] = pick(fine_own[:, 2 + q : 3 + q], (slots, leaves), 1)
        kept["fine_near"][rows, :] = pick_near(
            fine_one[:, 2 + q : 3 + q], fine_two[:, 2 + q : 3 + q], (slots, leaves)
        )
        kept["fine_back"][:, rows] = pick(fine_rows[2 + q : 3 + q, :], (leaves, slots), 0)
    for copy in copies[1:]:
        copy.wait()
    weights = jnp.where(on_face(face, slots), 1.0, 0.0).astype(BF16)
    kept["coarse_count"][...] = dot(coarse_back, weights)
    kept["diagonal"][...] = local["counts"][0:1, :] + fine_count(
        kept["fine_back"][...], on_face(opposite(face), slots), local["spread"][...]
    )
    wide = jnp.concatenate([local["stiffness"][...]] * 2, axis=1)
    wide = jnp.concatenate([wide, wide], axis=0)
    same = (lax.broadcasted_iota(jnp.int32, wide.shape, 0) < NODES) == (
        lax.broadcasted_iota(jnp.int32, wide.shape, 1) < NODES
    )
    wide = split(jnp.where(same, wide, 0.0))
    kept["stiff"][...] = jnp.concatenate([wide, wide], axis=0)
    kept["mass"][...] = jnp.concatenate([local["mass"][...]] * 2, axis=0).T
    curve = local["curve"][...]
    kept["curve"][...] = jnp.concatenate([-curve, jnp.zeros_like(curve)], axis=0).T
    kept["scale"][...] = level_rows(local["levels"][...])
    kept["partial"][...] = own_part(pack_ref[0:leaves, :], kept)


def near_part(rows, kept, picks, backs, faces):
    leaves = rows.shape[0] // 2
    slots = picks.shape[0] // 2
    parts = split(rows)
    chosen = dot(kept["oh_near"][...], parts).astype(BF16)
    moved = jnp.zeros((leaves, LANES), F32)
    for face in range(FACES):
        moved = moved + dot(
            chosen[leaves * face : leaves * (face + 1), :],
            kept["across"][2 * LANES * face : 2 * LANES * (face + 1), :],
        )
    trace = jnp.concatenate(
        [
            dot(picks[slots * k : slots * (k + 1), :], parts[leaves * k : leaves * (k + 1), :])
            for k in range(2)
        ],
        axis=0,
    )
    trace = dot(trace.astype(BF16), kept["traces"][...])
    trace = jnp.where(on_face(faces, 2 * slots), trace, 0.0)
    lifted = dot_parts(trace, kept["to_fine"][...])
    lifted = jnp.concatenate(
        [split(fold(lifted[:, TRACE * q : TRACE * (q + 1)])) for q in range(4)], axis=0
    )
    return -moved - fold(dot(backs, lifted)) - from_fine(kept["fine_near"], parts, kept)


def apply_t(vector, lapped, kept):
    first = lax.broadcasted_iota(jnp.int32, vector.shape, 1) < NODES
    turned = pltpu.roll(lapped, NODES, 1)
    swapped = pltpu.roll(vector, NODES, 1)
    weight = jnp.where(first, -EPS_WEIGHT, TAU_WEIGHT)
    return kept["mass"][...] * vector + kept["curve"][...] * swapped + weight * turned


KEPT_FIRST = ("oh_near", "fine_near", "coarse_back", "mass", "curve", "scale") + TABLES[:4] + ("face",)
KEPT_AGAIN = (
    "oh_own", "coarse_pick", "fine_own", "fine_back", "coarse_back", "coarse_count", "diagonal",
    "stiff", "face",
) + TABLES


def first_kernel(place_ref, pack_ref, one_ref, two_ref, spread_ref, partial_ref, *refs):
    kept = dict(zip(KEPT_FIRST, refs))
    image_ref, send_ref, picks_ref, backs_ref, faces_ref, extra_ref = refs[len(KEPT_FIRST) :]
    leaves = pack_ref.shape[0] - 8
    offset, first = place_ref[0], place_ref[1]
    tables, columns = [], []
    for ref in (one_ref, two_ref):
        table = ref[leaves : leaves + 8, :]
        tables.append(table.astype(jnp.int32) - 1)
        columns.append(to_columns(table) - 1)
    slots = tables[0].shape[1]
    starts = (offset + first, offset - first)
    picks_ref[...] = jnp.concatenate(
        [pick(columns[k][:, 0:1] - starts[k], (slots, leaves), 1) for k in range(2)], axis=0
    )
    faces = jnp.concatenate([column[:, 1:2] for column in columns], axis=0)
    faces_ref[...] = faces
    index = jnp.concatenate([own_index(table, offset) for table in tables], axis=1)
    for q in range(4):
        backs_ref[:, 2 * slots * q : 2 * slots * (q + 1)] = pick(
            index[2 + q : 3 + q, :], (leaves, 2 * slots), 0
        )
    extra = fine_count(backs_ref[...], on_face(opposite(faces), 2 * slots), spread_ref[...])
    extra_ref[...] = extra
    own = pack_ref[0:leaves, :]
    rows = jnp.concatenate([one_ref[0:leaves, :], two_ref[0:leaves, :]], axis=0)
    lapped = partial_ref[...] + extra * own + near_part(
        rows, kept, picks_ref[...], backs_ref[...], faces
    )
    scale = kept["scale"][...]
    image = apply_t(own / scale, lapped, kept)
    image_ref[...] = image
    send_ref[...] = image * scale


def again_kernel(send_ref, extra_ref, *refs):
    kept = dict(zip(KEPT_AGAIN, refs))
    partial_ref = refs[len(KEPT_AGAIN)]
    rows = send_ref[...]
    partial_ref[...] = own_part(rows, kept) + extra_ref[...] * rows


def over(top, bottom):
    return jnp.where(bottom > 0.0, top / jnp.where(bottom > 0.0, bottom, 1.0), 0.0)


def total(values):
    return jnp.sum(values, keepdims=True)


def second_kernel(
    pack_ref, one_ref, two_ref, partial_ref, image_ref, picks_ref, backs_ref, faces_ref, *refs
):
    kept = dict(zip(KEPT_FIRST, refs))
    stats_ref = refs[len(KEPT_FIRST)]
    leaves = pack_ref.shape[0] - 8
    rows = jnp.concatenate([one_ref[...], two_ref[...]], axis=0)
    lapped = partial_ref[...] + near_part(
        rows, kept, picks_ref[...], backs_ref[...], faces_ref[...]
    )
    one = image_ref[...]
    two = apply_t(one, lapped, kept)
    base = pack_ref[0:leaves, :] / kept["scale"][...]
    r00 = jnp.sqrt(total(base * base))
    r01 = over(total(base * one), r00)
    r02 = over(total(base * two), r00)
    one = one - over(r01, r00) * base
    two = two - over(r02, r00) * base
    r11 = jnp.sqrt(total(one * one))
    r12 = over(total(one * two), r11)
    two = two - over(r12, r11) * one
    r22 = jnp.sqrt(total(two * two))
    lane = lax.broadcasted_iota(jnp.int32, stats_ref.shape, 1)
    row = jnp.zeros(stats_ref.shape, F32)
    for at, value in enumerate((r00, r01, r02, r11, r12, r22)):
        row = jnp.where(lane == at, value, row)
    stats_ref[...] = row


def final_kernel(stats_ref, cot_ref, image_ref, out_ref):
    table = stats_ref[...].T
    a0, a1, a2, b1, b2, c2 = [table[at : at + 1, :] for at in range(6)]
    r00_sq = total(a0 * a0)
    r00 = jnp.sqrt(r00_sq)
    f01 = total(a0 * a1) / r00_sq
    f02 = total(a0 * a2) / r00_sq
    a1 = a1 - f01 * a0
    a2 = a2 - f02 * a0
    r11_sq = total(a1 * a1) + total(b1 * b1)
    r11 = jnp.sqrt(r11_sq)
    f12 = (total(a1 * a2) + total(b1 * b2)) / r11_sq
    a2 = a2 - f12 * a1
    b2 = b2 - f12 * b1
    r22 = jnp.sqrt(total(a2 * a2) + total(b2 * b2) + total(c2 * c2))
    rhs_norm = r00
    first_diag = f01
    first_below = r11 / r00
    upper_right = (f02 - first_diag * f01) / first_below
    second_diag = f12 - first_diag
    second_below = r22 / r11
    first_len = jnp.sqrt(first_diag * first_diag + first_below * first_below)
    cos_one = first_diag / first_len
    sin_one = first_below / first_len
    rotated_top = cos_one * upper_right + sin_one * second_diag
    rotated_low = cos_one * second_diag - sin_one * upper_right
    second_len = jnp.sqrt(rotated_low * rotated_low + second_below * second_below)
    cos_two = rotated_low / second_len
    y_two = cos_two * (-sin_one * rhs_norm) / second_len
    y_one = (cos_one * rhs_norm - rotated_top * y_two) / first_len
    on_one = y_two / r11
    on_base = y_one / r00 - on_one * f01
    out_ref[...] = on_base * cot_ref[...] + on_one * image_ref[...].T


def on_device(cotangent, nodal_mass, curvature, stiffness, levels, neighbours, mortars):
    fields, nodes, leaves = cotangent.shape
    slots = mortars.shape[1]
    count = lax.axis_size("leaf")
    flat = cotangent.reshape(fields * nodes, leaves)
    levels = levels.reshape(1, leaves)
    me = lax.axis_index("leaf").astype(jnp.int32)
    place = jnp.stack([me * leaves, leaves - 2 * leaves * (me % 2)])
    traces, across, spread, to_fine, to_coarse, stay, counts = [
        jnp.asarray(table) for table in matrices()
    ]
    vmem = pl.BlockSpec(memory_space=pltpu.VMEM)
    smem = pl.BlockSpec(memory_space=pltpu.SMEM)
    hbm = pl.BlockSpec(memory_space=pltpu.HBM)

    def call(kernel, outs, specs, operands, scratch=(), flops=0, moved=0, mib=40):
        return pl.pallas_call(
            kernel,
            out_shape=outs,
            in_specs=specs,
            out_specs=jax.tree.map(lambda _: vmem, outs),
            scratch_shapes=scratch,
            compiler_params=pltpu.CompilerParams(vmem_limit_bytes=mib * 1024 * 1024),
            cost_estimate=pl.CostEstimate(flops=flops, bytes_accessed=moved, transcendentals=0),
        )(*operands)

    def shape(*dims, dtype=F32):
        return jax.ShapeDtypeStruct(dims, dtype)

    def exchange(values):
        pairs = [(i, i ^ 1) for i in range(count) if i ^ 1 < count]
        across_pairs = [(i, i + 1) for i in range(1, count - 1, 2)]
        across_pairs = across_pairs + [(j, i) for i, j in across_pairs]
        second = lax.ppermute(values, "leaf", across_pairs)
        return lax.ppermute(values, "leaf", pairs), second

    wide = 2 * LANES
    kept_shapes = dict(
        oh_own=shape(FACES * leaves, leaves, dtype=BF16),
        oh_near=shape(FACES * leaves, 2 * leaves, dtype=BF16),
        coarse_pick=shape(slots, leaves, dtype=BF16),
        fine_own=shape(4 * slots, leaves, dtype=BF16),
        fine_near=shape(4 * slots, 2 * leaves, dtype=BF16),
        fine_back=shape(leaves, 4 * slots, dtype=BF16),
        coarse_back=shape(leaves, slots, dtype=BF16),
        coarse_count=shape(leaves, TRACE),
        diagonal=shape(leaves, LANES),
        stiff=shape(wide, wide, dtype=BF16),
        mass=shape(leaves, LANES),
        curve=shape(leaves, LANES),
        scale=shape(leaves, LANES),
        traces=shape(*traces.shape, dtype=BF16),
        across=shape(*across.shape, dtype=BF16),
        to_fine=shape(*to_fine.shape, dtype=BF16),
        to_coarse=shape(*to_coarse.shape, dtype=BF16),
        stay=shape(*stay.shape, dtype=BF16),
        face=shape(slots, 1, dtype=jnp.int32),
        partial=shape(leaves, LANES),
    )
    rows = shape(leaves, LANES)
    def stay_out(*arrays):
        return tuple(pltpu.with_memory_space_constraint(array, pltpu.HBM) for array in arrays)

    pack = call(
        prep_kernel,
        shape(leaves + 8, LANES),
        [hbm] * 3,
        stay_out(flat, levels, mortars),
        scratch=[
            pltpu.VMEM(flat.shape, F32),
            pltpu.VMEM(levels.shape, jnp.int32),
            pltpu.VMEM(mortars.shape, jnp.int32),
            pltpu.SemaphoreType.DMA((3,)),
        ],
    )
    one, two = exchange(pack)
    sources = (neighbours, nodal_mass, curvature, stiffness, levels, spread, counts)
    loaded = sources + (traces, across, to_fine, to_coarse, stay)
    names = KEPT + ("face", "partial")
    kept = call(
        near_kernel,
        [kept_shapes[name] for name in names],
        [smem, vmem] + [hbm] * len(loaded),
        (place, pack) + stay_out(*loaded),
        scratch=[pltpu.VMEM(source.shape, source.dtype) for source in sources]
        + [pltpu.SemaphoreType.DMA((len(loaded),))],
        flops=2_000_000_000,
        moved=4_000_000,
    )
    kept = dict(zip(names, kept))
    first_kept = [kept[name] for name in KEPT_FIRST]
    image, send, picks, backs, faces, extra = call(
        first_kernel,
        [
            rows, rows, shape(2 * slots, leaves, dtype=BF16),
            shape(leaves, 8 * slots, dtype=BF16), shape(2 * slots, 1, dtype=jnp.int32), rows,
        ],
        [smem] + [vmem] * (5 + len(first_kept)),
        [place, pack, one, two, spread, kept["partial"]] + first_kept,
    )
    one, two = exchange(send)
    partial = call(
        again_kernel,
        rows,
        [vmem] * (2 + len(KEPT_AGAIN)),
        [send, extra] + [kept[name] for name in KEPT_AGAIN],
        flops=2_000_000_000,
        moved=4_000_000,
    )
    stats = call(
        second_kernel,
        shape(1, LANES),
        [vmem] * (8 + len(first_kept)),
        [pack, one, two, partial, image, picks, backs, faces] + first_kept,
    )
    gathered = lax.all_to_all(
        jnp.broadcast_to(stats, (count, LANES)), "leaf", 0, 0, tiled=True
    )
    out = call(final_kernel, shape(*flat.shape), [vmem] * 3, (gathered, flat, image))
    return out.reshape(cotangent.shape)


def solution(mesh):
    placed = (
        P(None, None, "leaf"),
        P(None, "leaf"),
        P(None, "leaf"),
        P(),
        P("leaf"),
        P(None, "leaf"),
        P(None, "leaf"),
    )
    return jax.shard_map(
        on_device, mesh=mesh, in_specs=placed, out_specs=P(None, None, "leaf"), check_vma=False
    )
```

```python
import jax
import jax.numpy as jnp
import ml_dtypes
import numpy as np
from jax import lax
from jax.experimental import pallas as pl
from jax.experimental.pallas import tpu as pltpu
from jax.sharding import PartitionSpec as P

TAU_WEIGHT = 0.15
EPS_WEIGHT = 0.1
FACES = 6
NODES = 64
LANES = 128
TRACE = 256
F32 = jnp.float32
BF16 = jnp.bfloat16


def face_tables():
    node_at = np.zeros((6, 16), dtype=np.int64)
    for face_id in range(6):
        for row_pos in range(4):
            for col_pos in range(4):
                coords = [row_pos, col_pos]
                coords.insert(face_id // 2, 3 * (face_id % 2))
                node_at[face_id, 4 * row_pos + col_pos] = (
                    16 * coords[0] + 4 * coords[1] + coords[2]
                )
    counts = np.zeros(64)
    for face_id in range(6):
        counts[node_at[face_id]] += 1.0
    points = np.array([-1.0, -1.0 / np.sqrt(5.0), 1.0 / np.sqrt(5.0), 1.0])
    halves = np.zeros((2, 4, 4))
    for half_id in range(2):
        target = (points + 2.0 * half_id - 1.0) / 2.0
        for column in range(4):
            lagrange = np.ones(4)
            for other_id in range(4):
                if other_id != column:
                    lagrange = (
                        lagrange * (target - points[other_id]) / (points[column] - points[other_id])
                    )
            halves[half_id, :, column] = lagrange
    mortar = np.stack([np.kron(halves[quarter // 2], halves[quarter % 2]) for quarter in range(4)])
    return node_at, counts, mortar


def two_parts(table):
    high = table.astype(np.float32).astype(ml_dtypes.bfloat16)
    low = (table - high.astype(np.float64)).astype(np.float32).astype(ml_dtypes.bfloat16)
    return np.concatenate([high, low], axis=-1)


def matrices():
    node_at, counts, mortar = face_tables()
    traces = np.zeros((2 * LANES, TRACE))
    across = np.zeros((FACES * 2 * LANES, LANES))
    spread = np.zeros((TRACE, LANES))
    to_fine = np.zeros((4, TRACE, LANES))
    to_coarse = np.zeros((4, TRACE, LANES))
    stay = np.zeros((TRACE, LANES))
    square = sum(mortar[quarter].T @ mortar[quarter] for quarter in range(4))
    for face in range(FACES):
        other = face ^ 1
        for field in range(2):
            base = 32 * face + 16 * field
            lifted = 32 * other + 16 * field
            nodes = 64 * field + node_at[face]
            facing = 64 * field + node_at[other]
            for place in range(16):
                spread[base + place, nodes[place]] = 1.0
                for part in range(2):
                    traces[part * LANES + nodes[place], base + place] = 1.0
                    across[(2 * face + part) * LANES + facing[place], nodes[place]] = 1.0
                stay[base + place, nodes] = square[:, place]
                for quarter in range(4):
                    to_fine[quarter, base + place, facing] = mortar[quarter][:, place]
                    to_coarse[quarter, lifted + place, nodes] = mortar[quarter][place, :]
    small = ml_dtypes.bfloat16
    counts = np.tile(np.concatenate([counts, counts])[None, :], (8, 1)).astype(np.float32)
    return (
        traces.astype(small),
        across.astype(small),
        spread.astype(small),
        np.concatenate(list(two_parts(to_fine)), axis=-1),
        np.concatenate(list(two_parts(to_coarse)), axis=0),
        two_parts(stay),
        counts,
    )


def split(values, axis=1):
    high = values.astype(BF16)
    return jnp.concatenate([high, (values - high.astype(F32)).astype(BF16)], axis=axis)


def dot(left, right):
    return jnp.dot(left, right, preferred_element_type=F32)


def fold(values):
    return values[:, :LANES] + values[:, LANES:]


def dot_parts(values, table):
    high = values.astype(BF16)
    low = (values - high.astype(F32)).astype(BF16)
    return dot(high, table) + dot(low, table)


def pick(index, shape, dim):
    places = lax.broadcasted_iota(jnp.int32, shape, dim).astype(F32).astype(BF16)
    index = jnp.broadcast_to(index.astype(F32), shape).astype(BF16)
    return jnp.where(index == places, jnp.ones(shape, BF16), jnp.zeros(shape, BF16))


def on_face(face, slots):
    return lax.broadcasted_iota(jnp.int32, (slots, TRACE), 1) // 32 == face


def opposite(face):
    return jnp.where(face >= 0, face ^ 1, -1)


def level_rows(levels):
    scale = jnp.left_shift(jnp.ones_like(levels), levels).astype(F32)
    return jnp.broadcast_to(scale, (LANES, levels.shape[1])).T


def fetch(pairs, sems):
    copies = [
        pltpu.make_async_copy(source, target, sems.at[at])
        for at, (source, target) in enumerate(pairs)
    ]
    for copy in copies:
        copy.start()
    return copies


def prep_kernel(cot_hbm, levels_hbm, mortars_hbm, pack_ref, cot_ref, levels_ref, mortars_ref, sems):
    for copy in fetch(
        ((cot_hbm, cot_ref), (levels_hbm, levels_ref), (mortars_hbm, mortars_ref)), sems
    ):
        copy.wait()
    leaves = cot_ref.shape[1]
    scale = jnp.left_shift(jnp.ones_like(levels_ref[...]), levels_ref[...]).astype(F32)
    pack_ref[0:leaves, :] = (cot_ref[...] * scale).T
    table = mortars_ref[...].astype(F32) + 1.0
    pack_ref[leaves : leaves + 8, :] = jnp.concatenate(
        [table, jnp.zeros((2, table.shape[1]), F32)], axis=0
    )


TABLES = ("traces", "across", "to_fine", "to_coarse", "stay")
LOCAL = ("neighbours", "mass", "curve", "stiffness", "levels", "spread", "counts")
KEPT = (
    "oh_own", "oh_one", "oh_two", "coarse_pick", "fine_own", "fine_one", "fine_two", "fine_back",
    "coarse_back", "coarse_count", "diagonal", "stiff", "mass", "curve", "scale", "face",
) + TABLES
KEPT_SIDE = ("coarse_back", "face") + TABLES[:4]
KEPT_OWN = (
    "oh_own", "coarse_pick", "fine_own", "fine_back", "coarse_count", "stiff", "mass", "curve",
    "stay",
) + KEPT_SIDE


def from_faces(chosen, across):
    leaves = chosen.shape[0] // FACES
    moved = jnp.zeros((leaves, LANES), F32)
    for face in range(FACES):
        moved = moved + dot(
            chosen[leaves * face : leaves * (face + 1), :],
            across[2 * LANES * face : 2 * LANES * (face + 1), :],
        )
    return moved


def to_fine(picks, backs, face, parts, kept):
    trace = dot(dot(picks, parts).astype(BF16), kept["traces"][...])
    trace = jnp.where(on_face(face, picks.shape[0]), trace, 0.0)
    lifted = dot_parts(trace, kept["to_fine"][...])
    lifted = jnp.concatenate(
        [split(fold(lifted[:, TRACE * q : TRACE * (q + 1)])) for q in range(4)], axis=0
    )
    return fold(dot(backs, lifted))


def to_coarse(picks, parts, kept):
    slots = kept["coarse_back"].shape[1]
    trace = dot(dot(picks, parts).astype(BF16), kept["traces"][...])
    other = on_face(opposite(kept["face"][...]), slots)
    sent = jnp.zeros((slots, 2 * LANES), F32)
    for quarter in range(4):
        part = jnp.where(other, trace[slots * quarter : slots * (quarter + 1), :], 0.0)
        sent = sent + dot_parts(part, kept["to_coarse"][TRACE * quarter : TRACE * (quarter + 1), :])
    return fold(dot(kept["coarse_back"][...], split(fold(sent))))


def placed(lapped):
    first = lax.broadcasted_iota(jnp.int32, lapped.shape, 1) < NODES
    return jnp.where(first, -EPS_WEIGHT, TAU_WEIGHT) * pltpu.roll(lapped, NODES, 1)


def own_part(rows, vector, diagonal, kept):
    parts = split(rows)
    lapped = diagonal * rows + fold(dot(parts, kept["stiff"][...]))
    lapped = lapped - from_faces(dot(kept["oh_own"][...], parts).astype(BF16), kept["across"])
    here = dot(parts, kept["traces"][...]) * kept["coarse_count"][...]
    lapped = lapped + fold(dot_parts(here, kept["stay"][...]))
    lapped = lapped - to_fine(
        kept["coarse_pick"][...], kept["fine_back"][...], kept["face"][...], parts, kept
    )
    lapped = lapped - to_coarse(kept["fine_own"][...], parts, kept)
    swapped = pltpu.roll(vector, NODES, 1)
    return kept["mass"][...] * vector + kept["curve"][...] * swapped + placed(lapped)


def side_part(rows, chooser, fine, picks, backs, face, kept):
    parts = split(rows)
    moved = from_faces(dot(chooser, parts).astype(BF16), kept["across"])
    return -moved - to_fine(picks, backs, face, parts, kept) - to_coarse(fine, parts, kept)


def fine_count(back, other, spread):
    weights = jnp.where(other, 1.0, 0.0).astype(BF16)
    times = dot(back, jnp.concatenate([weights] * 4, axis=0))
    return dot_parts(times, spread)


def own_index(index, offset):
    return jnp.where(index < 0, -1, index - offset)


def to_columns(table):
    return table.astype(F32).T.astype(jnp.int32)


def near_kernel(place_ref, pack_ref, *refs):
    names = LOCAL + TABLES
    sources = dict(zip(names, refs))
    refs = refs[len(names) :]
    kept = dict(zip(KEPT + ("partial",), refs))
    refs = refs[len(KEPT) + 1 :]
    local = dict(zip(LOCAL, refs))
    sems = refs[-1]
    targets = [local[name] if name in local else kept[name] for name in names]
    copies = fetch(tuple(zip((sources[name] for name in names), targets)), sems)
    leaves = pack_ref.shape[0] - 8
    offset, first = place_ref[0], place_ref[1]
    table = pack_ref[leaves : leaves + 8, :].astype(jnp.int32) - 1
    columns = to_columns(pack_ref[leaves : leaves + 8, :]) - 1
    slots = table.shape[1]
    face = columns[:, 1:2]
    kept["face"][...] = face
    copies[0].wait()
    neighbours = jnp.concatenate(
        [local["neighbours"][...], jnp.full((2, leaves), -1, jnp.int32)], axis=0
    )
    for name, start in (("own", offset), ("one", offset + first), ("two", offset - first)):
        places = to_columns(own_index(neighbours, start))
        for f in range(FACES):
            kept["oh_" + name][leaves * f : leaves * (f + 1), :] = pick(
                places[:, f : f + 1], (leaves, leaves), 1
            )
        fine = own_index(columns, start)
        for q in range(4):
            kept["fine_" + name][slots * q : slots * (q + 1), :] = pick(
                fine[:, 2 + q : 3 + q], (slots, leaves), 1
            )
    kept["coarse_pick"][...] = pick(columns[:, 0:1] - offset, (slots, leaves), 1)
    coarse_back = pick(table[0:1, :] - offset, (leaves, slots), 0)
    kept["coarse_back"][...] = coarse_back
    fine_rows = own_index(table, offset)
    for q in range(4):
        kept["fine_back"][:, slots * q : slots * (q + 1)] = pick(
            fine_rows[2 + q : 3 + q, :], (leaves, slots), 0
        )
    for copy in copies[1:]:
        copy.wait()
    weights = jnp.where(on_face(face, slots), 1.0, 0.0).astype(BF16)
    kept["coarse_count"][...] = dot(coarse_back, weights)
    diagonal = local["counts"][0:1, :] + fine_count(
        kept["fine_back"][...], on_face(opposite(face), slots), local["spread"][...]
    )
    kept["diagonal"][...] = diagonal
    wide = jnp.concatenate([local["stiffness"][...]] * 2, axis=1)
    wide = jnp.concatenate([wide, wide], axis=0)
    same = (lax.broadcasted_iota(jnp.int32, wide.shape, 0) < NODES) == (
        lax.broadcasted_iota(jnp.int32, wide.shape, 1) < NODES
    )
    wide = split(jnp.where(same, wide, 0.0))
    kept["stiff"][...] = jnp.concatenate([wide, wide], axis=0)
    kept["mass"][...] = jnp.concatenate([local["mass"][...]] * 2, axis=0).T
    curve = local["curve"][...]
    kept["curve"][...] = jnp.concatenate([-curve, jnp.zeros_like(curve)], axis=0).T
    scale = level_rows(local["levels"][...])
    kept["scale"][...] = scale
    rows = pack_ref[0:leaves, :]
    kept["partial"][...] = own_part(rows, rows / scale, diagonal, kept)


def first_side(place_ref, pack_ref, other_ref, partial_ref, diagonal_ref, spread_ref, oh_ref,
               fine_ref, kept, made, direction):
    picks_ref, backs_ref, face_ref, total_ref = made
    leaves = pack_ref.shape[0] - 8
    offset = place_ref[0]
    table = other_ref[leaves : leaves + 8, :]
    columns = to_columns(table) - 1
    table = table.astype(jnp.int32) - 1
    slots = table.shape[1]
    face = columns[:, 1:2]
    picks = pick(columns[:, 0:1] - (offset + direction * place_ref[1]), (slots, leaves), 1)
    index = own_index(table, offset)
    backs = jnp.concatenate(
        [pick(index[2 + q : 3 + q, :], (leaves, slots), 0) for q in range(4)], axis=1
    )
    extra = fine_count(backs, on_face(opposite(face), slots), spread_ref[...])
    picks_ref[...] = picks
    backs_ref[...] = backs
    face_ref[...] = face
    total_ref[...] = diagonal_ref[...] + extra
    lapped = extra * pack_ref[0:leaves, :] + side_part(
        other_ref[0:leaves, :], oh_ref[...], fine_ref[...], picks, backs, face, kept
    )
    return partial_ref[...] + placed(lapped)


def first_one_kernel(*refs):
    kept = dict(zip(KEPT_SIDE, refs[8:]))
    out_ref = refs[8 + len(KEPT_SIDE)]
    out_ref[...] = first_side(*refs[:8], kept, refs[9 + len(KEPT_SIDE) :], 1)


def first_two_kernel(scale_ref, *refs):
    kept = dict(zip(KEPT_SIDE, refs[8:]))
    image_ref, send_ref = refs[8 + len(KEPT_SIDE) : 10 + len(KEPT_SIDE)]
    image = first_side(*refs[:8], kept, refs[10 + len(KEPT_SIDE) :], -1)
    image_ref[...] = image
    send_ref[...] = image * scale_ref[...]


def total(values):
    return jnp.sum(values, keepdims=True)


def unit(values):
    length = jnp.sqrt(total(values * values))
    return length, values * jnp.where(length > 0.0, 1.0 / jnp.where(length > 0.0, length, 1.0), 0.0)


def in_lanes(shape, values):
    lane = lax.broadcasted_iota(jnp.int32, shape, 1)
    row = jnp.zeros(shape, F32)
    for at, value in enumerate(values):
        row = jnp.where(lane == at, value, row)
    return row


def again_kernel(pack_ref, send_ref, image_ref, scale_ref, total_ref, *refs):
    kept = dict(zip(KEPT_OWN, refs))
    partial_ref, zero_ref, one_ref, stats_ref, turned_ref = refs[len(KEPT_OWN) :]
    image = image_ref[...]
    partial_ref[...] = own_part(send_ref[...], image, total_ref[...], kept)
    turned_ref[...] = image.T
    r00, zero = unit(pack_ref[0 : image.shape[0], :] / scale_ref[...])
    r01 = total(zero * image)
    image = image - r01 * zero
    again = total(zero * image)
    r11, one = unit(image - again * zero)
    zero_ref[...] = zero
    one_ref[...] = one
    stats_ref[...] = in_lanes(stats_ref.shape, (r00, r01 + again, r11))


def second_one_kernel(other_ref, partial_ref, oh_ref, fine_ref, picks_ref, backs_ref, face_ref, *refs):
    kept = dict(zip(KEPT_SIDE, refs))
    refs[len(KEPT_SIDE)][...] = partial_ref[...] + placed(
        side_part(
            other_ref[...], oh_ref[...], fine_ref[...], picks_ref[...], backs_ref[...],
            face_ref[...], kept,
        )
    )


def second_two_kernel(
    zero_ref, one_ref, known_ref, other_ref, partial_ref, oh_ref, fine_ref, picks_ref, backs_ref,
    face_ref, *refs
):
    kept = dict(zip(KEPT_SIDE, refs))
    stats_ref = refs[len(KEPT_SIDE)]
    image = partial_ref[...] + placed(
        side_part(
            other_ref[...], oh_ref[...], fine_ref[...], picks_ref[...], backs_ref[...],
            face_ref[...], kept,
        )
    )
    zero, one = zero_ref[...], one_ref[...]
    r02 = total(zero * image)
    r12 = total(one * image)
    rest = image - r02 * zero - r12 * one
    r22 = jnp.sqrt(total(rest * rest))
    stats_ref[...] = known_ref[...] + in_lanes(stats_ref.shape, (0.0, 0.0, 0.0, r02, r12, r22))


def final_kernel(stats_ref, cot_ref, image_ref, out_ref):
    table = stats_ref[...].T
    a0, a1, b1, a2, b2, c2 = [table[at : at + 1, :] for at in range(6)]
    r00_sq = total(a0 * a0)
    r00 = jnp.sqrt(r00_sq)
    f01 = total(a0 * a1) / r00_sq
    f02 = total(a0 * a2) / r00_sq
    a1 = a1 - f01 * a0
    a2 = a2 - f02 * a0
    r11_sq = total(a1 * a1) + total(b1 * b1)
    r11 = jnp.sqrt(r11_sq)
    f12 = (total(a1 * a2) + total(b1 * b2)) / r11_sq
    a2 = a2 - f12 * a1
    b2 = b2 - f12 * b1
    r22 = jnp.sqrt(total(a2 * a2) + total(b2 * b2) + total(c2 * c2))
    rhs_norm = r00
    first_diag = f01
    first_below = r11 / r00
    upper_right = (f02 - first_diag * f01) / first_below
    second_diag = f12 - first_diag
    second_below = r22 / r11
    first_len = jnp.sqrt(first_diag * first_diag + first_below * first_below)
    cos_one = first_diag / first_len
    sin_one = first_below / first_len
    rotated_top = cos_one * upper_right + sin_one * second_diag
    rotated_low = cos_one * second_diag - sin_one * upper_right
    second_len = jnp.sqrt(rotated_low * rotated_low + second_below * second_below)
    cos_two = rotated_low / second_len
    y_two = cos_two * (-sin_one * rhs_norm) / second_len
    y_one = (cos_one * rhs_norm - rotated_top * y_two) / first_len
    on_one = y_two / r11
    on_base = y_one / r00 - on_one * f01
    out_ref[...] = on_base * cot_ref[...] + on_one * image_ref[...]


def on_device(cotangent, nodal_mass, curvature, stiffness, levels, neighbours, mortars):
    fields, nodes, leaves = cotangent.shape
    slots = mortars.shape[1]
    count = lax.axis_size("leaf")
    flat = cotangent.reshape(fields * nodes, leaves)
    levels = levels.reshape(1, leaves)
    me = lax.axis_index("leaf").astype(jnp.int32)
    place = jnp.stack([me * leaves, leaves - 2 * leaves * (me % 2)])
    traces, across, spread, to_fine_table, to_coarse_table, stay, counts = [
        jnp.asarray(table) for table in matrices()
    ]
    vmem = pl.BlockSpec(memory_space=pltpu.VMEM)
    smem = pl.BlockSpec(memory_space=pltpu.SMEM)
    hbm = pl.BlockSpec(memory_space=pltpu.HBM)

    def call(kernel, outs, specs, operands, scratch=(), flops=0, moved=0, mib=40):
        return pl.pallas_call(
            kernel,
            out_shape=outs,
            in_specs=specs,
            out_specs=jax.tree.map(lambda _: vmem, outs),
            scratch_shapes=scratch,
            compiler_params=pltpu.CompilerParams(vmem_limit_bytes=mib * 1024 * 1024),
            cost_estimate=pl.CostEstimate(flops=flops, bytes_accessed=moved, transcendentals=0),
        )(*operands)

    def shape(*dims, dtype=F32):
        return jax.ShapeDtypeStruct(dims, dtype)

    def exchange(values):
        pairs = [(i, i ^ 1) for i in range(count) if i ^ 1 < count]
        across_pairs = [(i, i + 1) for i in range(1, count - 1, 2)]
        across_pairs = across_pairs + [(j, i) for i, j in across_pairs]
        second = lax.ppermute(values, "leaf", across_pairs)
        return lax.ppermute(values, "leaf", pairs), second

    wide = 2 * LANES
    rows = shape(leaves, LANES)
    chooser = shape(FACES * leaves, leaves, dtype=BF16)
    fine = shape(4 * slots, leaves, dtype=BF16)
    kept_shapes = dict(
        oh_own=chooser,
        oh_one=chooser,
        oh_two=chooser,
        coarse_pick=shape(slots, leaves, dtype=BF16),
        fine_own=fine,
        fine_one=fine,
        fine_two=fine,
        fine_back=shape(leaves, 4 * slots, dtype=BF16),
        coarse_back=shape(leaves, slots, dtype=BF16),
        coarse_count=shape(leaves, TRACE),
        diagonal=rows,
        stiff=shape(wide, wide, dtype=BF16),
        mass=rows,
        curve=rows,
        scale=rows,
        face=shape(slots, 1, dtype=jnp.int32),
        traces=shape(*traces.shape, dtype=BF16),
        across=shape(*across.shape, dtype=BF16),
        to_fine=shape(*to_fine_table.shape, dtype=BF16),
        to_coarse=shape(*to_coarse_table.shape, dtype=BF16),
        stay=shape(*stay.shape, dtype=BF16),
        partial=rows,
    )

    def stay_out(*arrays):
        return tuple(pltpu.with_memory_space_constraint(array, pltpu.HBM) for array in arrays)

    pack = call(
        prep_kernel,
        shape(leaves + 8, LANES),
        [hbm] * 3,
        stay_out(flat, levels, mortars),
        scratch=[
            pltpu.VMEM(flat.shape, F32),
            pltpu.VMEM(levels.shape, jnp.int32),
            pltpu.VMEM(mortars.shape, jnp.int32),
            pltpu.SemaphoreType.DMA((3,)),
        ],
    )
    one, two = exchange(pack)
    sources = (neighbours, nodal_mass, curvature, stiffness, levels, spread, counts)
    loaded = sources + (traces, across, to_fine_table, to_coarse_table, stay)
    names = KEPT + ("partial",)
    kept = call(
        near_kernel,
        [kept_shapes[name] for name in names],
        [smem, vmem] + [hbm] * len(loaded),
        (place, pack) + stay_out(*loaded),
        scratch=[pltpu.VMEM(source.shape, source.dtype) for source in sources]
        + [pltpu.SemaphoreType.DMA((len(loaded),))],
        flops=2_000_000_000,
        moved=4_000_000,
    )
    kept = dict(zip(names, kept))
    side = [kept[name] for name in KEPT_SIDE]
    made = [
        shape(slots, leaves, dtype=BF16), shape(leaves, 4 * slots, dtype=BF16),
        shape(slots, 1, dtype=jnp.int32), rows,
    ]
    partial, *made_one = call(
        first_one_kernel,
        [rows] + made,
        [smem] + [vmem] * (7 + len(side)),
        [place, pack, one, kept["partial"], kept["diagonal"], spread, kept["oh_one"],
         kept["fine_one"]] + side,
        flops=1_000_000_000,
        moved=2_000_000,
    )
    image, send, *made_two = call(
        first_two_kernel,
        [rows, rows] + made,
        [vmem, smem] + [vmem] * (7 + len(side)),
        [kept["scale"], place, pack, two, partial, made_one[3], spread, kept["oh_two"],
         kept["fine_two"]] + side,
    )
    one, two = exchange(send)
    own = [kept[name] for name in KEPT_OWN]
    partial, zero, unit_one, known, turned = call(
        again_kernel,
        [rows, rows, rows, shape(1, LANES), shape(LANES, leaves)],
        [vmem] * (5 + len(own)),
        [pack, send, image, kept["scale"], made_two[3]] + own,
        flops=2_000_000_000,
        moved=4_000_000,
    )
    partial = call(
        second_one_kernel,
        rows,
        [vmem] * (7 + len(side)),
        [one, partial, kept["oh_one"], kept["fine_one"], *made_one[:3]] + side,
        flops=1_000_000_000,
        moved=2_000_000,
    )
    stats = call(
        second_two_kernel,
        shape(1, LANES),
        [vmem] * (10 + len(side)),
        [zero, unit_one, known, two, partial, kept["oh_two"], kept["fine_two"], *made_two[:3]]
        + side,
    )
    gathered = lax.all_to_all(
        jnp.broadcast_to(stats, (count, LANES)), "leaf", 0, 0, tiled=True
    )
    out = call(final_kernel, shape(*flat.shape), [vmem] * 3, (gathered, flat, turned))
    return out.reshape(cotangent.shape)


def solution(mesh):
    placed = (
        P(None, None, "leaf"),
        P(None, "leaf"),
        P(None, "leaf"),
        P(),
        P("leaf"),
        P(None, "leaf"),
        P(None, "leaf"),
    )
    return jax.shard_map(
        on_device, mesh=mesh, in_specs=placed, out_specs=P(None, None, "leaf"), check_vma=False
    )
```

```python
import jax
import jax.numpy as jnp
import ml_dtypes
import numpy as np
from jax import lax
from jax.experimental import pallas as pl
from jax.experimental.pallas import tpu as pltpu
from jax.sharding import PartitionSpec as P

TAU_WEIGHT = 0.15
EPS_WEIGHT = 0.1
FACES = 6
NODES = 64
LANES = 128
TRACE = 256
F32 = jnp.float32
BF16 = jnp.bfloat16


def face_tables():
    node_at = np.zeros((6, 16), dtype=np.int64)
    for face_id in range(6):
        for row_pos in range(4):
            for col_pos in range(4):
                coords = [row_pos, col_pos]
                coords.insert(face_id // 2, 3 * (face_id % 2))
                node_at[face_id, 4 * row_pos + col_pos] = (
                    16 * coords[0] + 4 * coords[1] + coords[2]
                )
    points = np.array([-1.0, -1.0 / np.sqrt(5.0), 1.0 / np.sqrt(5.0), 1.0])
    halves = np.zeros((2, 4, 4))
    for half_id in range(2):
        target = (points + 2.0 * half_id - 1.0) / 2.0
        for column in range(4):
            lagrange = np.ones(4)
            for other_id in range(4):
                if other_id != column:
                    lagrange = (
                        lagrange * (target - points[other_id]) / (points[column] - points[other_id])
                    )
            halves[half_id, :, column] = lagrange
    mortar = np.stack([np.kron(halves[quarter // 2], halves[quarter % 2]) for quarter in range(4)])
    return node_at, mortar


def two_parts(table):
    high = table.astype(np.float32).astype(ml_dtypes.bfloat16)
    low = (table - high.astype(np.float64)).astype(np.float32).astype(ml_dtypes.bfloat16)
    return np.concatenate([high, low], axis=-1)


def matrices():
    node_at, mortar = face_tables()
    traces = np.zeros((2 * LANES, TRACE))
    across = np.zeros((FACES, 2 * LANES, LANES))
    to_fine = np.zeros((4, TRACE, LANES))
    to_coarse = np.zeros((4, TRACE, LANES))
    stay = np.zeros((TRACE, LANES))
    square = sum(mortar[quarter].T @ mortar[quarter] for quarter in range(4))
    for face in range(FACES):
        other = face ^ 1
        for field in range(2):
            base = 32 * face + 16 * field
            lifted = 32 * other + 16 * field
            nodes = 64 * field + node_at[face]
            facing = 64 * field + node_at[other]
            for place in range(16):
                for part in range(2):
                    traces[part * LANES + nodes[place], base + place] = 1.0
                    across[face, part * LANES + facing[place], nodes[place]] = 1.0
                stay[base + place, nodes] = square[:, place]
                for quarter in range(4):
                    to_fine[quarter, base + place, facing] = mortar[quarter][:, place]
                    to_coarse[quarter, lifted + place, nodes] = mortar[quarter][place, :]
    small = ml_dtypes.bfloat16
    pairs = [np.concatenate([across[f], across[f + 1]], axis=1) for f in (0, 2, 4)]
    return np.concatenate(
        [traces.astype(small)]
        + [pair.astype(small) for pair in pairs]
        + list(two_parts(to_fine))
        + list(two_parts(to_coarse))
        + [two_parts(stay)],
        axis=0,
    )


TRACES_AT, ACROSS_AT, FINE_AT, COARSE_AT, STAY_AT = 0, 256, 1024, 2048, 3072


def split(values, axis=1):
    high = values.astype(BF16)
    return jnp.concatenate([high, (values - high.astype(F32)).astype(BF16)], axis=axis)


def dot(left, right):
    return jnp.dot(left, right, preferred_element_type=F32)


def fold(values):
    return values[:, :LANES] + values[:, LANES:]


def dot_parts(values, table):
    products = dot(split(values, 0), table)
    return products[: values.shape[0], :] + products[values.shape[0] :, :]


def pick(index, shape, dim):
    places = lax.broadcasted_iota(jnp.int32, shape, dim).astype(F32).astype(BF16)
    index = jnp.broadcast_to(index.astype(F32), shape).astype(BF16)
    return jnp.where(index == places, jnp.ones(shape, BF16), jnp.zeros(shape, BF16))


def on_face(face, slots):
    return lax.broadcasted_iota(jnp.int32, (slots, TRACE), 1) // 32 == face


def face_nodes(face, shape):
    node = lax.broadcasted_iota(jnp.int32, shape, 1) % NODES
    place = jnp.right_shift(node, 4 - 2 * (face // 2)) & 3
    return (place == 3 * (face % 2)) & (face >= 0)


def opposite(face):
    return jnp.where(face >= 0, face ^ 1, -1)


def level_rows(levels):
    scale = jnp.left_shift(jnp.ones_like(levels), levels).astype(F32)
    return jnp.broadcast_to(scale, (LANES, levels.shape[1])).T


def fetch(pairs, sems):
    copies = [
        pltpu.make_async_copy(source, target, sems.at[at])
        for at, (source, target) in enumerate(pairs)
    ]
    for copy in copies:
        copy.start()
    return copies


def prep_kernel(cot_hbm, levels_hbm, mortars_hbm, pack_ref, cot_ref, levels_ref, mortars_ref, sems):
    for copy in fetch(
        ((cot_hbm, cot_ref), (levels_hbm, levels_ref), (mortars_hbm, mortars_ref)), sems
    ):
        copy.wait()
    leaves = cot_ref.shape[1]
    scale = jnp.left_shift(jnp.ones_like(levels_ref[...]), levels_ref[...]).astype(F32)
    pack_ref[0:leaves, :] = (cot_ref[...] * scale).T
    table = mortars_ref[...].astype(F32) + 1.0
    pack_ref[leaves : leaves + 8, :] = jnp.concatenate(
        [table, jnp.zeros((2, table.shape[1]), F32)], axis=0
    )


LOCAL = ("neighbours", "mass", "curve", "stiffness", "levels")
KEPT = (
    "own", "one", "two", "own_back", "coarse_count", "diagonal", "stiff", "mass", "curve", "scale",
    "face",
)
KEPT_SIDE = ("own_back", "face")
KEPT_OWN = KEPT_SIDE + ("own", "coarse_count", "stiff", "mass", "curve")


def from_rows(parts, chooser, picks, backs, coarse_face, kept, table):
    own_back, face = kept["own_back"], kept["face"]
    slots, leaves = own_back.shape[1], own_back.shape[0]
    chosen = dot(jnp.concatenate([chooser, picks], axis=0), parts).astype(BF16)
    moved = jnp.zeros((leaves, LANES), F32)
    for f in range(FACES):
        start = ACROSS_AT + 256 * (f // 2)
        moved = moved + dot(
            chosen[leaves * f : leaves * (f + 1), :],
            table[start : start + 256, LANES * (f % 2) : LANES * (f % 2 + 1)],
        )
    trace = dot(chosen[leaves * FACES :, :], table[TRACES_AT : TRACES_AT + 256, :])
    coarse = jnp.where(on_face(coarse_face, slots), trace[4 * slots :, :], 0.0)
    sent = [
        split(fold(dot_parts(coarse, table[FINE_AT + 256 * q : FINE_AT + 256 * (q + 1), :])))
        for q in range(4)
    ]
    other = on_face(opposite(face[...]), slots)
    fine = jnp.concatenate(
        [jnp.where(other, trace[slots * q : slots * (q + 1), :], 0.0) for q in range(4)], axis=1
    )
    sent.append(split(fold(dot_parts(fine, table[COARSE_AT : COARSE_AT + 1024, :]))))
    backs = jnp.concatenate([backs, own_back[...]], axis=1)
    return moved + fold(dot(backs, jnp.concatenate(sent, axis=0)))


def placed(lapped):
    first = lax.broadcasted_iota(jnp.int32, lapped.shape, 1) < NODES
    return jnp.where(first, -EPS_WEIGHT, TAU_WEIGHT) * pltpu.roll(lapped, NODES, 1)


def own_part(rows, vector, diagonal, backs, kept, table):
    parts = split(rows)
    slots = kept["own_back"].shape[1]
    above = kept["own"].shape[0] - slots
    here = dot(parts, table[TRACES_AT : TRACES_AT + 256, :]) * kept["coarse_count"][...]
    lapped = (
        diagonal * rows
        + fold(dot(parts, kept["stiff"][...]))
        + fold(dot_parts(here, table[STAY_AT : STAY_AT + 256, :]))
        - from_rows(
            parts, kept["own"][:above, :], kept["own"][above:, :], backs, kept["face"][...], kept,
            table,
        )
    )
    swapped = pltpu.roll(vector, NODES, 1)
    return kept["mass"][...] * vector + kept["curve"][...] * swapped + placed(lapped)


def fine_count(back, face):
    weights = jnp.where(
        face_nodes(opposite(face), (face.shape[0], LANES)), 1.0, 0.0
    ).astype(BF16)
    return dot(back, jnp.concatenate([weights] * 4, axis=0))


def own_index(index, offset):
    return jnp.where(index < 0, -1, index - offset)


def to_columns(table):
    return table.astype(F32).T.astype(jnp.int32)


def fine_backs(table, offset, leaves):
    index = own_index(table, offset)
    return jnp.concatenate(
        [pick(index[2 + q : 3 + q, :], (leaves, table.shape[1]), 0) for q in range(4)], axis=1
    )


def near_kernel(place_ref, pack_ref, table, *refs):
    sources = refs[: len(LOCAL)]
    refs = refs[len(LOCAL) :]
    kept = dict(zip(KEPT + ("fine_back", "partial"), refs))
    refs = refs[len(KEPT) + 2 :]
    local = dict(zip(LOCAL, refs))
    copies = fetch(tuple(zip(sources, refs)), refs[-1])
    leaves = pack_ref.shape[0] - 8
    offset, first = place_ref[0], place_ref[1]
    mortars = pack_ref[leaves : leaves + 8, :].astype(jnp.int32) - 1
    columns = to_columns(pack_ref[leaves : leaves + 8, :]) - 1
    slots = mortars.shape[1]
    face = columns[:, 1:2]
    kept["face"][...] = face
    backs = fine_backs(mortars, offset, leaves)
    kept["fine_back"][...] = backs
    own_back = pick(mortars[0:1, :] - offset, (leaves, slots), 0)
    kept["own_back"][...] = own_back
    copies[0].wait()
    neighbours = jnp.concatenate(
        [local["neighbours"][...], jnp.full((2, leaves), -1, jnp.int32)], axis=0
    )
    for name, start in (("own", offset), ("one", offset + first), ("two", offset - first)):
        places = to_columns(own_index(neighbours, start))
        for f in range(FACES):
            kept[name][leaves * f : leaves * (f + 1), :] = pick(
                places[:, f : f + 1], (leaves, leaves), 1
            )
        fine = own_index(columns, start)
        for q in range(4):
            at = leaves * FACES + slots * q
            kept[name][at : at + slots, :] = pick(fine[:, 2 + q : 3 + q], (slots, leaves), 1)
    at = leaves * FACES + slots * 4
    kept["own"][at : at + slots, :] = pick(columns[:, 0:1] - offset, (slots, leaves), 1)
    weights = jnp.where(on_face(face, slots), 1.0, 0.0).astype(BF16)
    kept["coarse_count"][...] = dot(own_back, weights)
    diagonal = fine_count(backs, face)
    for f in range(FACES):
        diagonal = diagonal + jnp.where(face_nodes(jnp.int32(f), diagonal.shape), 1.0, 0.0)
    kept["diagonal"][...] = diagonal
    for copy in copies[1:]:
        copy.wait()
    wide = jnp.concatenate([local["stiffness"][...]] * 2, axis=1)
    wide = jnp.concatenate([wide, wide], axis=0)
    same = (lax.broadcasted_iota(jnp.int32, wide.shape, 0) < NODES) == (
        lax.broadcasted_iota(jnp.int32, wide.shape, 1) < NODES
    )
    wide = split(jnp.where(same, wide, 0.0))
    kept["stiff"][...] = jnp.concatenate([wide, wide], axis=0)
    kept["mass"][...] = jnp.concatenate([local["mass"][...]] * 2, axis=0).T
    curve = local["curve"][...]
    kept["curve"][...] = jnp.concatenate([-curve, jnp.zeros_like(curve)], axis=0).T
    scale = level_rows(local["levels"][...])
    kept["scale"][...] = scale
    rows = pack_ref[0:leaves, :]
    kept["partial"][...] = own_part(rows, rows / scale, diagonal, backs, kept, table)


def first_side(
    place_ref, table, pack_ref, other_ref, partial_ref, diagonal_ref, chooser_ref, kept, made,
    direction,
):
    picks_ref, backs_ref, face_ref, total_ref = made
    leaves = pack_ref.shape[0] - 8
    mortars = other_ref[leaves : leaves + 8, :]
    columns = to_columns(mortars) - 1
    mortars = mortars.astype(jnp.int32) - 1
    slots = mortars.shape[1]
    face = columns[:, 1:2]
    start = place_ref[0] + direction * place_ref[1]
    picks = pick(columns[:, 0:1] - start, (slots, leaves), 1)
    backs = fine_backs(mortars, place_ref[0], leaves)
    extra = fine_count(backs, face)
    picks_ref[...] = picks
    backs_ref[...] = backs
    face_ref[...] = face
    total_ref[...] = diagonal_ref[...] + extra
    lapped = extra * pack_ref[0:leaves, :] - from_rows(
        split(other_ref[0:leaves, :]), chooser_ref[...], picks, backs, face, kept, table
    )
    return partial_ref[...] + placed(lapped)


def first_one_kernel(*refs):
    kept = dict(zip(KEPT_SIDE, refs[7:]))
    refs, rest = refs[:7], refs[7 + len(KEPT_SIDE) :]
    rest[0][...] = first_side(*refs, kept, rest[1:], 1)


def first_two_kernel(scale_ref, *refs):
    kept = dict(zip(KEPT_SIDE, refs[7:]))
    refs, rest = refs[:7], refs[7 + len(KEPT_SIDE) :]
    image = first_side(*refs, kept, rest[2:], -1)
    rest[0][...] = image
    rest[1][...] = image * scale_ref[...]


def total(values):
    return jnp.sum(values, keepdims=True)


def unit(values):
    length = jnp.sqrt(total(values * values))
    return length, values * jnp.where(length > 0.0, 1.0 / jnp.where(length > 0.0, length, 1.0), 0.0)


def in_lanes(shape, values):
    lane = lax.broadcasted_iota(jnp.int32, shape, 1)
    row = jnp.zeros(shape, F32)
    for at, value in enumerate(values):
        row = jnp.where(lane == at, value, row)
    return row


def again_kernel(
    table, pack_ref, send_ref, image_ref, scale_ref, total_ref, fine_back_ref, *refs
):
    kept = dict(zip(KEPT_OWN, refs))
    partial_ref, zero_ref, one_ref, stats_ref, turned_ref = refs[len(KEPT_OWN) :]
    image = image_ref[...]
    partial_ref[...] = own_part(
        send_ref[...], image, total_ref[...], fine_back_ref[...], kept, table
    )
    turned_ref[...] = image.T
    r00, zero = unit(pack_ref[0 : image.shape[0], :] / scale_ref[...])
    r01 = total(zero * image)
    image = image - r01 * zero
    again = total(zero * image)
    r11, one = unit(image - again * zero)
    zero_ref[...] = zero
    one_ref[...] = one
    stats_ref[...] = in_lanes(stats_ref.shape, (r00, r01 + again, r11))


def second_side(table, other_ref, partial_ref, chooser_ref, picks_ref, backs_ref, face_ref, kept):
    lapped = from_rows(
        split(other_ref[...]), chooser_ref[...], picks_ref[...], backs_ref[...], face_ref[...],
        kept, table,
    )
    return partial_ref[...] - placed(lapped)


def second_one_kernel(*refs):
    refs, rest = refs[:7], refs[7:]
    rest[len(KEPT_SIDE)][...] = second_side(*refs, dict(zip(KEPT_SIDE, rest)))


def second_two_kernel(zero_ref, one_ref, known_ref, *refs):
    refs, rest = refs[:7], refs[7:]
    stats_ref = rest[len(KEPT_SIDE)]
    image = second_side(*refs, dict(zip(KEPT_SIDE, rest)))
    zero, one = zero_ref[...], one_ref[...]
    r02 = total(zero * image)
    r12 = total(one * image)
    rest = image - r02 * zero - r12 * one
    r22 = jnp.sqrt(total(rest * rest))
    stats_ref[...] = known_ref[...] + in_lanes(stats_ref.shape, (0.0, 0.0, 0.0, r02, r12, r22))


def final_kernel(stats_ref, cot_ref, image_ref, out_ref):
    table = stats_ref[...].T
    a0, a1, b1, a2, b2, c2 = [table[at : at + 1, :] for at in range(6)]
    r00_sq = total(a0 * a0)
    r00 = jnp.sqrt(r00_sq)
    f01 = total(a0 * a1) / r00_sq
    f02 = total(a0 * a2) / r00_sq
    a1 = a1 - f01 * a0
    a2 = a2 - f02 * a0
    r11_sq = total(a1 * a1) + total(b1 * b1)
    r11 = jnp.sqrt(r11_sq)
    f12 = (total(a1 * a2) + total(b1 * b2)) / r11_sq
    a2 = a2 - f12 * a1
    b2 = b2 - f12 * b1
    r22 = jnp.sqrt(total(a2 * a2) + total(b2 * b2) + total(c2 * c2))
    rhs_norm = r00
    first_diag = f01
    first_below = r11 / r00
    upper_right = (f02 - first_diag * f01) / first_below
    second_diag = f12 - first_diag
    second_below = r22 / r11
    first_len = jnp.sqrt(first_diag * first_diag + first_below * first_below)
    cos_one = first_diag / first_len
    sin_one = first_below / first_len
    rotated_top = cos_one * upper_right + sin_one * second_diag
    rotated_low = cos_one * second_diag - sin_one * upper_right
    second_len = jnp.sqrt(rotated_low * rotated_low + second_below * second_below)
    cos_two = rotated_low / second_len
    y_two = cos_two * (-sin_one * rhs_norm) / second_len
    y_one = (cos_one * rhs_norm - rotated_top * y_two) / first_len
    on_one = y_two / r11
    on_base = y_one / r00 - on_one * f01
    out_ref[...] = on_base * cot_ref[...] + on_one * image_ref[...]


def on_device(cotangent, nodal_mass, curvature, stiffness, levels, neighbours, mortars):
    fields, nodes, leaves = cotangent.shape
    slots = mortars.shape[1]
    count = lax.axis_size("leaf")
    flat = cotangent.reshape(fields * nodes, leaves)
    levels = levels.reshape(1, leaves)
    me = lax.axis_index("leaf").astype(jnp.int32)
    place = jnp.stack([me * leaves, leaves - 2 * leaves * (me % 2)])
    table = jnp.asarray(matrices())
    vmem = pl.BlockSpec(memory_space=pltpu.VMEM)
    smem = pl.BlockSpec(memory_space=pltpu.SMEM)
    hbm = pl.BlockSpec(memory_space=pltpu.HBM)

    def call(kernel, outs, specs, operands, scratch=(), flops=0, moved=0, mib=40):
        return pl.pallas_call(
            kernel,
            out_shape=outs,
            in_specs=specs,
            out_specs=jax.tree.map(lambda _: vmem, outs),
            scratch_shapes=scratch,
            compiler_params=pltpu.CompilerParams(vmem_limit_bytes=mib * 1024 * 1024),
            cost_estimate=pl.CostEstimate(flops=flops, bytes_accessed=moved, transcendentals=0),
        )(*operands)

    def shape(*dims, dtype=F32):
        return jax.ShapeDtypeStruct(dims, dtype)

    def exchange(values):
        pairs = [(i, i ^ 1) for i in range(count) if i ^ 1 < count]
        across_pairs = [(i, i + 1) for i in range(1, count - 1, 2)]
        across_pairs = across_pairs + [(j, i) for i, j in across_pairs]
        second = lax.ppermute(values, "leaf", across_pairs)
        return lax.ppermute(values, "leaf", pairs), second

    wide = 2 * LANES
    rows = shape(leaves, LANES)
    chosen = FACES * leaves + 4 * slots
    picks = shape(slots, leaves, dtype=BF16)
    backs = shape(leaves, 4 * slots, dtype=BF16)
    face = shape(slots, 1, dtype=jnp.int32)
    kept_shapes = dict(
        own=shape(chosen + slots, leaves, dtype=BF16),
        one=shape(chosen, leaves, dtype=BF16),
        two=shape(chosen, leaves, dtype=BF16),
        own_back=shape(leaves, slots, dtype=BF16),
        coarse_count=shape(leaves, TRACE),
        diagonal=rows,
        stiff=shape(wide, wide, dtype=BF16),
        mass=rows,
        curve=rows,
        scale=rows,
        face=face,
        fine_back=backs,
        partial=rows,
    )

    def stay_out(*arrays):
        return tuple(pltpu.with_memory_space_constraint(array, pltpu.HBM) for array in arrays)

    pack = call(
        prep_kernel,
        shape(leaves + 8, LANES),
        [hbm] * 3,
        stay_out(flat, levels, mortars),
        scratch=[
            pltpu.VMEM(flat.shape, F32),
            pltpu.VMEM(levels.shape, jnp.int32),
            pltpu.VMEM(mortars.shape, jnp.int32),
            pltpu.SemaphoreType.DMA((3,)),
        ],
        flops=10_000_000_000,
        moved=4_000_000,
    )
    one, two = exchange(pack)
    sources = (neighbours, nodal_mass, curvature, stiffness, levels)
    names = KEPT + ("fine_back", "partial")
    kept = call(
        near_kernel,
        [kept_shapes[name] for name in names],
        [smem, vmem, vmem] + [hbm] * len(sources),
        (place, pack, table) + stay_out(*sources),
        scratch=[pltpu.VMEM(source.shape, source.dtype) for source in sources]
        + [pltpu.SemaphoreType.DMA((len(sources),))],
        flops=2_000_000_000,
        moved=4_000_000,
    )
    kept = dict(zip(names, kept))
    side = [kept[name] for name in KEPT_SIDE]
    made = [picks, backs, face, rows]
    partial, *made_one = call(
        first_one_kernel,
        [rows] + made,
        [smem] + [vmem] * (6 + len(side)),
        [place, table, pack, one, kept["partial"], kept["diagonal"], kept["one"]] + side,
        flops=1_000_000_000,
        moved=2_000_000,
    )
    image, send, *made_two = call(
        first_two_kernel,
        [rows, rows] + made,
        [vmem, smem] + [vmem] * (6 + len(side)),
        [kept["scale"], place, table, pack, two, partial, made_one[3], kept["two"]] + side,
    )
    one, two = exchange(send)
    own = [kept[name] for name in KEPT_OWN]
    partial, zero, unit_one, known, turned = call(
        again_kernel,
        [rows, rows, rows, shape(1, LANES), shape(LANES, leaves)],
        [vmem] * (7 + len(own)),
        [table, pack, send, image, kept["scale"], made_two[3], kept["fine_back"]] + own,
        flops=2_000_000_000,
        moved=4_000_000,
    )
    partial = call(
        second_one_kernel,
        rows,
        [vmem] * (7 + len(side)),
        [table, one, partial, kept["one"], *made_one[:3]] + side,
        flops=1_000_000_000,
        moved=2_000_000,
    )
    stats = call(
        second_two_kernel,
        shape(1, LANES),
        [vmem] * (10 + len(side)),
        [zero, unit_one, known, table, two, partial, kept["two"], *made_two[:3]] + side,
    )
    gathered = lax.all_to_all(
        jnp.broadcast_to(stats, (count, LANES)), "leaf", 0, 0, tiled=True
    )
    out = call(final_kernel, shape(*flat.shape), [vmem] * 3, (gathered, flat, turned))
    return out.reshape(cotangent.shape)


def solution(mesh):
    placed = (
        P(None, None, "leaf"),
        P(None, "leaf"),
        P(None, "leaf"),
        P(),
        P("leaf"),
        P(None, "leaf"),
        P(None, "leaf"),
    )
    return jax.shard_map(
        on_device, mesh=mesh, in_specs=placed, out_specs=P(None, None, "leaf"), check_vma=False
    )
```

```python
import jax
import jax.numpy as jnp
import ml_dtypes
import numpy as np
from jax import lax
from jax.experimental import pallas as pl
from jax.experimental.pallas import tpu as pltpu
from jax.sharding import PartitionSpec as P

TAU_WEIGHT = 0.15
EPS_WEIGHT = 0.1
FACES = 6
NODES = 64
LANES = 128
F32 = jnp.float32
BF16 = jnp.bfloat16


def face_tables():
    node_at = np.zeros((6, 16), dtype=np.int64)
    for face_id in range(6):
        for row_pos in range(4):
            for col_pos in range(4):
                coords = [row_pos, col_pos]
                coords.insert(face_id // 2, 3 * (face_id % 2))
                node_at[face_id, 4 * row_pos + col_pos] = (
                    16 * coords[0] + 4 * coords[1] + coords[2]
                )
    points = np.array([-1.0, -1.0 / np.sqrt(5.0), 1.0 / np.sqrt(5.0), 1.0])
    halves = np.zeros((2, 4, 4))
    for half_id in range(2):
        target = (points + 2.0 * half_id - 1.0) / 2.0
        for column in range(4):
            lagrange = np.ones(4)
            for other_id in range(4):
                if other_id != column:
                    lagrange = (
                        lagrange * (target - points[other_id]) / (points[column] - points[other_id])
                    )
            halves[half_id, :, column] = lagrange
    mortar = np.stack([np.kron(halves[quarter // 2], halves[quarter % 2]) for quarter in range(4)])
    return node_at, mortar


def two_parts(table):
    high = table.astype(np.float32).astype(ml_dtypes.bfloat16)
    low = (table - high.astype(np.float64)).astype(np.float32).astype(ml_dtypes.bfloat16)
    return np.concatenate([high, low], axis=-1)


def matrices():
    node_at, mortar = face_tables()
    traces = np.zeros((2 * LANES, 2 * LANES))
    to_fine = np.zeros((4, 2 * LANES, LANES))
    to_coarse = np.zeros((4, 2 * LANES, LANES))
    stay = np.zeros((2 * LANES, LANES))
    square = sum(mortar[quarter].T @ mortar[quarter] for quarter in range(4))
    for face in range(FACES):
        for field in range(2):
            nodes = 64 * field + node_at[face]
            for part in range(2):
                for place in range(16):
                    at = part * LANES + 32 * (face // 2) + 16 * field + place
                    traces[part * LANES + nodes[place], at] = 1.0
                    stay[at, nodes] = -square[:, place]
                    for quarter in range(4):
                        to_fine[quarter, at, nodes] = mortar[quarter][:, place]
                        to_coarse[quarter, at, nodes] = mortar[quarter][place, :]
    return np.concatenate(
        [traces.astype(ml_dtypes.bfloat16)]
        + list(two_parts(to_fine))
        + list(two_parts(to_coarse))
        + [two_parts(stay)],
        axis=0,
    )


TRACES_AT, FINE_AT, COARSE_AT, STAY_AT, TABLE_ROWS = 0, 256, 1280, 2304, 2560


def split(values, axis=1):
    high = values.astype(BF16)
    return jnp.concatenate([high, (values - high.astype(F32)).astype(BF16)], axis=axis)


def dot(left, right):
    return jnp.dot(left, right, preferred_element_type=F32)


def fold(values):
    return values[:, :LANES] + values[:, LANES:]


def pick(index, shape, dim):
    places = lax.broadcasted_iota(jnp.int32, shape, dim).astype(F32).astype(BF16)
    index = jnp.broadcast_to(index.astype(F32), shape).astype(BF16)
    return jnp.where(index == places, jnp.ones(shape, BF16), jnp.zeros(shape, BF16))


def on_axis(face):
    lane = lax.broadcasted_iota(jnp.int32, (1, 2 * LANES), 1)
    axis = jnp.right_shift(face, 1)
    return jnp.where((jnp.right_shift(lane, 5) & 3) == axis, 1.0, 0.0).astype(BF16)


def face_nodes(face):
    lane = lax.broadcasted_iota(jnp.int32, (1, LANES), 1)
    axis = jnp.right_shift(face, 1)
    place = jnp.right_shift(lane, 4 - 2 * axis) & 3
    return jnp.where((place == 3 * (face & 1)) & (face >= 0), 1.0, 0.0)


def opposite(face):
    return jnp.where(face >= 0, face ^ 1, -1)


def level_rows(levels):
    scale = jnp.left_shift(jnp.ones_like(levels), levels).astype(F32)
    return jnp.broadcast_to(scale, (LANES, levels.shape[1])).T


def fetch(pairs, sems):
    copies = [
        pltpu.make_async_copy(source, target, sems.at[at])
        for at, (source, target) in enumerate(pairs)
    ]
    for copy in copies:
        copy.start()
    return copies


def prep_kernel(cot_hbm, levels_hbm, mortars_hbm, pack_ref, cot_ref, levels_ref, mortars_ref, sems):
    for copy in fetch(
        ((cot_hbm, cot_ref), (levels_hbm, levels_ref), (mortars_hbm, mortars_ref)), sems
    ):
        copy.wait()
    leaves = cot_ref.shape[1]
    scale = jnp.left_shift(jnp.ones_like(levels_ref[...]), levels_ref[...]).astype(F32)
    pack_ref[0:leaves, :] = (cot_ref[...] * scale).T
    table = mortars_ref[...].astype(F32) + 1.0
    pack_ref[leaves : leaves + 8, :] = jnp.concatenate(
        [table, jnp.zeros((2, table.shape[1]), F32)], axis=0
    )


CHOSEN = (
    "own", "one", "two", "own_fine", "one_fine", "two_fine", "own_pick", "own_back", "fine_back",
    "face",
)
LOCAL = ("diagonal", "stiff", "mass", "curve", "scale")
KEPT_SIDE = ("own_back", "face")
KEPT_OWN = KEPT_SIDE + ("own", "own_fine", "own_pick", "fine_back", "stiff", "mass", "curve")


def from_rows(parts, chooser, picks, backs, coarse_face, kept, table, own=False):
    own_back, face = kept["own_back"], kept["face"][...]
    slots, leaves = own_back.shape[1], own_back.shape[0]
    faces, fine = chooser
    chosen = dot(jnp.concatenate([fine[...], picks], axis=0), parts).astype(BF16)
    other, coarse_other = opposite(face), opposite(coarse_face)
    nodes = [face_nodes(other)] * 4 + [face_nodes(coarse_face)]
    nodes = jnp.concatenate([mask.astype(BF16) for mask in nodes], axis=0)
    trace = dot(
        chosen * jnp.concatenate([nodes, nodes], axis=1), table[TRACES_AT : TRACES_AT + 256, :]
    ).astype(BF16)
    axis = on_axis(face)
    trace = [trace[slots * q : slots * (q + 1), :] * axis for q in range(4)] + [
        trace[4 * slots :, :] * (axis if own else on_axis(coarse_face))
    ]
    mask = face_nodes(coarse_other)
    sent = [
        split(mask * fold(dot(trace[4], table[FINE_AT + 256 * q : FINE_AT + 256 * (q + 1), :])))
        for q in range(4)
    ]
    last = TABLE_ROWS if own else STAY_AT
    back = dot(jnp.concatenate(trace if own else trace[:4], axis=1), table[COARSE_AT:last, :])
    sent.append(split(face_nodes(face) * fold(back)))
    mortars = dot(
        jnp.concatenate([backs, own_back[...]], axis=1), jnp.concatenate(sent, axis=0)
    )
    result = fold(mortars)
    seen = dot(faces[...], parts)
    for f in range(FACES):
        shift = 3 * 4 ** (2 - f // 2)
        part = fold(seen[leaves * f : leaves * (f + 1), :])
        part = pltpu.roll(part, shift if f % 2 else LANES - shift, 1)
        result = result + face_nodes(jnp.int32(f)) * part
    return result


def placed(lapped):
    first = lax.broadcasted_iota(jnp.int32, lapped.shape, 1) < NODES
    return jnp.where(first, -EPS_WEIGHT, TAU_WEIGHT) * pltpu.roll(lapped, NODES, 1)


def own_part(rows, vector, diagonal, kept, table):
    parts = split(rows)
    lapped = (
        diagonal * rows
        + fold(dot(parts, kept["stiff"][...]))
        - from_rows(
            parts, (kept["own"], kept["own_fine"]), kept["own_pick"][...],
            kept["fine_back"][...], kept["face"][...], kept, table, own=True,
        )
    )
    swapped = pltpu.roll(vector, NODES, 1)
    return kept["mass"][...] * vector + kept["curve"][...] * swapped + placed(lapped)


def fine_count(back, face):
    weights = face_nodes(opposite(face)).astype(BF16)
    return dot(back, jnp.concatenate([weights] * 4, axis=0))


def own_index(index, offset):
    return jnp.where(index < 0, -1, index - offset)


def to_columns(table):
    return table.astype(F32).T.astype(jnp.int32)


def fine_backs(table, offset, leaves):
    index = own_index(table, offset)
    return jnp.concatenate(
        [pick(index[2 + q : 3 + q, :], (leaves, table.shape[1]), 0) for q in range(4)], axis=1
    )


def choose_kernel(place_ref, pack_ref, neighbours_ref, same_ref, *refs):
    made = dict(zip(CHOSEN, refs))
    same_ref[...] = pack_ref[...]
    leaves = pack_ref.shape[0] - 8
    offset, first = place_ref[0:1, 0:1], place_ref[0:1, 1:2]
    mortars = pack_ref[leaves : leaves + 8, :].astype(jnp.int32) - 1
    columns = to_columns(pack_ref[leaves : leaves + 8, :]) - 1
    slots = mortars.shape[1]
    made["face"][...] = columns[:, 1:2]
    made["fine_back"][...] = fine_backs(mortars, offset, leaves)
    made["own_back"][...] = pick(mortars[0:1, :] - offset, (leaves, slots), 0)
    made["own_pick"][...] = pick(columns[:, 0:1] - offset, (slots, leaves), 1)
    neighbours = jnp.concatenate(
        [neighbours_ref[...], jnp.full((2, leaves), -1, jnp.int32)], axis=0
    )
    for name, start in (("own", offset), ("one", offset + first), ("two", offset - first)):
        places = to_columns(own_index(neighbours, start))
        for f in range(FACES):
            made[name][leaves * f : leaves * (f + 1), :] = pick(
                places[:, f : f + 1], (leaves, leaves), 1
            )
        fine = own_index(columns, start)
        for q in range(4):
            made[name + "_fine"][slots * q : slots * (q + 1), :] = pick(
                fine[:, 2 + q : 3 + q], (slots, leaves), 1
            )


def near_kernel(pack_ref, table, mass_ref, curve_ref, stiffness_ref, levels_ref, *refs):
    names = KEPT_OWN[:6]
    kept = dict(zip(names + LOCAL, refs))
    partial_ref = refs[len(names) + len(LOCAL)]
    leaves = pack_ref.shape[0] - 8
    diagonal = fine_count(kept["fine_back"][...], kept["face"][...]) + sum(
        face_nodes(jnp.int32(f)) for f in range(FACES)
    )
    kept["diagonal"][...] = diagonal
    wide = jnp.concatenate([stiffness_ref[...]] * 2, axis=1)
    wide = jnp.concatenate([wide, wide], axis=0)
    same = (lax.broadcasted_iota(jnp.int32, wide.shape, 0) < NODES) == (
        lax.broadcasted_iota(jnp.int32, wide.shape, 1) < NODES
    )
    wide = split(jnp.where(same, wide, 0.0))
    kept["stiff"][...] = jnp.concatenate([wide, wide], axis=0)
    kept["mass"][...] = jnp.concatenate([mass_ref[...]] * 2, axis=0).T
    curve = curve_ref[...]
    kept["curve"][...] = jnp.concatenate([-curve, jnp.zeros_like(curve)], axis=0).T
    scale = level_rows(levels_ref[...])
    kept["scale"][...] = scale
    rows = pack_ref[0:leaves, :]
    partial_ref[...] = own_part(rows, rows / scale, diagonal, kept, table)


def first_side(
    place_ref, table, pack_ref, other_ref, partial_ref, diagonal_ref, faces_ref, fine_ref, kept,
    made, direction,
):
    picks_ref, backs_ref, face_ref, total_ref = made
    leaves = pack_ref.shape[0] - 8
    mortars = other_ref[leaves : leaves + 8, :]
    columns = to_columns(mortars) - 1
    mortars = mortars.astype(jnp.int32) - 1
    slots = mortars.shape[1]
    face = columns[:, 1:2]
    offset = place_ref[0:1, 0:1]
    start = offset + direction * place_ref[0:1, 1:2]
    picks = pick(columns[:, 0:1] - start, (slots, leaves), 1)
    backs = fine_backs(mortars, offset, leaves)
    extra = fine_count(backs, face)
    picks_ref[...] = picks
    backs_ref[...] = backs
    face_ref[...] = face
    total_ref[...] = diagonal_ref[...] + extra
    lapped = extra * pack_ref[0:leaves, :] - from_rows(
        split(other_ref[0:leaves, :]), (faces_ref, fine_ref), picks, backs, face, kept, table
    )
    return partial_ref[...] + placed(lapped)


def first_one_kernel(*refs):
    kept = dict(zip(KEPT_SIDE, refs[8:]))
    refs, rest = refs[:8], refs[8 + len(KEPT_SIDE) :]
    rest[0][...] = first_side(*refs, kept, rest[1:], 1)


def first_two_kernel(scale_ref, *refs):
    kept = dict(zip(KEPT_SIDE, refs[8:]))
    refs, rest = refs[:8], refs[8 + len(KEPT_SIDE) :]
    image = first_side(*refs, kept, rest[2:], -1)
    rest[0][...] = image
    rest[1][...] = image * scale_ref[...]


def total(values):
    return jnp.sum(values, keepdims=True)


def unit(values):
    length = jnp.sqrt(total(values * values))
    return length, values * jnp.where(length > 0.0, 1.0 / jnp.where(length > 0.0, length, 1.0), 0.0)


def in_lanes(shape, values):
    lane = lax.broadcasted_iota(jnp.int32, shape, 1)
    row = jnp.zeros(shape, F32)
    for at, value in enumerate(values):
        row = jnp.where(lane == at, value, row)
    return row


def factor_kernel(pack_ref, send_ref, image_ref, scale_ref, *refs):
    same_ref, zero_ref, one_ref, stats_ref, turned_ref = refs
    same_ref[...] = send_ref[...]
    image = image_ref[...]
    turned_ref[...] = image.T
    r00, zero = unit(pack_ref[0 : image.shape[0], :] / scale_ref[...])
    r01 = total(zero * image)
    image = image - r01 * zero
    again = total(zero * image)
    r11, one = unit(image - again * zero)
    zero_ref[...] = zero
    one_ref[...] = one
    stats_ref[...] = in_lanes(stats_ref.shape, (r00, r01 + again, r11))


def again_kernel(table, send_ref, image_ref, total_ref, *refs):
    kept = dict(zip(KEPT_OWN, refs))
    refs[len(KEPT_OWN)][...] = own_part(
        send_ref[...], image_ref[...], total_ref[...], kept, table
    )


def second_side(
    table, other_ref, partial_ref, faces_ref, fine_ref, picks_ref, backs_ref, face_ref, kept
):
    lapped = from_rows(
        split(other_ref[...]), (faces_ref, fine_ref), picks_ref[...], backs_ref[...],
        face_ref[...], kept, table,
    )
    return partial_ref[...] - placed(lapped)


def second_one_kernel(*refs):
    refs, rest = refs[:8], refs[8:]
    rest[len(KEPT_SIDE)][...] = second_side(*refs, dict(zip(KEPT_SIDE, rest)))


def second_two_kernel(zero_ref, one_ref, known_ref, *refs):
    refs, rest = refs[:8], refs[8:]
    stats_ref = rest[len(KEPT_SIDE)]
    image = second_side(*refs, dict(zip(KEPT_SIDE, rest)))
    zero, one = zero_ref[...], one_ref[...]
    r02 = total(zero * image)
    r12 = total(one * image)
    rest = image - r02 * zero - r12 * one
    r22 = jnp.sqrt(total(rest * rest))
    stats_ref[...] = known_ref[...] + in_lanes(stats_ref.shape, (0.0, 0.0, 0.0, r02, r12, r22))


def final_kernel(stats_ref, cot_ref, image_ref, out_ref):
    table = stats_ref[...].T
    a0, a1, b1, a2, b2, c2 = [table[at : at + 1, :] for at in range(6)]
    r00_sq = total(a0 * a0)
    r00 = jnp.sqrt(r00_sq)
    f01 = total(a0 * a1) / r00_sq
    f02 = total(a0 * a2) / r00_sq
    a1 = a1 - f01 * a0
    a2 = a2 - f02 * a0
    r11_sq = total(a1 * a1) + total(b1 * b1)
    r11 = jnp.sqrt(r11_sq)
    f12 = (total(a1 * a2) + total(b1 * b2)) / r11_sq
    a2 = a2 - f12 * a1
    b2 = b2 - f12 * b1
    r22 = jnp.sqrt(total(a2 * a2) + total(b2 * b2) + total(c2 * c2))
    rhs_norm = r00
    first_diag = f01
    first_below = r11 / r00
    upper_right = (f02 - first_diag * f01) / first_below
    second_diag = f12 - first_diag
    second_below = r22 / r11
    first_len = jnp.sqrt(first_diag * first_diag + first_below * first_below)
    cos_one = first_diag / first_len
    sin_one = first_below / first_len
    rotated_top = cos_one * upper_right + sin_one * second_diag
    rotated_low = cos_one * second_diag - sin_one * upper_right
    second_len = jnp.sqrt(rotated_low * rotated_low + second_below * second_below)
    cos_two = rotated_low / second_len
    y_two = cos_two * (-sin_one * rhs_norm) / second_len
    y_one = (cos_one * rhs_norm - rotated_top * y_two) / first_len
    on_one = y_two / r11
    on_base = y_one / r00 - on_one * f01
    out_ref[...] = on_base * cot_ref[...] + on_one * image_ref[...]


def on_device(cotangent, nodal_mass, curvature, stiffness, levels, neighbours, mortars):
    fields, nodes, leaves = cotangent.shape
    slots = mortars.shape[1]
    count = lax.axis_size("leaf")
    flat = cotangent.reshape(fields * nodes, leaves)
    levels = levels.reshape(1, leaves)
    me = lax.axis_index("leaf").astype(jnp.int32)
    place = jnp.stack([me * leaves, leaves - 2 * leaves * (me & 1)]).reshape(1, 2)
    table = jnp.asarray(matrices())
    vmem = pl.BlockSpec(memory_space=pltpu.VMEM)
    hbm = pl.BlockSpec(memory_space=pltpu.HBM)

    def call(kernel, outs, specs, operands, scratch=(), flops=0, moved=0, mib=40):
        return pl.pallas_call(
            kernel,
            out_shape=outs,
            in_specs=specs,
            out_specs=jax.tree.map(lambda _: vmem, outs),
            scratch_shapes=scratch,
            compiler_params=pltpu.CompilerParams(vmem_limit_bytes=mib * 1024 * 1024),
            cost_estimate=pl.CostEstimate(flops=flops, bytes_accessed=moved, transcendentals=0),
        )(*operands)

    def shape(*dims, dtype=F32):
        return jax.ShapeDtypeStruct(dims, dtype)

    pairs_one = [(i, i ^ 1) for i in range(count) if i ^ 1 < count]
    pairs_two = [(i, i + 1) for i in range(1, count - 1, 2)]
    pairs_two = pairs_two + [(j, i) for i, j in pairs_two]

    wide = 2 * LANES
    rows = shape(leaves, LANES)
    faces = shape(FACES * leaves, leaves, dtype=BF16)
    fine = shape(4 * slots, leaves, dtype=BF16)
    picks = shape(slots, leaves, dtype=BF16)
    backs = shape(leaves, 4 * slots, dtype=BF16)
    face = shape(slots, 1, dtype=jnp.int32)
    shapes = dict(
        own=faces,
        one=faces,
        two=faces,
        own_fine=fine,
        one_fine=fine,
        two_fine=fine,
        own_pick=picks,
        own_back=shape(leaves, slots, dtype=BF16),
        fine_back=backs,
        face=face,
        diagonal=rows,
        stiff=shape(wide, wide, dtype=BF16),
        mass=rows,
        curve=rows,
        scale=rows,
    )

    def stay_out(*arrays):
        return tuple(pltpu.with_memory_space_constraint(array, pltpu.HBM) for array in arrays)

    pack = call(
        prep_kernel,
        shape(leaves + 8, LANES),
        [hbm] * 3,
        stay_out(flat, levels, mortars),
        scratch=[
            pltpu.VMEM(flat.shape, F32),
            pltpu.VMEM(levels.shape, jnp.int32),
            pltpu.VMEM(mortars.shape, jnp.int32),
            pltpu.SemaphoreType.DMA((3,)),
        ],
        flops=10_000_000_000,
        moved=4_000_000,
    )
    two = lax.ppermute(pack, "leaf", pairs_two)
    same, *chosen = call(
        choose_kernel,
        [shape(leaves + 8, LANES)] + [shapes[name] for name in CHOSEN],
        [vmem] * 3,
        (place, pack, neighbours),
        flops=1_000_000_000,
        moved=2_000_000,
    )
    kept = dict(zip(CHOSEN, chosen))
    one = lax.ppermute(same, "leaf", pairs_one)
    own = KEPT_OWN[:6]
    *local, partial = call(
        near_kernel,
        [shapes[name] for name in LOCAL] + [rows],
        [vmem] * (6 + len(own)),
        [pack, table, nodal_mass, curvature, stiffness, levels] + [kept[name] for name in own],
        flops=2_000_000_000,
        moved=4_000_000,
    )
    kept.update(zip(LOCAL, local))
    side = [kept[name] for name in KEPT_SIDE]
    made = [picks, backs, face, rows]
    partial, *made_one = call(
        first_one_kernel,
        [rows] + made,
        [vmem] * (8 + len(side)),
        [place, table, pack, one, partial, kept["diagonal"], kept["one"],
         kept["one_fine"]] + side,
        flops=1_000_000_000,
        moved=2_000_000,
    )
    image, send, *made_two = call(
        first_two_kernel,
        [rows, rows] + made,
        [vmem] * (9 + len(side)),
        [kept["scale"], place, table, pack, two, partial, made_one[3], kept["two"],
         kept["two_fine"]] + side,
    )
    two = lax.ppermute(send, "leaf", pairs_two)
    same, zero, unit_one, known, turned = call(
        factor_kernel,
        [rows, rows, rows, shape(1, LANES), shape(LANES, leaves)],
        [vmem] * 4,
        [pack, send, image, kept["scale"]],
        flops=1_000_000_000,
        moved=2_000_000,
    )
    one = lax.ppermute(same, "leaf", pairs_one)
    partial = call(
        again_kernel,
        rows,
        [vmem] * (4 + len(KEPT_OWN)),
        [table, send, image, made_two[3]] + [kept[name] for name in KEPT_OWN],
        flops=2_000_000_000,
        moved=4_000_000,
    )
    partial = call(
        second_one_kernel,
        rows,
        [vmem] * (8 + len(side)),
        [table, one, partial, kept["one"], kept["one_fine"], *made_one[:3]] + side,
        flops=1_000_000_000,
        moved=2_000_000,
    )
    stats = call(
        second_two_kernel,
        shape(1, LANES),
        [vmem] * (11 + len(side)),
        [zero, unit_one, known, table, two, partial, kept["two"], kept["two_fine"], *made_two[:3]]
        + side,
    )
    gathered = lax.all_to_all(
        jnp.broadcast_to(stats, (count, LANES)), "leaf", 0, 0, tiled=True
    )
    out = call(final_kernel, shape(*flat.shape), [vmem] * 3, (gathered, flat, turned))
    return out.reshape(cotangent.shape)


def solution(mesh):
    placed = (
        P(None, None, "leaf"),
        P(None, "leaf"),
        P(None, "leaf"),
        P(),
        P("leaf"),
        P(None, "leaf"),
        P(None, "leaf"),
    )
    return jax.shard_map(
        on_device, mesh=mesh, in_specs=placed, out_specs=P(None, None, "leaf"), check_vma=False
    )
```

```python
import jax
import jax.numpy as jnp
import ml_dtypes
import numpy as np
from jax import lax
from jax.experimental import pallas as pl
from jax.experimental.pallas import tpu as pltpu
from jax.sharding import PartitionSpec as P

TAU_WEIGHT = 0.15
EPS_WEIGHT = 0.1
FACES = 6
NODES = 64
LANES = 128
F32 = jnp.float32
BF16 = jnp.bfloat16


def face_tables():
    node_at = np.zeros((6, 16), dtype=np.int64)
    for face_id in range(6):
        for row_pos in range(4):
            for col_pos in range(4):
                coords = [row_pos, col_pos]
                coords.insert(face_id // 2, 3 * (face_id % 2))
                node_at[face_id, 4 * row_pos + col_pos] = (
                    16 * coords[0] + 4 * coords[1] + coords[2]
                )
    points = np.array([-1.0, -1.0 / np.sqrt(5.0), 1.0 / np.sqrt(5.0), 1.0])
    halves = np.zeros((2, 4, 4))
    for half_id in range(2):
        target = (points + 2.0 * half_id - 1.0) / 2.0
        for column in range(4):
            lagrange = np.ones(4)
            for other_id in range(4):
                if other_id != column:
                    lagrange = (
                        lagrange * (target - points[other_id]) / (points[column] - points[other_id])
                    )
            halves[half_id, :, column] = lagrange
    mortar = np.stack([np.kron(halves[quarter // 2], halves[quarter % 2]) for quarter in range(4)])
    return node_at, mortar


def two_parts(table):
    high = table.astype(np.float32).astype(ml_dtypes.bfloat16)
    low = (table - high.astype(np.float64)).astype(np.float32).astype(ml_dtypes.bfloat16)
    return np.concatenate([high, low], axis=-1)


def matrices():
    node_at, mortar = face_tables()
    traces = np.zeros((2 * LANES, 2 * LANES))
    to_fine = np.zeros((4, 2 * LANES, LANES))
    to_coarse = np.zeros((4, 2 * LANES, LANES))
    stay = np.zeros((2 * LANES, LANES))
    square = sum(mortar[quarter].T @ mortar[quarter] for quarter in range(4))
    for face in range(FACES):
        for field in range(2):
            nodes = 64 * field + node_at[face]
            for part in range(2):
                for place in range(16):
                    at = part * LANES + 32 * (face // 2) + 16 * field + place
                    traces[part * LANES + nodes[place], at] = 1.0
                    stay[at, nodes] = -square[:, place]
                    for quarter in range(4):
                        to_fine[quarter, at, nodes] = mortar[quarter][:, place]
                        to_coarse[quarter, at, nodes] = mortar[quarter][place, :]
    return np.concatenate(
        [traces.astype(ml_dtypes.bfloat16)]
        + list(two_parts(to_fine))
        + list(two_parts(to_coarse))
        + [two_parts(stay)],
        axis=0,
    )


TRACES_AT, FINE_AT, COARSE_AT, STAY_AT, TABLE_ROWS = 0, 256, 1280, 2304, 2560


def split(values, axis=1):
    high = values.astype(BF16)
    return jnp.concatenate([high, (values - high.astype(F32)).astype(BF16)], axis=axis)


def dot(left, right):
    return jnp.dot(left, right, preferred_element_type=F32)


def fold(values):
    return values[:, :LANES] + values[:, LANES:]


def pick(index, shape, dim):
    places = lax.broadcasted_iota(jnp.int32, shape, dim).astype(F32).astype(BF16)
    index = jnp.broadcast_to(index.astype(F32), shape).astype(BF16)
    return jnp.where(index == places, jnp.ones(shape, BF16), jnp.zeros(shape, BF16))


def on_axis(face):
    lane = lax.broadcasted_iota(jnp.int32, (1, 2 * LANES), 1)
    axis = jnp.right_shift(face, 1)
    return jnp.where((jnp.right_shift(lane, 5) & 3) == axis, 1.0, 0.0).astype(BF16)


def face_nodes(face):
    lane = lax.broadcasted_iota(jnp.int32, (1, LANES), 1)
    axis = jnp.right_shift(face, 1)
    place = jnp.right_shift(lane, 4 - 2 * axis) & 3
    return jnp.where((place == 3 * (face & 1)) & (face >= 0), 1.0, 0.0)


def opposite(face):
    return jnp.where(face >= 0, face ^ 1, -1)


def level_rows(levels):
    scale = jnp.left_shift(jnp.ones_like(levels), levels).astype(F32)
    return jnp.broadcast_to(scale, (LANES, levels.shape[1])).T


def fetch(pairs, sems):
    copies = [
        pltpu.make_async_copy(source, target, sems.at[at])
        for at, (source, target) in enumerate(pairs)
    ]
    for copy in copies:
        copy.start()
    return copies


def prep_kernel(cot_hbm, levels_hbm, mortars_hbm, pack_ref, cot_ref, levels_ref, mortars_ref, sems):
    for copy in fetch(
        ((cot_hbm, cot_ref), (levels_hbm, levels_ref), (mortars_hbm, mortars_ref)), sems
    ):
        copy.wait()
    leaves = cot_ref.shape[1]
    scale = jnp.left_shift(jnp.ones_like(levels_ref[...]), levels_ref[...]).astype(F32)
    pack_ref[0:leaves, :] = (cot_ref[...] * scale).T
    table = mortars_ref[...].astype(F32) + 1.0
    halves = [scale[:, k * table.shape[1] : (k + 1) * table.shape[1]] for k in range(2)]
    pack_ref[leaves : leaves + 8, :] = jnp.concatenate([table] + halves, axis=0)


CHOSEN = (
    "own", "one", "own_fine", "one_fine", "own_pick", "own_back", "fine_back", "face",
)
MADE = ("diagonal", "stiff", "mass", "curve", "scale", "one_pick", "one_back", "one_face")


def across_faces(seen):
    leaves = seen.shape[0] // FACES
    result = jnp.zeros((leaves, LANES), F32)
    for f in range(FACES):
        shift = 3 * 4 ** (2 - f // 2)
        part = fold(seen[leaves * f : leaves * (f + 1), :])
        part = pltpu.roll(part, shift if f % 2 else LANES - shift, 1)
        result = result + face_nodes(jnp.int32(f)) * part
    return result


def side_traces(chosen, faces, table):
    nodes = jnp.concatenate([face_nodes(face).astype(BF16) for face in faces], axis=0)
    axes = jnp.concatenate([on_axis(face) for face in faces], axis=0)
    nodes = jnp.concatenate([nodes, nodes], axis=1)
    trace = dot(chosen.astype(BF16) * nodes, table[TRACES_AT : TRACES_AT + 256, :])
    return trace.astype(BF16) * axes


def lift(trace, faces, table):
    mask = jnp.concatenate([face_nodes(opposite(face)) for face in faces], axis=0)
    return [
        split(mask * fold(dot(trace, table[FINE_AT + 256 * q : FINE_AT + 256 * (q + 1), :])))
        for q in range(4)
    ]


def lower(traces, face, table, last):
    back = dot(jnp.concatenate(traces, axis=1), table[COARSE_AT:last, :])
    return split(face_nodes(face) * fold(back))


def from_blocks(parts, faces, fine, picks, backs, coarse_faces, face, own_back, table, own):
    slots = own_back.shape[1]
    rows = jnp.concatenate(parts, axis=0)
    seen = dot(jnp.concatenate(faces, axis=1), rows)
    chosen = [dot(jnp.concatenate(fine, axis=1), rows)]
    chosen += [dot(pick_rows, part) for pick_rows, part in zip(picks, parts)]
    trace = side_traces(
        jnp.concatenate(chosen, axis=0), [opposite(face)] * 4 + coarse_faces, table
    )
    quarters = [trace[slots * q : slots * (q + 1), :] for q in range(4)]
    sent = lift(trace[4 * slots :, :], coarse_faces, table)
    ordered = [
        sent[q][slots * k : slots * (k + 1), :] for k in range(len(parts)) for q in range(4)
    ]
    if own:
        quarters.append(trace[4 * slots : 5 * slots, :])
    ordered.append(lower(quarters, face, table, TABLE_ROWS if own else STAY_AT))
    mortars = dot(jnp.concatenate(backs + [own_back], axis=1), jnp.concatenate(ordered, axis=0))
    return fold(mortars) + across_faces(seen)


def placed(lapped):
    first = lax.broadcasted_iota(jnp.int32, lapped.shape, 1) < NODES
    return jnp.where(first, -EPS_WEIGHT, TAU_WEIGHT) * pltpu.roll(lapped, NODES, 1)


def fine_count(backs, faces):
    weights = [face_nodes(opposite(face)).astype(BF16) for face in faces for _ in range(4)]
    return dot(jnp.concatenate(backs, axis=1), jnp.concatenate(weights, axis=0))


def own_index(index, offset):
    return jnp.where(index < 0, -1, index - offset)


def to_columns(table):
    return table.astype(F32).T.astype(jnp.int32)


def fine_backs(table, offset, leaves):
    index = own_index(table, offset)
    return jnp.concatenate(
        [pick(index[2 + q : 3 + q, :], (leaves, table.shape[1]), 0) for q in range(4)], axis=1
    )


def choose(refs, kinds, columns, neighbours, leaves):
    slots = columns.shape[0]
    for faces_ref, fine_ref, start in kinds:
        places = to_columns(own_index(neighbours, start))
        for f in range(FACES):
            refs[faces_ref][leaves * f : leaves * (f + 1), :] = pick(
                places[:, f : f + 1], (leaves, leaves), 1
            )
        fine = own_index(columns, start)
        for q in range(4):
            refs[fine_ref][slots * q : slots * (q + 1), :] = pick(
                fine[:, 2 + q : 3 + q], (slots, leaves), 1
            )


def read_tables(pack_ref, leaves):
    table = pack_ref[leaves : leaves + 8, :]
    columns = table.T
    scale = jnp.concatenate([columns[:, 6:7], columns[:, 7:8]], axis=0)
    return table.astype(jnp.int32) - 1, columns.astype(jnp.int32) - 1, scale


def pad_rows(neighbours):
    return jnp.concatenate(
        [neighbours, jnp.full((2, neighbours.shape[1]), -1, jnp.int32)], axis=0
    )


def choose_kernel(place_ref, pack_ref, neighbours_ref, *refs):
    made = dict(zip(CHOSEN, refs))
    leaves = pack_ref.shape[0] - 8
    offset, first = place_ref[0:1, 0:1], place_ref[0:1, 1:2]
    mortars, columns, _ = read_tables(pack_ref, leaves)
    slots = mortars.shape[1]
    made["face"][...] = columns[:, 1:2]
    made["fine_back"][...] = fine_backs(mortars, offset, leaves)
    made["own_back"][...] = pick(mortars[0:1, :] - offset, (leaves, slots), 0)
    made["own_pick"][...] = pick(columns[:, 0:1] - offset, (slots, leaves), 1)
    kinds = (("own", "own_fine", offset), ("one", "one_fine", offset + first))
    choose(made, kinds, columns, pad_rows(neighbours_ref[...]), leaves)


def image_of(vector, lapped, kept):
    swapped = pltpu.roll(vector, NODES, 1)
    return kept["mass"][...] * vector + kept["curve"][...] * swapped + placed(lapped)


def first_kernel(
    place_ref, pack_ref, other_ref, table, mass_ref, curve_ref, stiffness_ref, levels_ref, *refs
):
    kept = dict(zip(CHOSEN + MADE, refs))
    image_ref, far_ref = refs[len(CHOSEN) + len(MADE) :]
    leaves = pack_ref.shape[0] - 8
    offset, first = place_ref[0:1, 0:1], place_ref[0:1, 1:2]
    mortars, columns, _ = read_tables(other_ref, leaves)
    slots = mortars.shape[1]
    face, other_face = kept["face"][...], columns[:, 1:2]
    other_pick = pick(columns[:, 0:1] - (offset + first), (slots, leaves), 1)
    other_back = fine_backs(mortars, offset, leaves)
    kept["one_pick"][...] = other_pick
    kept["one_back"][...] = other_back
    kept["one_face"][...] = other_face
    back = kept["fine_back"][...]
    diagonal = (
        fine_count([back, other_back], [face, other_face])
        + sum(face_nodes(jnp.int32(f)) for f in range(FACES))
    )
    kept["diagonal"][...] = diagonal
    wide = jnp.concatenate([stiffness_ref[...]] * 2, axis=1)
    wide = jnp.concatenate([wide, wide], axis=0)
    same = (lax.broadcasted_iota(jnp.int32, wide.shape, 0) < NODES) == (
        lax.broadcasted_iota(jnp.int32, wide.shape, 1) < NODES
    )
    wide = split(jnp.where(same, wide, 0.0))
    wide = jnp.concatenate([wide, wide], axis=0)
    kept["stiff"][...] = wide
    kept["mass"][...] = jnp.concatenate([mass_ref[...]] * 2, axis=0).T
    curve = curve_ref[...]
    kept["curve"][...] = jnp.concatenate([-curve, jnp.zeros_like(curve)], axis=0).T
    scale = level_rows(levels_ref[...])
    kept["scale"][...] = scale
    rows = pack_ref[0:leaves, :]
    parts = [split(rows), split(other_ref[0:leaves, :])]
    lapped = diagonal * rows + fold(dot(parts[0], wide)) - from_blocks(
        parts,
        [kept["own"][...], kept["one"][...]],
        [kept["own_fine"][...], kept["one_fine"][...]],
        [kept["own_pick"][...], other_pick],
        [back, other_back],
        [face, other_face],
        face,
        kept["own_back"][...],
        table,
        True,
    )
    image = image_of(rows / scale, lapped, kept)
    image_ref[...] = image
    far_ref[0 : leaves + 8, :] = pack_ref[...]
    far_ref[leaves + 8 :, :] = image * scale


def over_there_kernel(
    place_ref, pack_ref, neighbours_ref, table, scale_ref, face_ref, own_pick_ref, two_ref,
    two_fine_ref, given_ref, extra_ref, zero_ref, length_ref
):
    leaves = pack_ref.shape[0] - 8
    offset = place_ref[0:1, 0:1]
    far = offset - place_ref[0:1, 1:2]
    mortars, columns, _ = read_tables(pack_ref, leaves)
    neighbours = pad_rows(neighbours_ref[...])
    choose((two_ref, two_fine_ref), ((0, 1, far),), columns, neighbours, leaves)
    face = face_ref[...]
    rows = pack_ref[0:leaves, :]
    parts = split(rows)
    index = own_index(neighbours, far)
    seen = jnp.concatenate(
        [dot(pick(index[f ^ 1 : (f ^ 1) + 1, :], (leaves, leaves), 0), parts) for f in range(FACES)],
        axis=0,
    )
    back = fine_backs(mortars, far, leaves)
    trace = side_traces(dot(own_pick_ref[...], parts), [face], table)
    sent = jnp.concatenate(lift(trace, [face], table), axis=0)
    given_ref[...] = -across_faces(seen) - fold(dot(back, sent))
    extra_ref[...] = fine_count([back], [face])
    length, zero = unit(rows / scale_ref[...])
    zero_ref[...] = zero
    length_ref[...] = length


def far_kernel(
    place_ref, pack_ref, far_ref, table, scale_ref, diagonal_ref, partial_ref, two_ref,
    two_fine_ref, own_back_ref, face_ref, image_ref, send_ref, pick_ref, back_ref, far_face_ref,
    total_ref
):
    leaves = pack_ref.shape[0] - 8
    offset = place_ref[0:1, 0:1]
    mortars, columns, _ = read_tables(far_ref, leaves)
    slots = mortars.shape[1]
    face = columns[:, 1:2]
    chosen = pick(columns[:, 0:1] - (offset - place_ref[0:1, 1:2]), (slots, leaves), 1)
    back = fine_backs(mortars, offset, leaves)
    pick_ref[...] = chosen
    back_ref[...] = back
    far_face_ref[...] = face
    extra = fine_count([back], [face])
    total_ref[...] = diagonal_ref[...] + extra
    lapped = extra * pack_ref[0:leaves, :] - from_blocks(
        [split(far_ref[0:leaves, :])], [two_ref[...]], [two_fine_ref[...]], [chosen], [back],
        [face], face_ref[...], own_back_ref[...], table, False,
    )
    image = partial_ref[...] + placed(lapped)
    image_ref[...] = image
    send_ref[...] = image * scale_ref[...]


def far_rows_kernel(
    place_ref, pack_ref, far_ref, table, given_ref, extra_ref, image_ref, rows_ref, turned_ref
):
    leaves = pack_ref.shape[0] - 8
    offset = place_ref[0:1, 0:1]
    mortars, columns, scale = read_tables(far_ref, leaves)
    slots = mortars.shape[1]
    face = columns[:, 1:2]
    fine = own_index(columns, offset)
    fine = jnp.concatenate(
        [pick(fine[:, 2 + q : 3 + q], (slots, leaves), 1) for q in range(4)], axis=0
    )
    trace = side_traces(
        dot(fine, split(pack_ref[0:leaves, :])), [opposite(face)] * 4, table
    )
    quarters = [trace[slots * q : slots * (q + 1), :] for q in range(4)]
    back = pick(mortars[0:1, :] - (offset - place_ref[0:1, 1:2]), (leaves, slots), 0)
    lapped = (
        given_ref[...]
        + extra_ref[...] * far_ref[0:leaves, :]
        - fold(dot(back, lower(quarters, face, table, STAY_AT)))
    )
    rows_ref[...] = far_ref[leaves + 8 :, :] + scale * placed(lapped)
    turned_ref[...] = image_ref[...].T


def total(values):
    return jnp.sum(values, keepdims=True)


def unit(values):
    length = jnp.sqrt(total(values * values))
    return length, values * jnp.where(length > 0.0, 1.0 / jnp.where(length > 0.0, length, 1.0), 0.0)


def in_lanes(shape, values):
    lane = lax.broadcasted_iota(jnp.int32, shape, 1)
    row = jnp.zeros(shape, F32)
    for at, value in enumerate(values):
        row = jnp.where(lane == at, value, row)
    return row


def second_kernel(
    table, send_ref, one_ref, two_ref, image_ref, total_ref, zero_ref, length_ref, faces_two_ref,
    two_fine_ref, two_pick_ref, two_back_ref, two_face_ref, *refs
):
    kept = dict(zip(CHOSEN + MADE[1:], refs))
    stats_ref = refs[len(CHOSEN) + len(MADE) - 1]
    image, zero = image_ref[...], zero_ref[...]
    r01 = total(zero * image)
    rest = image - r01 * zero
    again = total(zero * rest)
    r11, one = unit(rest - again * zero)
    rows = send_ref[...]
    parts = [split(rows), split(one_ref[...]), split(two_ref[...])]
    face = kept["face"][...]
    lapped = total_ref[...] * rows + fold(dot(parts[0], kept["stiff"][...])) - from_blocks(
        parts,
        [kept["own"][...], kept["one"][...], faces_two_ref[...]],
        [kept["own_fine"][...], kept["one_fine"][...], two_fine_ref[...]],
        [kept["own_pick"][...], kept["one_pick"][...], two_pick_ref[...]],
        [kept["fine_back"][...], kept["one_back"][...], two_back_ref[...]],
        [face, kept["one_face"][...], two_face_ref[...]],
        face,
        kept["own_back"][...],
        table,
        True,
    )
    image = image_of(image, lapped, kept)
    r02 = total(zero * image)
    r12 = total(one * image)
    rest = image - r02 * zero - r12 * one
    r22 = jnp.sqrt(total(rest * rest))
    values = (length_ref[...], r01 + again, r11, r02, r12, r22)
    stats_ref[...] = in_lanes(stats_ref.shape, values)


def final_kernel(stats_ref, cot_ref, image_ref, out_ref):
    table = stats_ref[...].T
    a0, a1, b1, a2, b2, c2 = [table[at : at + 1, :] for at in range(6)]
    r00_sq = total(a0 * a0)
    r00 = jnp.sqrt(r00_sq)
    f01 = total(a0 * a1) / r00_sq
    f02 = total(a0 * a2) / r00_sq
    a1 = a1 - f01 * a0
    a2 = a2 - f02 * a0
    r11_sq = total(a1 * a1) + total(b1 * b1)
    r11 = jnp.sqrt(r11_sq)
    f12 = (total(a1 * a2) + total(b1 * b2)) / r11_sq
    a2 = a2 - f12 * a1
    b2 = b2 - f12 * b1
    r22 = jnp.sqrt(total(a2 * a2) + total(b2 * b2) + total(c2 * c2))
    rhs_norm = r00
    first_diag = f01
    first_below = r11 / r00
    upper_right = (f02 - first_diag * f01) / first_below
    second_diag = f12 - first_diag
    second_below = r22 / r11
    first_len = jnp.sqrt(first_diag * first_diag + first_below * first_below)
    cos_one = first_diag / first_len
    sin_one = first_below / first_len
    rotated_top = cos_one * upper_right + sin_one * second_diag
    rotated_low = cos_one * second_diag - sin_one * upper_right
    second_len = jnp.sqrt(rotated_low * rotated_low + second_below * second_below)
    cos_two = rotated_low / second_len
    y_two = cos_two * (-sin_one * rhs_norm) / second_len
    y_one = (cos_one * rhs_norm - rotated_top * y_two) / first_len
    on_one = y_two / r11
    on_base = y_one / r00 - on_one * f01
    out_ref[...] = on_base * cot_ref[...] + on_one * image_ref[...]


def on_device(cotangent, nodal_mass, curvature, stiffness, levels, neighbours, mortars):
    fields, nodes, leaves = cotangent.shape
    slots = mortars.shape[1]
    count = lax.axis_size("leaf")
    flat = cotangent.reshape(fields * nodes, leaves)
    levels = levels.reshape(1, leaves)
    me = lax.axis_index("leaf").astype(jnp.int32)
    place = jnp.stack([me * leaves, leaves - 2 * leaves * (me & 1)]).reshape(1, 2)
    table = jnp.asarray(matrices())
    vmem = pl.BlockSpec(memory_space=pltpu.VMEM)
    hbm = pl.BlockSpec(memory_space=pltpu.HBM)

    def call(kernel, outs, specs, operands, scratch=(), flops=0, moved=0, mib=40):
        return pl.pallas_call(
            kernel,
            out_shape=outs,
            in_specs=specs,
            out_specs=jax.tree.map(lambda _: vmem, outs),
            scratch_shapes=scratch,
            compiler_params=pltpu.CompilerParams(vmem_limit_bytes=mib * 1024 * 1024),
            cost_estimate=pl.CostEstimate(flops=flops, bytes_accessed=moved, transcendentals=0),
        )(*operands)

    def shape(*dims, dtype=F32):
        return jax.ShapeDtypeStruct(dims, dtype)

    pairs_one = [(i, i ^ 1) for i in range(count) if i ^ 1 < count]
    pairs_two = [(i, i + 1) for i in range(1, count - 1, 2)]
    pairs_two = pairs_two + [(j, i) for i, j in pairs_two]

    wide = 2 * LANES
    rows = shape(leaves, LANES)
    faces = shape(FACES * leaves, leaves, dtype=BF16)
    fine = shape(4 * slots, leaves, dtype=BF16)
    picks = shape(slots, leaves, dtype=BF16)
    backs = shape(leaves, 4 * slots, dtype=BF16)
    face = shape(slots, 1, dtype=jnp.int32)
    shapes = dict(
        own=faces,
        one=faces,
        own_fine=fine,
        one_fine=fine,
        own_pick=picks,
        own_back=shape(leaves, slots, dtype=BF16),
        fine_back=backs,
        face=face,
        diagonal=rows,
        stiff=shape(wide, wide, dtype=BF16),
        mass=rows,
        curve=rows,
        scale=rows,
        one_pick=picks,
        one_back=backs,
        one_face=face,
    )

    def stay_out(*arrays):
        return tuple(pltpu.with_memory_space_constraint(array, pltpu.HBM) for array in arrays)

    pack = call(
        prep_kernel,
        shape(leaves + 8, LANES),
        [hbm] * 3,
        stay_out(flat, levels, mortars),
        scratch=[
            pltpu.VMEM(flat.shape, F32),
            pltpu.VMEM(levels.shape, jnp.int32),
            pltpu.VMEM(mortars.shape, jnp.int32),
            pltpu.SemaphoreType.DMA((3,)),
        ],
        flops=10_000_000_000,
        moved=4_000_000,
    )
    one = lax.ppermute(pack, "leaf", pairs_one)
    chosen = call(
        choose_kernel,
        [shapes[name] for name in CHOSEN],
        [vmem] * 3,
        (place, pack, neighbours),
        flops=1_000_000_000,
        moved=2_000_000,
    )
    *made, partial, far = call(
        first_kernel,
        [shapes[name] for name in MADE] + [rows, shape(2 * leaves + 8, LANES)],
        [vmem] * (8 + len(CHOSEN)),
        [place, pack, one, table, nodal_mass, curvature, stiffness, levels, *chosen],
    )
    kept = dict(zip(CHOSEN + MADE, [*chosen, *made]))
    far = lax.ppermute(far, "leaf", pairs_two)
    faces_two, two_fine, given, extra, zero, length = call(
        over_there_kernel,
        [faces, fine, rows, rows, rows, shape(1, 1)],
        [vmem] * 7,
        [place, pack, neighbours, table, kept["scale"], kept["face"], kept["own_pick"]],
        flops=2_000_000_000,
        moved=4_000_000,
    )
    image, send, two_pick, two_back, two_face, diagonal = call(
        far_kernel,
        [rows, rows, picks, backs, face, rows],
        [vmem] * 11,
        [place, pack, far, table, kept["scale"], kept["diagonal"], partial, faces_two, two_fine,
         kept["own_back"], kept["face"]],
    )
    one = lax.ppermute(send, "leaf", pairs_one)
    two, turned = call(
        far_rows_kernel,
        [rows, shape(LANES, leaves)],
        [vmem] * 7,
        [place, pack, far, table, given, extra, image],
        flops=1_000_000_000,
        moved=2_000_000,
    )
    stats = call(
        second_kernel,
        shape(1, LANES),
        [vmem] * (13 + len(CHOSEN) + len(MADE) - 1),
        [table, send, one, two, image, diagonal, zero, length, faces_two, two_fine, two_pick,
         two_back, two_face] + [kept[name] for name in CHOSEN + MADE[1:]],
    )
    gathered = lax.all_to_all(
        jnp.broadcast_to(stats, (count, LANES)), "leaf", 0, 0, tiled=True
    )
    out = call(final_kernel, shape(*flat.shape), [vmem] * 3, (gathered, flat, turned))
    return out.reshape(cotangent.shape)


def solution(mesh):
    placed = (
        P(None, None, "leaf"),
        P(None, "leaf"),
        P(None, "leaf"),
        P(),
        P("leaf"),
        P(None, "leaf"),
        P(None, "leaf"),
    )
    return jax.shard_map(
        on_device, mesh=mesh, in_specs=placed, out_specs=P(None, None, "leaf"), check_vma=False
    )
```

```python
import jax
import jax.numpy as jnp
import ml_dtypes
import numpy as np
from jax import lax
from jax.experimental import pallas as pl
from jax.experimental.pallas import tpu as pltpu
from jax.sharding import PartitionSpec as P

TAU_WEIGHT = 0.15
EPS_WEIGHT = 0.1
FACES = 6
NODES = 64
LANES = 128
F32 = jnp.float32
BF16 = jnp.bfloat16


def face_tables():
    node_at = np.zeros((6, 16), dtype=np.int64)
    for face_id in range(6):
        for row_pos in range(4):
            for col_pos in range(4):
                coords = [row_pos, col_pos]
                coords.insert(face_id // 2, 3 * (face_id % 2))
                node_at[face_id, 4 * row_pos + col_pos] = (
                    16 * coords[0] + 4 * coords[1] + coords[2]
                )
    points = np.array([-1.0, -1.0 / np.sqrt(5.0), 1.0 / np.sqrt(5.0), 1.0])
    halves = np.zeros((2, 4, 4))
    for half_id in range(2):
        target = (points + 2.0 * half_id - 1.0) / 2.0
        for column in range(4):
            lagrange = np.ones(4)
            for other_id in range(4):
                if other_id != column:
                    lagrange = (
                        lagrange * (target - points[other_id]) / (points[column] - points[other_id])
                    )
            halves[half_id, :, column] = lagrange
    mortar = np.stack([np.kron(halves[quarter // 2], halves[quarter % 2]) for quarter in range(4)])
    return node_at, mortar


def two_parts(table):
    high = table.astype(np.float32).astype(ml_dtypes.bfloat16)
    low = (table - high.astype(np.float64)).astype(np.float32).astype(ml_dtypes.bfloat16)
    return np.concatenate([high, low], axis=-1)


def matrices():
    node_at, mortar = face_tables()
    traces = np.zeros((2 * LANES, 2 * LANES))
    to_fine = np.zeros((4, 2 * LANES, LANES))
    to_coarse = np.zeros((4, 2 * LANES, LANES))
    stay = np.zeros((2 * LANES, LANES))
    square = sum(mortar[quarter].T @ mortar[quarter] for quarter in range(4))
    for face in range(FACES):
        for field in range(2):
            nodes = 64 * field + node_at[face]
            for part in range(2):
                for place in range(16):
                    at = part * LANES + 32 * (face // 2) + 16 * field + place
                    traces[part * LANES + nodes[place], at] = 1.0
                    stay[at, nodes] = -square[:, place]
                    for quarter in range(4):
                        to_fine[quarter, at, nodes] = mortar[quarter][:, place]
                        to_coarse[quarter, at, nodes] = mortar[quarter][place, :]
    return np.concatenate(
        [traces.astype(ml_dtypes.bfloat16)]
        + list(two_parts(to_fine))
        + list(two_parts(to_coarse))
        + [two_parts(stay)],
        axis=0,
    )


TRACES_AT, FINE_AT, COARSE_AT, STAY_AT, TABLE_ROWS = 0, 256, 1280, 2304, 2560


def split(values, axis=1):
    high = values.astype(BF16)
    return jnp.concatenate([high, (values - high.astype(F32)).astype(BF16)], axis=axis)


def dot(left, right):
    return jnp.dot(left, right, preferred_element_type=F32)


def fold(values):
    return values[:, :LANES] + values[:, LANES:]


def pick(index, shape, dim):
    places = lax.broadcasted_iota(jnp.int32, shape, dim).astype(F32).astype(BF16)
    index = jnp.broadcast_to(index.astype(F32), shape).astype(BF16)
    return jnp.where(index == places, jnp.ones(shape, BF16), jnp.zeros(shape, BF16))


def on_axis(face):
    lane = lax.broadcasted_iota(jnp.int32, (1, 2 * LANES), 1)
    axis = jnp.right_shift(face, 1)
    return jnp.where((jnp.right_shift(lane, 5) & 3) == axis, 1.0, 0.0).astype(BF16)


def face_nodes(face):
    lane = lax.broadcasted_iota(jnp.int32, (1, LANES), 1)
    axis = jnp.right_shift(face, 1)
    place = jnp.right_shift(lane, 4 - 2 * axis) & 3
    return jnp.where((place == 3 * (face & 1)) & (face >= 0), 1.0, 0.0)


def opposite(face):
    return jnp.where(face >= 0, face ^ 1, -1)


def level_rows(levels):
    scale = jnp.left_shift(jnp.ones_like(levels), levels).astype(F32)
    return jnp.broadcast_to(scale, (LANES, levels.shape[1])).T


def fetch(pairs, sems):
    copies = [
        pltpu.make_async_copy(source, target, sems.at[at])
        for at, (source, target) in enumerate(pairs)
    ]
    for copy in copies:
        copy.start()
    return copies


def prep_kernel(cot_hbm, levels_hbm, mortars_hbm, pack_ref, cot_ref, levels_ref, mortars_ref, sems):
    for copy in fetch(
        ((cot_hbm, cot_ref), (levels_hbm, levels_ref), (mortars_hbm, mortars_ref)), sems
    ):
        copy.wait()
    leaves = cot_ref.shape[1]
    scale = jnp.left_shift(jnp.ones_like(levels_ref[...]), levels_ref[...]).astype(F32)
    pack_ref[0:leaves, :] = (cot_ref[...] * scale).T
    table = mortars_ref[...].astype(F32) + 1.0
    halves = [scale[:, k * table.shape[1] : (k + 1) * table.shape[1]] for k in range(2)]
    pack_ref[leaves : leaves + 8, :] = jnp.concatenate([table] + halves, axis=0)


CHOSEN = (
    "own", "one", "own_fine", "one_fine", "own_pick", "own_back", "fine_back", "face",
)
MADE = ("diagonal", "stiff", "mass", "curve", "scale", "one_pick", "one_back", "one_face")


def across_faces(seen):
    leaves = seen.shape[0] // FACES
    result = jnp.zeros((leaves, LANES), F32)
    for f in range(FACES):
        shift = 3 * 4 ** (2 - f // 2)
        part = fold(seen[leaves * f : leaves * (f + 1), :])
        part = pltpu.roll(part, shift if f % 2 else LANES - shift, 1)
        result = result + face_nodes(jnp.int32(f)) * part
    return result


def side_traces(chosen, faces, table):
    nodes = jnp.concatenate([face_nodes(face).astype(BF16) for face in faces], axis=0)
    axes = jnp.concatenate([on_axis(face) for face in faces], axis=0)
    nodes = jnp.concatenate([nodes, nodes], axis=1)
    trace = dot(chosen.astype(BF16) * nodes, table[TRACES_AT : TRACES_AT + 256, :])
    return trace.astype(BF16) * axes


def lift(trace, faces, table):
    mask = jnp.concatenate([face_nodes(opposite(face)) for face in faces], axis=0)
    return [
        split(mask * fold(dot(trace, table[FINE_AT + 256 * q : FINE_AT + 256 * (q + 1), :])))
        for q in range(4)
    ]


def lower(traces, face, table, last):
    back = dot(jnp.concatenate(traces, axis=1), table[COARSE_AT:last, :])
    return split(face_nodes(face) * fold(back))


def from_blocks(parts, faces, fine, picks, backs, coarse_faces, face, own_back, table, own):
    slots = own_back.shape[1]
    rows = jnp.concatenate(parts, axis=0)
    seen = dot(jnp.concatenate(faces, axis=1), rows)
    chosen = [dot(jnp.concatenate(fine, axis=1), rows)]
    chosen += [dot(pick_rows, part) for pick_rows, part in zip(picks, parts)]
    trace = side_traces(
        jnp.concatenate(chosen, axis=0), [opposite(face)] * 4 + coarse_faces, table
    )
    quarters = [trace[slots * q : slots * (q + 1), :] for q in range(4)]
    sent = lift(trace[4 * slots :, :], coarse_faces, table)
    ordered = [
        sent[q][slots * k : slots * (k + 1), :] for k in range(len(parts)) for q in range(4)
    ]
    if own:
        quarters.append(trace[4 * slots : 5 * slots, :])
    ordered.append(lower(quarters, face, table, TABLE_ROWS if own else STAY_AT))
    mortars = dot(jnp.concatenate(backs + [own_back], axis=1), jnp.concatenate(ordered, axis=0))
    return fold(mortars) + across_faces(seen)


def placed(lapped):
    first = lax.broadcasted_iota(jnp.int32, lapped.shape, 1) < NODES
    return jnp.where(first, -EPS_WEIGHT, TAU_WEIGHT) * pltpu.roll(lapped, NODES, 1)


def fine_count(backs, faces):
    weights = [face_nodes(opposite(face)).astype(BF16) for face in faces for _ in range(4)]
    return dot(jnp.concatenate(backs, axis=1), jnp.concatenate(weights, axis=0))


def own_index(index, offset):
    return jnp.where(index < 0, -1, index - offset)


def to_columns(table):
    return table.astype(F32).T.astype(jnp.int32)


def fine_backs(table, offset, leaves):
    index = own_index(table, offset)
    return jnp.concatenate(
        [pick(index[2 + q : 3 + q, :], (leaves, table.shape[1]), 0) for q in range(4)], axis=1
    )


def choose(refs, kinds, columns, neighbours, leaves):
    slots = columns.shape[0]
    for faces_ref, fine_ref, start in kinds:
        places = to_columns(own_index(neighbours, start))
        for f in range(FACES):
            refs[faces_ref][leaves * f : leaves * (f + 1), :] = pick(
                places[:, f : f + 1], (leaves, leaves), 1
            )
        fine = own_index(columns, start)
        for q in range(4):
            refs[fine_ref][slots * q : slots * (q + 1), :] = pick(
                fine[:, 2 + q : 3 + q], (slots, leaves), 1
            )


def read_tables(pack_ref, leaves):
    table = pack_ref[leaves : leaves + 8, :]
    columns = table.T
    scale = jnp.concatenate([columns[:, 6:7], columns[:, 7:8]], axis=0)
    return table.astype(jnp.int32) - 1, columns.astype(jnp.int32) - 1, scale


def pad_rows(neighbours):
    return jnp.concatenate(
        [neighbours, jnp.full((2, neighbours.shape[1]), -1, jnp.int32)], axis=0
    )


def choose_kernel(place_ref, pack_ref, neighbours_ref, *refs):
    made = dict(zip(CHOSEN, refs))
    leaves = pack_ref.shape[0] - 8
    offset, first = place_ref[0:1, 0:1], place_ref[0:1, 1:2]
    mortars, columns, _ = read_tables(pack_ref, leaves)
    slots = mortars.shape[1]
    made["face"][...] = columns[:, 1:2]
    made["fine_back"][...] = fine_backs(mortars, offset, leaves)
    made["own_back"][...] = pick(mortars[0:1, :] - offset, (leaves, slots), 0)
    made["own_pick"][...] = pick(columns[:, 0:1] - offset, (slots, leaves), 1)
    kinds = (("own", "own_fine", offset), ("one", "one_fine", offset + first))
    choose(made, kinds, columns, pad_rows(neighbours_ref[...]), leaves)


def image_of(vector, lapped, kept):
    swapped = pltpu.roll(vector, NODES, 1)
    return kept["mass"][...] * vector + kept["curve"][...] * swapped + placed(lapped)


def first_kernel(
    place_ref, pack_ref, other_ref, table, mass_ref, curve_ref, stiffness_ref, levels_ref, *refs
):
    kept = dict(zip(CHOSEN + MADE, refs))
    image_ref, far_ref = refs[len(CHOSEN) + len(MADE) :]
    leaves = pack_ref.shape[0] - 8
    offset, first = place_ref[0:1, 0:1], place_ref[0:1, 1:2]
    mortars, columns, _ = read_tables(other_ref, leaves)
    slots = mortars.shape[1]
    face, other_face = kept["face"][...], columns[:, 1:2]
    other_pick = pick(columns[:, 0:1] - (offset + first), (slots, leaves), 1)
    other_back = fine_backs(mortars, offset, leaves)
    kept["one_pick"][...] = other_pick
    kept["one_back"][...] = other_back
    kept["one_face"][...] = other_face
    back = kept["fine_back"][...]
    diagonal = (
        fine_count([back, other_back], [face, other_face])
        + sum(face_nodes(jnp.int32(f)) for f in range(FACES))
    )
    kept["diagonal"][...] = diagonal
    wide = jnp.concatenate([stiffness_ref[...]] * 2, axis=1)
    wide = jnp.concatenate([wide, wide], axis=0)
    same = (lax.broadcasted_iota(jnp.int32, wide.shape, 0) < NODES) == (
        lax.broadcasted_iota(jnp.int32, wide.shape, 1) < NODES
    )
    wide = split(jnp.where(same, wide, 0.0))
    wide = jnp.concatenate([wide, wide], axis=0)
    kept["stiff"][...] = wide
    kept["mass"][...] = jnp.concatenate([mass_ref[...]] * 2, axis=0).T
    curve = curve_ref[...]
    kept["curve"][...] = jnp.concatenate([-curve, jnp.zeros_like(curve)], axis=0).T
    scale = level_rows(levels_ref[...])
    kept["scale"][...] = scale
    rows = pack_ref[0:leaves, :]
    parts = [split(rows), split(other_ref[0:leaves, :])]
    lapped = diagonal * rows + fold(dot(parts[0], wide)) - from_blocks(
        parts,
        [kept["own"][...], kept["one"][...]],
        [kept["own_fine"][...], kept["one_fine"][...]],
        [kept["own_pick"][...], other_pick],
        [back, other_back],
        [face, other_face],
        face,
        kept["own_back"][...],
        table,
        True,
    )
    image = image_of(rows / scale, lapped, kept)
    image_ref[...] = image
    far_ref[...] = image * scale


def over_there_kernel(
    place_ref, pack_ref, neighbours_ref, table, scale_ref, face_ref, own_pick_ref, two_ref,
    two_fine_ref, given_ref, extra_ref, zero_ref, length_ref
):
    leaves = pack_ref.shape[0] - 8
    offset = place_ref[0:1, 0:1]
    far = offset - place_ref[0:1, 1:2]
    mortars, columns, _ = read_tables(pack_ref, leaves)
    neighbours = pad_rows(neighbours_ref[...])
    choose((two_ref, two_fine_ref), ((0, 1, far),), columns, neighbours, leaves)
    face = face_ref[...]
    rows = pack_ref[0:leaves, :]
    parts = split(rows)
    index = own_index(neighbours, far)
    seen = jnp.concatenate(
        [dot(pick(index[f ^ 1 : (f ^ 1) + 1, :], (leaves, leaves), 0), parts) for f in range(FACES)],
        axis=0,
    )
    back = fine_backs(mortars, far, leaves)
    trace = side_traces(dot(own_pick_ref[...], parts), [face], table)
    sent = jnp.concatenate(lift(trace, [face], table), axis=0)
    given_ref[...] = -across_faces(seen) - fold(dot(back, sent))
    extra_ref[...] = fine_count([back], [face])
    length, zero = unit(rows / scale_ref[...])
    zero_ref[...] = zero
    length_ref[...] = length


def far_kernel(
    place_ref, pack_ref, far_ref, table, scale_ref, diagonal_ref, partial_ref, two_ref,
    two_fine_ref, own_back_ref, face_ref, image_ref, send_ref, pick_ref, back_ref, far_face_ref,
    total_ref
):
    leaves = pack_ref.shape[0] - 8
    offset = place_ref[0:1, 0:1]
    mortars, columns, _ = read_tables(far_ref, leaves)
    slots = mortars.shape[1]
    face = columns[:, 1:2]
    chosen = pick(columns[:, 0:1] - (offset - place_ref[0:1, 1:2]), (slots, leaves), 1)
    back = fine_backs(mortars, offset, leaves)
    pick_ref[...] = chosen
    back_ref[...] = back
    far_face_ref[...] = face
    extra = fine_count([back], [face])
    total_ref[...] = diagonal_ref[...] + extra
    lapped = extra * pack_ref[0:leaves, :] - from_blocks(
        [split(far_ref[0:leaves, :])], [two_ref[...]], [two_fine_ref[...]], [chosen], [back],
        [face], face_ref[...], own_back_ref[...], table, False,
    )
    image = partial_ref[...] + placed(lapped)
    image_ref[...] = image
    send_ref[...] = image * scale_ref[...]


def far_rows_kernel(
    place_ref, pack_ref, far_ref, table, given_ref, extra_ref, image_ref, rows_ref, turned_ref
):
    leaves = pack_ref.shape[0] - 8
    offset = place_ref[0:1, 0:1]
    mortars, columns, scale = read_tables(far_ref, leaves)
    slots = mortars.shape[1]
    face = columns[:, 1:2]
    fine = own_index(columns, offset)
    fine = jnp.concatenate(
        [pick(fine[:, 2 + q : 3 + q], (slots, leaves), 1) for q in range(4)], axis=0
    )
    trace = side_traces(
        dot(fine, split(pack_ref[0:leaves, :])), [opposite(face)] * 4, table
    )
    quarters = [trace[slots * q : slots * (q + 1), :] for q in range(4)]
    back = pick(mortars[0:1, :] - (offset - place_ref[0:1, 1:2]), (leaves, slots), 0)
    lapped = (
        given_ref[...]
        + extra_ref[...] * far_ref[0:leaves, :]
        - fold(dot(back, lower(quarters, face, table, STAY_AT)))
    )
    rows_ref[...] = scale * placed(lapped)
    turned_ref[...] = image_ref[...].T


def total(values):
    return jnp.sum(values, keepdims=True)


def unit(values):
    length = jnp.sqrt(total(values * values))
    return length, values * jnp.where(length > 0.0, 1.0 / jnp.where(length > 0.0, length, 1.0), 0.0)


def in_lanes(shape, values):
    lane = lax.broadcasted_iota(jnp.int32, shape, 1)
    row = jnp.zeros(shape, F32)
    for at, value in enumerate(values):
        row = jnp.where(lane == at, value, row)
    return row


def second_kernel(
    table, send_ref, one_ref, two_ref, lacked_ref, image_ref, total_ref, zero_ref, length_ref, faces_two_ref,
    two_fine_ref, two_pick_ref, two_back_ref, two_face_ref, *refs
):
    kept = dict(zip(CHOSEN + MADE[1:], refs))
    stats_ref = refs[len(CHOSEN) + len(MADE) - 1]
    image, zero = image_ref[...], zero_ref[...]
    r01 = total(zero * image)
    rest = image - r01 * zero
    again = total(zero * rest)
    r11, one = unit(rest - again * zero)
    rows = send_ref[...]
    parts = [split(rows), split(one_ref[...]), split(two_ref[...] + lacked_ref[...])]
    face = kept["face"][...]
    lapped = total_ref[...] * rows + fold(dot(parts[0], kept["stiff"][...])) - from_blocks(
        parts,
        [kept["own"][...], kept["one"][...], faces_two_ref[...]],
        [kept["own_fine"][...], kept["one_fine"][...], two_fine_ref[...]],
        [kept["own_pick"][...], kept["one_pick"][...], two_pick_ref[...]],
        [kept["fine_back"][...], kept["one_back"][...], two_back_ref[...]],
        [face, kept["one_face"][...], two_face_ref[...]],
        face,
        kept["own_back"][...],
        table,
        True,
    )
    image = image_of(image, lapped, kept)
    r02 = total(zero * image)
    r12 = total(one * image)
    rest = image - r02 * zero - r12 * one
    r22 = jnp.sqrt(total(rest * rest))
    values = (length_ref[...], r01 + again, r11, r02, r12, r22)
    stats_ref[...] = in_lanes(stats_ref.shape, values)


def final_kernel(stats_ref, cot_ref, image_ref, out_ref):
    table = stats_ref[...].T
    a0, a1, b1, a2, b2, c2 = [table[at : at + 1, :] for at in range(6)]
    r00_sq = total(a0 * a0)
    r00 = jnp.sqrt(r00_sq)
    f01 = total(a0 * a1) / r00_sq
    f02 = total(a0 * a2) / r00_sq
    a1 = a1 - f01 * a0
    a2 = a2 - f02 * a0
    r11_sq = total(a1 * a1) + total(b1 * b1)
    r11 = jnp.sqrt(r11_sq)
    f12 = (total(a1 * a2) + total(b1 * b2)) / r11_sq
    a2 = a2 - f12 * a1
    b2 = b2 - f12 * b1
    r22 = jnp.sqrt(total(a2 * a2) + total(b2 * b2) + total(c2 * c2))
    rhs_norm = r00
    first_diag = f01
    first_below = r11 / r00
    upper_right = (f02 - first_diag * f01) / first_below
    second_diag = f12 - first_diag
    second_below = r22 / r11
    first_len = jnp.sqrt(first_diag * first_diag + first_below * first_below)
    cos_one = first_diag / first_len
    sin_one = first_below / first_len
    rotated_top = cos_one * upper_right + sin_one * second_diag
    rotated_low = cos_one * second_diag - sin_one * upper_right
    second_len = jnp.sqrt(rotated_low * rotated_low + second_below * second_below)
    cos_two = rotated_low / second_len
    y_two = cos_two * (-sin_one * rhs_norm) / second_len
    y_one = (cos_one * rhs_norm - rotated_top * y_two) / first_len
    on_one = y_two / r11
    on_base = y_one / r00 - on_one * f01
    out_ref[...] = on_base * cot_ref[...] + on_one * image_ref[...]


def on_device(cotangent, nodal_mass, curvature, stiffness, levels, neighbours, mortars):
    fields, nodes, leaves = cotangent.shape
    slots = mortars.shape[1]
    count = lax.axis_size("leaf")
    flat = cotangent.reshape(fields * nodes, leaves)
    levels = levels.reshape(1, leaves)
    me = lax.axis_index("leaf").astype(jnp.int32)
    place = jnp.stack([me * leaves, leaves - 2 * leaves * (me & 1)]).reshape(1, 2)
    table = jnp.asarray(matrices())
    vmem = pl.BlockSpec(memory_space=pltpu.VMEM)
    hbm = pl.BlockSpec(memory_space=pltpu.HBM)

    def call(kernel, outs, specs, operands, scratch=(), flops=0, moved=0, mib=40):
        return pl.pallas_call(
            kernel,
            out_shape=outs,
            in_specs=specs,
            out_specs=jax.tree.map(lambda _: vmem, outs),
            scratch_shapes=scratch,
            compiler_params=pltpu.CompilerParams(vmem_limit_bytes=mib * 1024 * 1024),
            cost_estimate=pl.CostEstimate(flops=flops, bytes_accessed=moved, transcendentals=0),
        )(*operands)

    def shape(*dims, dtype=F32):
        return jax.ShapeDtypeStruct(dims, dtype)

    pairs_one = [(i, i ^ 1) for i in range(count) if i ^ 1 < count]
    pairs_two = [(i, i + 1) for i in range(1, count - 1, 2)]
    pairs_two = pairs_two + [(j, i) for i, j in pairs_two]

    wide = 2 * LANES
    rows = shape(leaves, LANES)
    faces = shape(FACES * leaves, leaves, dtype=BF16)
    fine = shape(4 * slots, leaves, dtype=BF16)
    picks = shape(slots, leaves, dtype=BF16)
    backs = shape(leaves, 4 * slots, dtype=BF16)
    face = shape(slots, 1, dtype=jnp.int32)
    shapes = dict(
        own=faces,
        one=faces,
        own_fine=fine,
        one_fine=fine,
        own_pick=picks,
        own_back=shape(leaves, slots, dtype=BF16),
        fine_back=backs,
        face=face,
        diagonal=rows,
        stiff=shape(wide, wide, dtype=BF16),
        mass=rows,
        curve=rows,
        scale=rows,
        one_pick=picks,
        one_back=backs,
        one_face=face,
    )

    def stay_out(*arrays):
        return tuple(pltpu.with_memory_space_constraint(array, pltpu.HBM) for array in arrays)

    pack = call(
        prep_kernel,
        shape(leaves + 8, LANES),
        [hbm] * 3,
        stay_out(flat, levels, mortars),
        scratch=[
            pltpu.VMEM(flat.shape, F32),
            pltpu.VMEM(levels.shape, jnp.int32),
            pltpu.VMEM(mortars.shape, jnp.int32),
            pltpu.SemaphoreType.DMA((3,)),
        ],
        flops=10_000_000_000,
        moved=4_000_000,
    )
    far = lax.ppermute(pack, "leaf", pairs_two)
    one = lax.ppermute(pack, "leaf", pairs_one)
    chosen = call(
        choose_kernel,
        [shapes[name] for name in CHOSEN],
        [vmem] * 3,
        (place, pack, neighbours),
        flops=1_000_000_000,
        moved=2_000_000,
    )
    *made, partial, scaled = call(
        first_kernel,
        [shapes[name] for name in MADE] + [rows, rows],
        [vmem] * (8 + len(CHOSEN)),
        [place, pack, one, table, nodal_mass, curvature, stiffness, levels, *chosen],
    )
    kept = dict(zip(CHOSEN + MADE, [*chosen, *made]))
    two = lax.ppermute(scaled, "leaf", pairs_two)
    faces_two, two_fine, given, extra, zero, length = call(
        over_there_kernel,
        [faces, fine, rows, rows, rows, shape(1, 1)],
        [vmem] * 7,
        [place, pack, neighbours, table, kept["scale"], kept["face"], kept["own_pick"]],
        flops=2_000_000_000,
        moved=4_000_000,
    )
    image, send, two_pick, two_back, two_face, diagonal = call(
        far_kernel,
        [rows, rows, picks, backs, face, rows],
        [vmem] * 11,
        [place, pack, far, table, kept["scale"], kept["diagonal"], partial, faces_two, two_fine,
         kept["own_back"], kept["face"]],
    )
    one = lax.ppermute(send, "leaf", pairs_one)
    lacked, turned = call(
        far_rows_kernel,
        [rows, shape(LANES, leaves)],
        [vmem] * 7,
        [place, pack, far, table, given, extra, image],
        flops=1_000_000_000,
        moved=2_000_000,
    )
    stats = call(
        second_kernel,
        shape(1, LANES),
        [vmem] * (14 + len(CHOSEN) + len(MADE) - 1),
        [table, send, one, two, lacked, image, diagonal, zero, length, faces_two, two_fine, two_pick,
         two_back, two_face] + [kept[name] for name in CHOSEN + MADE[1:]],
    )
    gathered = lax.all_to_all(
        jnp.broadcast_to(stats, (count, LANES)), "leaf", 0, 0, tiled=True
    )
    out = call(final_kernel, shape(*flat.shape), [vmem] * 3, (gathered, flat, turned))
    return out.reshape(cotangent.shape)


def solution(mesh):
    placed = (
        P(None, None, "leaf"),
        P(None, "leaf"),
        P(None, "leaf"),
        P(),
        P("leaf"),
        P(None, "leaf"),
        P(None, "leaf"),
    )
    return jax.shard_map(
        on_device, mesh=mesh, in_specs=placed, out_specs=P(None, None, "leaf"), check_vma=False
    )
```

```python
import jax
import jax.numpy as jnp
import ml_dtypes
import numpy as np
from jax import lax
from jax.experimental import pallas as pl
from jax.experimental.pallas import tpu as pltpu
from jax.sharding import PartitionSpec as P

TAU_WEIGHT = 0.15
EPS_WEIGHT = 0.1
FACES = 6
NODES = 64
LANES = 128
F32 = jnp.float32
BF16 = jnp.bfloat16


def face_tables():
    node_at = np.zeros((6, 16), dtype=np.int64)
    for face_id in range(6):
        for row_pos in range(4):
            for col_pos in range(4):
                coords = [row_pos, col_pos]
                coords.insert(face_id // 2, 3 * (face_id % 2))
                node_at[face_id, 4 * row_pos + col_pos] = (
                    16 * coords[0] + 4 * coords[1] + coords[2]
                )
    points = np.array([-1.0, -1.0 / np.sqrt(5.0), 1.0 / np.sqrt(5.0), 1.0])
    halves = np.zeros((2, 4, 4))
    for half_id in range(2):
        target = (points + 2.0 * half_id - 1.0) / 2.0
        for column in range(4):
            lagrange = np.ones(4)
            for other_id in range(4):
                if other_id != column:
                    lagrange = (
                        lagrange * (target - points[other_id]) / (points[column] - points[other_id])
                    )
            halves[half_id, :, column] = lagrange
    mortar = np.stack([np.kron(halves[quarter // 2], halves[quarter % 2]) for quarter in range(4)])
    return node_at, mortar


def two_parts(table):
    high = table.astype(np.float32).astype(ml_dtypes.bfloat16)
    low = (table - high.astype(np.float64)).astype(np.float32).astype(ml_dtypes.bfloat16)
    return np.concatenate([high, low], axis=-1)


def matrices():
    node_at, mortar = face_tables()
    traces = np.zeros((2 * LANES, 2 * LANES))
    to_fine = np.zeros((4, 2 * LANES, LANES))
    to_coarse = np.zeros((4, 2 * LANES, LANES))
    stay = np.zeros((2 * LANES, LANES))
    square = sum(mortar[quarter].T @ mortar[quarter] for quarter in range(4))
    for face in range(FACES):
        for field in range(2):
            nodes = 64 * field + node_at[face]
            for part in range(2):
                for place in range(16):
                    at = part * LANES + 32 * (face // 2) + 16 * field + place
                    traces[part * LANES + nodes[place], at] = 1.0
                    stay[at, nodes] = -square[:, place]
                    for quarter in range(4):
                        to_fine[quarter, at, nodes] = mortar[quarter][:, place]
                        to_coarse[quarter, at, nodes] = mortar[quarter][place, :]
    return np.concatenate(
        [traces.astype(ml_dtypes.bfloat16)]
        + list(two_parts(to_fine))
        + list(two_parts(to_coarse))
        + [two_parts(stay)],
        axis=0,
    )


TRACES_AT, FINE_AT, COARSE_AT, STAY_AT, TABLE_ROWS = 0, 256, 1280, 2304, 2560


def split(values, axis=1):
    high = values.astype(BF16)
    return jnp.concatenate([high, (values - high.astype(F32)).astype(BF16)], axis=axis)


def dot(left, right):
    return jnp.dot(left, right, preferred_element_type=F32)


def fold(values):
    return values[:, :LANES] + values[:, LANES:]


def pick(index, shape, dim):
    places = lax.broadcasted_iota(jnp.int32, shape, dim).astype(F32).astype(BF16)
    index = jnp.broadcast_to(index.astype(F32), shape).astype(BF16)
    return jnp.where(index == places, jnp.ones(shape, BF16), jnp.zeros(shape, BF16))


def on_axis(face):
    lane = lax.broadcasted_iota(jnp.int32, (1, 2 * LANES), 1)
    axis = jnp.right_shift(face, 1)
    return jnp.where((jnp.right_shift(lane, 5) & 3) == axis, 1.0, 0.0).astype(BF16)


def face_nodes(face):
    lane = lax.broadcasted_iota(jnp.int32, (1, LANES), 1)
    axis = jnp.right_shift(face, 1)
    place = jnp.right_shift(lane, 4 - 2 * axis) & 3
    return jnp.where((place == 3 * (face & 1)) & (face >= 0), 1.0, 0.0)


def opposite(face):
    return jnp.where(face >= 0, face ^ 1, -1)


def level_rows(levels):
    scale = jnp.left_shift(jnp.ones_like(levels), levels).astype(F32)
    return jnp.broadcast_to(scale, (LANES, levels.shape[1])).T


def fetch(pairs, sems):
    copies = [
        pltpu.make_async_copy(source, target, sems.at[at])
        for at, (source, target) in enumerate(pairs)
    ]
    for copy in copies:
        copy.start()
    return copies


def prep_kernel(cot_hbm, levels_hbm, mortars_hbm, pack_ref, cot_ref, levels_ref, mortars_ref, sems):
    for copy in fetch(
        ((cot_hbm, cot_ref), (levels_hbm, levels_ref), (mortars_hbm, mortars_ref)), sems
    ):
        copy.wait()
    leaves = cot_ref.shape[1]
    scale = jnp.left_shift(jnp.ones_like(levels_ref[...]), levels_ref[...]).astype(F32)
    pack_ref[0:leaves, :] = (cot_ref[...] * scale).T
    table = mortars_ref[...].astype(F32) + 1.0
    halves = [scale[:, k * table.shape[1] : (k + 1) * table.shape[1]] for k in range(2)]
    pack_ref[leaves : leaves + 8, :] = jnp.concatenate([table] + halves, axis=0)


CHOSEN = (
    "own", "one", "own_fine", "one_fine", "own_pick", "own_back", "fine_back", "face",
)
MADE = ("diagonal", "stiff", "mass", "curve", "scale", "one_pick", "one_back", "one_face")


def across_faces(seen):
    leaves = seen.shape[0] // FACES
    result = jnp.zeros((leaves, LANES), F32)
    for f in range(FACES):
        shift = 3 * 4 ** (2 - f // 2)
        part = fold(seen[leaves * f : leaves * (f + 1), :])
        part = pltpu.roll(part, shift if f % 2 else LANES - shift, 1)
        result = result + face_nodes(jnp.int32(f)) * part
    return result


def side_traces(chosen, faces, table):
    nodes = jnp.concatenate([face_nodes(face).astype(BF16) for face in faces], axis=0)
    axes = jnp.concatenate([on_axis(face) for face in faces], axis=0)
    nodes = jnp.concatenate([nodes, nodes], axis=1)
    trace = dot(chosen.astype(BF16) * nodes, table[TRACES_AT : TRACES_AT + 256, :])
    return trace.astype(BF16) * axes


def lift(trace, faces, table):
    mask = jnp.concatenate([face_nodes(opposite(face)) for face in faces], axis=0)
    return [
        split(mask * fold(dot(trace, table[FINE_AT + 256 * q : FINE_AT + 256 * (q + 1), :])))
        for q in range(4)
    ]


def lower(traces, face, table, last):
    back = dot(jnp.concatenate(traces, axis=1), table[COARSE_AT:last, :])
    return split(face_nodes(face) * fold(back))


def from_blocks(parts, faces, fine, picks, backs, coarse_faces, face, own_back, table, own):
    slots = own_back.shape[1]
    rows = jnp.concatenate(parts, axis=0)
    seen = dot(jnp.concatenate(faces, axis=1), rows)
    chosen = [dot(jnp.concatenate(fine, axis=1), rows)]
    chosen += [dot(pick_rows, part) for pick_rows, part in zip(picks, parts)]
    trace = side_traces(
        jnp.concatenate(chosen, axis=0), [opposite(face)] * 4 + coarse_faces, table
    )
    quarters = [trace[slots * q : slots * (q + 1), :] for q in range(4)]
    sent = lift(trace[4 * slots :, :], coarse_faces, table)
    ordered = [
        sent[q][slots * k : slots * (k + 1), :] for k in range(len(parts)) for q in range(4)
    ]
    if own:
        quarters.append(trace[4 * slots : 5 * slots, :])
    ordered.append(lower(quarters, face, table, TABLE_ROWS if own else STAY_AT))
    mortars = dot(jnp.concatenate(backs + [own_back], axis=1), jnp.concatenate(ordered, axis=0))
    return fold(mortars) + across_faces(seen)


def placed(lapped):
    first = lax.broadcasted_iota(jnp.int32, lapped.shape, 1) < NODES
    return jnp.where(first, -EPS_WEIGHT, TAU_WEIGHT) * pltpu.roll(lapped, NODES, 1)


def fine_count(backs, faces):
    weights = [face_nodes(opposite(face)).astype(BF16) for face in faces for _ in range(4)]
    return dot(jnp.concatenate(backs, axis=1), jnp.concatenate(weights, axis=0))


def own_index(index, offset):
    return jnp.where(index < 0, -1, index - offset)


def to_columns(table):
    return table.astype(F32).T.astype(jnp.int32)


def fine_backs(table, offset, leaves):
    index = own_index(table, offset)
    return jnp.concatenate(
        [pick(index[2 + q : 3 + q, :], (leaves, table.shape[1]), 0) for q in range(4)], axis=1
    )


def choose(refs, kinds, columns, neighbours, leaves):
    slots = columns.shape[0]
    for faces_ref, fine_ref, start in kinds:
        places = to_columns(own_index(neighbours, start))
        for f in range(FACES):
            refs[faces_ref][leaves * f : leaves * (f + 1), :] = pick(
                places[:, f : f + 1], (leaves, leaves), 1
            )
        fine = own_index(columns, start)
        for q in range(4):
            refs[fine_ref][slots * q : slots * (q + 1), :] = pick(
                fine[:, 2 + q : 3 + q], (slots, leaves), 1
            )


def read_tables(pack_ref, leaves):
    table = pack_ref[leaves : leaves + 8, :]
    columns = table.T
    scale = jnp.concatenate([columns[:, 6:7], columns[:, 7:8]], axis=0)
    return table.astype(jnp.int32) - 1, columns.astype(jnp.int32) - 1, scale


def pad_rows(neighbours):
    return jnp.concatenate(
        [neighbours, jnp.full((2, neighbours.shape[1]), -1, jnp.int32)], axis=0
    )


def choose_kernel(place_ref, pack_ref, neighbours_ref, *refs):
    made = dict(zip(CHOSEN, refs))
    leaves = pack_ref.shape[0] - 8
    offset, first = place_ref[0:1, 0:1], place_ref[0:1, 1:2]
    mortars, columns, _ = read_tables(pack_ref, leaves)
    slots = mortars.shape[1]
    made["face"][...] = columns[:, 1:2]
    made["fine_back"][...] = fine_backs(mortars, offset, leaves)
    made["own_back"][...] = pick(mortars[0:1, :] - offset, (leaves, slots), 0)
    made["own_pick"][...] = pick(columns[:, 0:1] - offset, (slots, leaves), 1)
    kinds = (("own", "own_fine", offset), ("one", "one_fine", offset + first))
    choose(made, kinds, columns, pad_rows(neighbours_ref[...]), leaves)


def image_of(vector, lapped, kept):
    swapped = pltpu.roll(vector, NODES, 1)
    return kept["mass"][...] * vector + kept["curve"][...] * swapped + placed(lapped)


def first_kernel(
    place_ref, pack_ref, other_ref, table, mass_ref, curve_ref, stiffness_ref, levels_ref, *refs
):
    kept = dict(zip(CHOSEN + MADE, refs))
    image_ref, far_ref = refs[len(CHOSEN) + len(MADE) :]
    leaves = pack_ref.shape[0] - 8
    offset, first = place_ref[0:1, 0:1], place_ref[0:1, 1:2]
    mortars, columns, _ = read_tables(other_ref, leaves)
    slots = mortars.shape[1]
    face, other_face = kept["face"][...], columns[:, 1:2]
    other_pick = pick(columns[:, 0:1] - (offset + first), (slots, leaves), 1)
    other_back = fine_backs(mortars, offset, leaves)
    kept["one_pick"][...] = other_pick
    kept["one_back"][...] = other_back
    kept["one_face"][...] = other_face
    back = kept["fine_back"][...]
    diagonal = (
        fine_count([back, other_back], [face, other_face])
        + sum(face_nodes(jnp.int32(f)) for f in range(FACES))
    )
    kept["diagonal"][...] = diagonal
    wide = jnp.concatenate([stiffness_ref[...]] * 2, axis=1)
    wide = jnp.concatenate([wide, wide], axis=0)
    same = (lax.broadcasted_iota(jnp.int32, wide.shape, 0) < NODES) == (
        lax.broadcasted_iota(jnp.int32, wide.shape, 1) < NODES
    )
    wide = split(jnp.where(same, wide, 0.0))
    wide = jnp.concatenate([wide, wide], axis=0)
    kept["stiff"][...] = wide
    kept["mass"][...] = jnp.concatenate([mass_ref[...]] * 2, axis=0).T
    curve = curve_ref[...]
    kept["curve"][...] = jnp.concatenate([-curve, jnp.zeros_like(curve)], axis=0).T
    scale = level_rows(levels_ref[...])
    kept["scale"][...] = scale
    rows = pack_ref[0:leaves, :]
    parts = [split(rows), split(other_ref[0:leaves, :])]
    lapped = diagonal * rows + fold(dot(parts[0], wide)) - from_blocks(
        parts,
        [kept["own"][...], kept["one"][...]],
        [kept["own_fine"][...], kept["one_fine"][...]],
        [kept["own_pick"][...], other_pick],
        [back, other_back],
        [face, other_face],
        face,
        kept["own_back"][...],
        table,
        True,
    )
    image = image_of(rows / scale, lapped, kept)
    image_ref[...] = image
    far_ref[...] = image * scale


def over_there_kernel(
    place_ref, pack_ref, neighbours_ref, table, scale_ref, face_ref, own_pick_ref, two_ref,
    two_fine_ref, given_ref, extra_ref, zero_ref, length_ref
):
    leaves = pack_ref.shape[0] - 8
    offset = place_ref[0:1, 0:1]
    far = offset - place_ref[0:1, 1:2]
    mortars, columns, _ = read_tables(pack_ref, leaves)
    neighbours = pad_rows(neighbours_ref[...])
    choose((two_ref, two_fine_ref), ((0, 1, far),), columns, neighbours, leaves)
    face = face_ref[...]
    rows = pack_ref[0:leaves, :]
    parts = split(rows)
    index = own_index(neighbours, far)
    seen = jnp.concatenate(
        [dot(pick(index[f ^ 1 : (f ^ 1) + 1, :], (leaves, leaves), 0), parts) for f in range(FACES)],
        axis=0,
    )
    back = fine_backs(mortars, far, leaves)
    trace = side_traces(dot(own_pick_ref[...], parts), [face], table)
    sent = jnp.concatenate(lift(trace, [face], table), axis=0)
    given_ref[...] = -across_faces(seen) - fold(dot(back, sent))
    extra_ref[...] = fine_count([back], [face])
    length, zero = unit(rows / scale_ref[...])
    zero_ref[...] = zero
    length_ref[...] = jnp.broadcast_to(length, length_ref.shape)


def far_kernel(
    place_ref, pack_ref, far_ref, table, scale_ref, diagonal_ref, partial_ref, two_ref,
    two_fine_ref, own_back_ref, face_ref, image_ref, send_ref, pick_ref, back_ref, far_face_ref,
    total_ref
):
    leaves = pack_ref.shape[0] - 8
    offset = place_ref[0:1, 0:1]
    mortars, columns, _ = read_tables(far_ref, leaves)
    slots = mortars.shape[1]
    face = columns[:, 1:2]
    chosen = pick(columns[:, 0:1] - (offset - place_ref[0:1, 1:2]), (slots, leaves), 1)
    back = fine_backs(mortars, offset, leaves)
    pick_ref[...] = chosen
    back_ref[...] = back
    far_face_ref[...] = face
    extra = fine_count([back], [face])
    total_ref[...] = diagonal_ref[...] + extra
    lapped = extra * pack_ref[0:leaves, :] - from_blocks(
        [split(far_ref[0:leaves, :])], [two_ref[...]], [two_fine_ref[...]], [chosen], [back],
        [face], face_ref[...], own_back_ref[...], table, False,
    )
    image = partial_ref[...] + placed(lapped)
    image_ref[...] = image
    send_ref[...] = image * scale_ref[...]


def far_rows_kernel(
    place_ref, pack_ref, far_ref, table, given_ref, extra_ref, image_ref, rows_ref, turned_ref
):
    leaves = pack_ref.shape[0] - 8
    offset = place_ref[0:1, 0:1]
    mortars, columns, scale = read_tables(far_ref, leaves)
    slots = mortars.shape[1]
    face = columns[:, 1:2]
    fine = own_index(columns, offset)
    fine = jnp.concatenate(
        [pick(fine[:, 2 + q : 3 + q], (slots, leaves), 1) for q in range(4)], axis=0
    )
    trace = side_traces(
        dot(fine, split(pack_ref[0:leaves, :])), [opposite(face)] * 4, table
    )
    quarters = [trace[slots * q : slots * (q + 1), :] for q in range(4)]
    back = pick(mortars[0:1, :] - (offset - place_ref[0:1, 1:2]), (leaves, slots), 0)
    lapped = (
        given_ref[...]
        + extra_ref[...] * far_ref[0:leaves, :]
        - fold(dot(back, lower(quarters, face, table, STAY_AT)))
    )
    rows_ref[...] = scale * placed(lapped)
    turned_ref[...] = image_ref[...].T


def total(values):
    return jnp.sum(values, keepdims=True)


def unit(values):
    length = jnp.sqrt(total(values * values))
    return length, values * jnp.where(length > 0.0, 1.0 / jnp.where(length > 0.0, length, 1.0), 0.0)


def in_lanes(shape, values):
    lane = lax.broadcasted_iota(jnp.int32, shape, 1)
    row = jnp.zeros(shape, F32)
    for at, value in enumerate(values):
        row = jnp.where(lane == at, value, row)
    return row


def second_kernel(
    table, send_ref, one_ref, two_ref, lacked_ref, image_ref, total_ref, zero_ref, length_ref, faces_two_ref,
    two_fine_ref, two_pick_ref, two_back_ref, two_face_ref, *refs
):
    kept = dict(zip(CHOSEN + MADE[1:], refs))
    stats_ref = refs[len(CHOSEN) + len(MADE) - 1]
    image, zero = image_ref[...], zero_ref[...]
    r01 = total(zero * image)
    rest = image - r01 * zero
    again = total(zero * rest)
    r11, one = unit(rest - again * zero)
    rows = send_ref[...]
    parts = [split(rows), split(one_ref[...]), split(two_ref[...] + lacked_ref[...])]
    face = kept["face"][...]
    lapped = total_ref[...] * rows + fold(dot(parts[0], kept["stiff"][...])) - from_blocks(
        parts,
        [kept["own"][...], kept["one"][...], faces_two_ref[...]],
        [kept["own_fine"][...], kept["one_fine"][...], two_fine_ref[...]],
        [kept["own_pick"][...], kept["one_pick"][...], two_pick_ref[...]],
        [kept["fine_back"][...], kept["one_back"][...], two_back_ref[...]],
        [face, kept["one_face"][...], two_face_ref[...]],
        face,
        kept["own_back"][...],
        table,
        True,
    )
    image = image_of(image, lapped, kept)
    r02 = total(zero * image)
    r12 = total(one * image)
    rest = image - r02 * zero - r12 * one
    r22 = jnp.sqrt(total(rest * rest))
    values = (length_ref[0:1, 0:1], r01 + again, r11, r02, r12, r22)
    stats_ref[...] = in_lanes(stats_ref.shape, values)


def final_kernel(stats_ref, cot_ref, image_ref, out_ref):
    table = stats_ref[...].T
    a0, a1, b1, a2, b2, c2 = [table[at : at + 1, :] for at in range(6)]
    r00_sq = total(a0 * a0)
    r00 = jnp.sqrt(r00_sq)
    f01 = total(a0 * a1) / r00_sq
    f02 = total(a0 * a2) / r00_sq
    a1 = a1 - f01 * a0
    a2 = a2 - f02 * a0
    r11_sq = total(a1 * a1) + total(b1 * b1)
    r11 = jnp.sqrt(r11_sq)
    f12 = (total(a1 * a2) + total(b1 * b2)) / r11_sq
    a2 = a2 - f12 * a1
    b2 = b2 - f12 * b1
    r22 = jnp.sqrt(total(a2 * a2) + total(b2 * b2) + total(c2 * c2))
    rhs_norm = r00
    first_diag = f01
    first_below = r11 / r00
    upper_right = (f02 - first_diag * f01) / first_below
    second_diag = f12 - first_diag
    second_below = r22 / r11
    first_len = jnp.sqrt(first_diag * first_diag + first_below * first_below)
    cos_one = first_diag / first_len
    sin_one = first_below / first_len
    rotated_top = cos_one * upper_right + sin_one * second_diag
    rotated_low = cos_one * second_diag - sin_one * upper_right
    second_len = jnp.sqrt(rotated_low * rotated_low + second_below * second_below)
    cos_two = rotated_low / second_len
    y_two = cos_two * (-sin_one * rhs_norm) / second_len
    y_one = (cos_one * rhs_norm - rotated_top * y_two) / first_len
    on_one = y_two / r11
    on_base = y_one / r00 - on_one * f01
    out_ref[...] = on_base * cot_ref[...] + on_one * image_ref[...]


def on_device(cotangent, nodal_mass, curvature, stiffness, levels, neighbours, mortars):
    fields, nodes, leaves = cotangent.shape
    slots = mortars.shape[1]
    count = lax.axis_size("leaf")
    flat = cotangent.reshape(fields * nodes, leaves)
    levels = levels.reshape(1, leaves)
    me = lax.axis_index("leaf").astype(jnp.int32)
    place = jnp.stack([me * leaves, leaves - 2 * leaves * (me & 1)]).reshape(1, 2)
    table = jnp.asarray(matrices())
    vmem = pl.BlockSpec(memory_space=pltpu.VMEM)
    hbm = pl.BlockSpec(memory_space=pltpu.HBM)

    def call(kernel, outs, specs, operands, scratch=(), flops=0, moved=0, mib=40):
        return pl.pallas_call(
            kernel,
            out_shape=outs,
            in_specs=specs,
            out_specs=jax.tree.map(lambda _: vmem, outs),
            scratch_shapes=scratch,
            compiler_params=pltpu.CompilerParams(vmem_limit_bytes=mib * 1024 * 1024),
            cost_estimate=pl.CostEstimate(flops=flops, bytes_accessed=moved, transcendentals=0),
        )(*operands)

    def shape(*dims, dtype=F32):
        return jax.ShapeDtypeStruct(dims, dtype)

    pairs_one = [(i, i ^ 1) for i in range(count) if i ^ 1 < count]
    pairs_two = [(i, i + 1) for i in range(1, count - 1, 2)]
    pairs_two = pairs_two + [(j, i) for i, j in pairs_two]

    wide = 2 * LANES
    rows = shape(leaves, LANES)
    faces = shape(FACES * leaves, leaves, dtype=BF16)
    fine = shape(4 * slots, leaves, dtype=BF16)
    picks = shape(slots, leaves, dtype=BF16)
    backs = shape(leaves, 4 * slots, dtype=BF16)
    face = shape(slots, 1, dtype=jnp.int32)
    shapes = dict(
        own=faces,
        one=faces,
        own_fine=fine,
        one_fine=fine,
        own_pick=picks,
        own_back=shape(leaves, slots, dtype=BF16),
        fine_back=backs,
        face=face,
        diagonal=rows,
        stiff=shape(wide, wide, dtype=BF16),
        mass=rows,
        curve=rows,
        scale=rows,
        one_pick=picks,
        one_back=backs,
        one_face=face,
    )

    def stay_out(*arrays):
        return tuple(pltpu.with_memory_space_constraint(array, pltpu.HBM) for array in arrays)

    pack = call(
        prep_kernel,
        shape(leaves + 8, LANES),
        [hbm] * 3,
        stay_out(flat, levels, mortars),
        scratch=[
            pltpu.VMEM(flat.shape, F32),
            pltpu.VMEM(levels.shape, jnp.int32),
            pltpu.VMEM(mortars.shape, jnp.int32),
            pltpu.SemaphoreType.DMA((3,)),
        ],
        flops=10_000_000_000,
        moved=4_000_000,
    )
    far = lax.ppermute(pack, "leaf", pairs_two)
    one = lax.ppermute(pack, "leaf", pairs_one)
    chosen = call(
        choose_kernel,
        [shapes[name] for name in CHOSEN],
        [vmem] * 3,
        (place, pack, neighbours),
    )
    *made, partial, scaled = call(
        first_kernel,
        [shapes[name] for name in MADE] + [rows, rows],
        [vmem] * (8 + len(CHOSEN)),
        [place, pack, one, table, nodal_mass, curvature, stiffness, levels, *chosen],
    )
    kept = dict(zip(CHOSEN + MADE, [*chosen, *made]))
    two = lax.ppermute(scaled, "leaf", pairs_two)
    faces_two, two_fine, given, extra, zero, length = call(
        over_there_kernel,
        [faces, fine, rows, rows, rows, shape(1, LANES)],
        [vmem] * 7,
        [place, pack, neighbours, table, kept["scale"], kept["face"], kept["own_pick"]],
        flops=2_000_000_000,
        moved=4_000_000,
    )
    image, send, two_pick, two_back, two_face, diagonal = call(
        far_kernel,
        [rows, rows, picks, backs, face, rows],
        [vmem] * 11,
        [place, pack, far, table, kept["scale"], kept["diagonal"], partial, faces_two, two_fine,
         kept["own_back"], kept["face"]],
    )
    one = lax.ppermute(send, "leaf", pairs_one)
    lacked, turned = call(
        far_rows_kernel,
        [rows, shape(LANES, leaves)],
        [vmem] * 7,
        [place, pack, far, table, given, extra, image],
        flops=1_000_000_000,
        moved=2_000_000,
    )
    stats = call(
        second_kernel,
        shape(1, LANES),
        [vmem] * (14 + len(CHOSEN) + len(MADE) - 1),
        [table, send, one, two, lacked, image, diagonal, zero, length, faces_two, two_fine, two_pick,
         two_back, two_face] + [kept[name] for name in CHOSEN + MADE[1:]],
    )
    gathered = lax.all_to_all(
        jnp.broadcast_to(stats, (count, LANES)), "leaf", 0, 0, tiled=True
    )
    out = call(final_kernel, shape(*flat.shape), [vmem] * 3, (gathered, flat, turned))
    return out.reshape(cotangent.shape)


def solution(mesh):
    placed = (
        P(None, None, "leaf"),
        P(None, "leaf"),
        P(None, "leaf"),
        P(),
        P("leaf"),
        P(None, "leaf"),
        P(None, "leaf"),
    )
    return jax.shard_map(
        on_device, mesh=mesh, in_specs=placed, out_specs=P(None, None, "leaf"), check_vma=False
    )
```

```python
import jax
import jax.numpy as jnp
import ml_dtypes
import numpy as np
from jax import lax
from jax.experimental import pallas as pl
from jax.experimental.pallas import tpu as pltpu
from jax.sharding import PartitionSpec as P

TAU_WEIGHT = 0.15
EPS_WEIGHT = 0.1
FACES = 6
NODES = 64
LANES = 128
F32 = jnp.float32
BF16 = jnp.bfloat16


def face_tables():
    node_at = np.zeros((6, 16), dtype=np.int64)
    for face_id in range(6):
        for row_pos in range(4):
            for col_pos in range(4):
                coords = [row_pos, col_pos]
                coords.insert(face_id // 2, 3 * (face_id % 2))
                node_at[face_id, 4 * row_pos + col_pos] = (
                    16 * coords[0] + 4 * coords[1] + coords[2]
                )
    points = np.array([-1.0, -1.0 / np.sqrt(5.0), 1.0 / np.sqrt(5.0), 1.0])
    halves = np.zeros((2, 4, 4))
    for half_id in range(2):
        target = (points + 2.0 * half_id - 1.0) / 2.0
        for column in range(4):
            lagrange = np.ones(4)
            for other_id in range(4):
                if other_id != column:
                    lagrange = (
                        lagrange * (target - points[other_id]) / (points[column] - points[other_id])
                    )
            halves[half_id, :, column] = lagrange
    mortar = np.stack([np.kron(halves[quarter // 2], halves[quarter % 2]) for quarter in range(4)])
    return node_at, mortar


def two_parts(table):
    high = table.astype(np.float32).astype(ml_dtypes.bfloat16)
    low = (table - high.astype(np.float64)).astype(np.float32).astype(ml_dtypes.bfloat16)
    return np.concatenate([high, low], axis=-1)


def matrices():
    node_at, mortar = face_tables()
    traces = np.zeros((2 * LANES, 2 * LANES))
    to_fine = np.zeros((4, 2 * LANES, LANES))
    to_coarse = np.zeros((4, 2 * LANES, LANES))
    stay = np.zeros((2 * LANES, LANES))
    square = sum(mortar[quarter].T @ mortar[quarter] for quarter in range(4))
    for face in range(FACES):
        for field in range(2):
            nodes = 64 * field + node_at[face]
            for part in range(2):
                for place in range(16):
                    at = part * LANES + 32 * (face // 2) + 16 * field + place
                    traces[part * LANES + nodes[place], at] = 1.0
                    stay[at, nodes] = -square[:, place]
                    for quarter in range(4):
                        to_fine[quarter, at, nodes] = mortar[quarter][:, place]
                        to_coarse[quarter, at, nodes] = mortar[quarter][place, :]
    return np.concatenate(
        [traces.astype(ml_dtypes.bfloat16)]
        + list(two_parts(to_fine))
        + list(two_parts(to_coarse))
        + [two_parts(stay)],
        axis=0,
    )


TRACES_AT, FINE_AT, COARSE_AT, STAY_AT, TABLE_ROWS = 0, 256, 1280, 2304, 2560


def split(values, axis=1):
    high = values.astype(BF16)
    return jnp.concatenate([high, (values - high.astype(F32)).astype(BF16)], axis=axis)


def dot(left, right):
    return jnp.dot(left, right, preferred_element_type=F32)


def fold(values):
    return values[:, :LANES] + values[:, LANES:]


def pick(index, shape, dim):
    places = lax.broadcasted_iota(jnp.int32, shape, dim).astype(F32).astype(BF16)
    index = jnp.broadcast_to(index.astype(F32), shape).astype(BF16)
    return jnp.where(index == places, jnp.ones(shape, BF16), jnp.zeros(shape, BF16))


def on_axis(face):
    lane = lax.broadcasted_iota(jnp.int32, (1, 2 * LANES), 1)
    axis = jnp.right_shift(face, 1)
    return jnp.where((jnp.right_shift(lane, 5) & 3) == axis, 1.0, 0.0).astype(BF16)


def face_nodes(face):
    lane = lax.broadcasted_iota(jnp.int32, (1, LANES), 1)
    axis = jnp.right_shift(face, 1)
    place = jnp.right_shift(lane, 4 - 2 * axis) & 3
    return jnp.where((place == 3 * (face & 1)) & (face >= 0), 1.0, 0.0)


def opposite(face):
    return jnp.where(face >= 0, face ^ 1, -1)


def level_rows(levels):
    scale = jnp.left_shift(jnp.ones_like(levels), levels).astype(F32)
    return jnp.broadcast_to(scale, (LANES, levels.shape[1])).T


def fetch(pairs, sems):
    copies = [
        pltpu.make_async_copy(source, target, sems.at[at])
        for at, (source, target) in enumerate(pairs)
    ]
    for copy in copies:
        copy.start()
    return copies


def prep_kernel(cot_hbm, levels_hbm, mortars_hbm, pack_ref, cot_ref, levels_ref, mortars_ref, sems):
    for copy in fetch(
        ((cot_hbm, cot_ref), (levels_hbm, levels_ref), (mortars_hbm, mortars_ref)), sems
    ):
        copy.wait()
    leaves = cot_ref.shape[1]
    scale = jnp.left_shift(jnp.ones_like(levels_ref[...]), levels_ref[...]).astype(F32)
    pack_ref[0:leaves, :] = (cot_ref[...] * scale).T
    table = mortars_ref[...].astype(F32) + 1.0
    halves = [scale[:, k * table.shape[1] : (k + 1) * table.shape[1]] for k in range(2)]
    pack_ref[leaves : leaves + 8, :] = jnp.concatenate([table] + halves, axis=0)


CHOSEN = (
    "own", "one", "own_fine", "one_fine", "own_pick", "own_back", "fine_back", "face",
)
MADE = ("diagonal", "stiff", "mass", "curve", "scale", "one_pick", "one_back", "one_face")


def across_faces(seen):
    leaves = seen.shape[0] // FACES
    result = jnp.zeros((leaves, LANES), F32)
    for f in range(FACES):
        shift = 3 * 4 ** (2 - f // 2)
        part = fold(seen[leaves * f : leaves * (f + 1), :])
        part = pltpu.roll(part, shift if f % 2 else LANES - shift, 1)
        result = result + face_nodes(jnp.int32(f)) * part
    return result


def side_traces(chosen, faces, table):
    nodes = jnp.concatenate([face_nodes(face).astype(BF16) for face in faces], axis=0)
    axes = jnp.concatenate([on_axis(face) for face in faces], axis=0)
    nodes = jnp.concatenate([nodes, nodes], axis=1)
    trace = dot(chosen.astype(BF16) * nodes, table[TRACES_AT : TRACES_AT + 256, :])
    return trace.astype(BF16) * axes


def lift(trace, faces, table):
    mask = jnp.concatenate([face_nodes(opposite(face)) for face in faces], axis=0)
    return [
        split(mask * fold(dot(trace, table[FINE_AT + 256 * q : FINE_AT + 256 * (q + 1), :])))
        for q in range(4)
    ]


def lower(traces, face, table, last):
    back = dot(jnp.concatenate(traces, axis=1), table[COARSE_AT:last, :])
    return split(face_nodes(face) * fold(back))


def from_blocks(parts, faces, fine, picks, backs, coarse_faces, face, own_back, table, own):
    slots = own_back.shape[1]
    rows = jnp.concatenate(parts, axis=0)
    seen = dot(jnp.concatenate(faces, axis=1), rows)
    chosen = [dot(jnp.concatenate(fine, axis=1), rows)]
    chosen += [dot(pick_rows, part) for pick_rows, part in zip(picks, parts)]
    trace = side_traces(
        jnp.concatenate(chosen, axis=0), [opposite(face)] * 4 + coarse_faces, table
    )
    quarters = [trace[slots * q : slots * (q + 1), :] for q in range(4)]
    sent = lift(trace[4 * slots :, :], coarse_faces, table)
    ordered = [
        sent[q][slots * k : slots * (k + 1), :] for k in range(len(parts)) for q in range(4)
    ]
    if own:
        quarters.append(trace[4 * slots : 5 * slots, :])
    ordered.append(lower(quarters, face, table, TABLE_ROWS if own else STAY_AT))
    mortars = dot(jnp.concatenate(backs + [own_back], axis=1), jnp.concatenate(ordered, axis=0))
    return fold(mortars) + across_faces(seen)


def placed(lapped):
    first = lax.broadcasted_iota(jnp.int32, lapped.shape, 1) < NODES
    return jnp.where(first, -EPS_WEIGHT, TAU_WEIGHT) * pltpu.roll(lapped, NODES, 1)


def fine_count(backs, faces):
    weights = [face_nodes(opposite(face)).astype(BF16) for face in faces for _ in range(4)]
    return dot(jnp.concatenate(backs, axis=1), jnp.concatenate(weights, axis=0))


def own_index(index, offset):
    return jnp.where(index < 0, -1, index - offset)


def to_columns(table):
    return table.astype(F32).T.astype(jnp.int32)


def fine_backs(table, offset, leaves):
    index = own_index(table, offset)
    return jnp.concatenate(
        [pick(index[2 + q : 3 + q, :], (leaves, table.shape[1]), 0) for q in range(4)], axis=1
    )


def choose(refs, kinds, columns, neighbours, leaves):
    slots = columns.shape[0]
    for faces_ref, fine_ref, start in kinds:
        places = to_columns(own_index(neighbours, start))
        for f in range(FACES):
            refs[faces_ref][leaves * f : leaves * (f + 1), :] = pick(
                places[:, f : f + 1], (leaves, leaves), 1
            )
        fine = own_index(columns, start)
        for q in range(4):
            refs[fine_ref][slots * q : slots * (q + 1), :] = pick(
                fine[:, 2 + q : 3 + q], (slots, leaves), 1
            )


def read_tables(pack_ref, leaves):
    table = pack_ref[leaves : leaves + 8, :]
    columns = table.T
    scale = jnp.concatenate([columns[:, 6:7], columns[:, 7:8]], axis=0)
    return table.astype(jnp.int32) - 1, columns.astype(jnp.int32) - 1, scale


def pad_rows(neighbours):
    return jnp.concatenate(
        [neighbours, jnp.full((2, neighbours.shape[1]), -1, jnp.int32)], axis=0
    )


def choose_kernel(place_ref, pack_ref, neighbours_ref, *refs):
    made = dict(zip(CHOSEN, refs))
    leaves = pack_ref.shape[0] - 8
    offset, first = place_ref[0:1, 0:1], place_ref[0:1, 1:2]
    mortars, columns, _ = read_tables(pack_ref, leaves)
    slots = mortars.shape[1]
    made["face"][...] = columns[:, 1:2]
    made["fine_back"][...] = fine_backs(mortars, offset, leaves)
    made["own_back"][...] = pick(mortars[0:1, :] - offset, (leaves, slots), 0)
    made["own_pick"][...] = pick(columns[:, 0:1] - offset, (slots, leaves), 1)
    kinds = (("own", "own_fine", offset), ("one", "one_fine", offset + first))
    choose(made, kinds, columns, pad_rows(neighbours_ref[...]), leaves)


def image_of(vector, lapped, kept):
    swapped = pltpu.roll(vector, NODES, 1)
    return kept["mass"][...] * vector + kept["curve"][...] * swapped + placed(lapped)


def first_kernel(
    place_ref, pack_ref, other_ref, table, mass_ref, curve_ref, stiffness_ref, levels_ref, *refs
):
    kept = dict(zip(CHOSEN + MADE, refs))
    image_ref, far_ref = refs[len(CHOSEN) + len(MADE) :]
    leaves = pack_ref.shape[0] - 8
    offset, first = place_ref[0:1, 0:1], place_ref[0:1, 1:2]
    mortars, columns, _ = read_tables(other_ref, leaves)
    slots = mortars.shape[1]
    face, other_face = kept["face"][...], columns[:, 1:2]
    other_pick = pick(columns[:, 0:1] - (offset + first), (slots, leaves), 1)
    other_back = fine_backs(mortars, offset, leaves)
    kept["one_pick"][...] = other_pick
    kept["one_back"][...] = other_back
    kept["one_face"][...] = other_face
    back = kept["fine_back"][...]
    diagonal = (
        fine_count([back, other_back], [face, other_face])
        + sum(face_nodes(jnp.int32(f)) for f in range(FACES))
    )
    kept["diagonal"][...] = diagonal
    wide = jnp.concatenate([stiffness_ref[...]] * 2, axis=1)
    wide = jnp.concatenate([wide, wide], axis=0)
    same = (lax.broadcasted_iota(jnp.int32, wide.shape, 0) < NODES) == (
        lax.broadcasted_iota(jnp.int32, wide.shape, 1) < NODES
    )
    wide = split(jnp.where(same, wide, 0.0))
    wide = jnp.concatenate([wide, wide], axis=0)
    kept["stiff"][...] = wide
    kept["mass"][...] = jnp.concatenate([mass_ref[...]] * 2, axis=0).T
    curve = curve_ref[...]
    kept["curve"][...] = jnp.concatenate([-curve, jnp.zeros_like(curve)], axis=0).T
    scale = level_rows(levels_ref[...])
    kept["scale"][...] = scale
    rows = pack_ref[0:leaves, :]
    parts = [split(rows), split(other_ref[0:leaves, :])]
    lapped = diagonal * rows + fold(dot(parts[0], wide)) - from_blocks(
        parts,
        [kept["own"][...], kept["one"][...]],
        [kept["own_fine"][...], kept["one_fine"][...]],
        [kept["own_pick"][...], other_pick],
        [back, other_back],
        [face, other_face],
        face,
        kept["own_back"][...],
        table,
        True,
    )
    image = image_of(rows / scale, lapped, kept)
    image_ref[...] = image
    far_ref[...] = image * scale


def far_kernel(
    place_ref, pack_ref, neighbours_ref, far_ref, table, scale_ref, diagonal_ref, partial_ref,
    own_back_ref, face_ref, image_ref, send_ref, two_ref, two_fine_ref, pick_ref, back_ref,
    far_face_ref, total_ref
):
    leaves = pack_ref.shape[0] - 8
    offset = place_ref[0:1, 0:1]
    start = offset - place_ref[0:1, 1:2]
    _, columns, _ = read_tables(pack_ref, leaves)
    neighbours = pad_rows(neighbours_ref[...])
    choose((two_ref, two_fine_ref), ((0, 1, start),), columns, neighbours, leaves)
    mortars, columns, _ = read_tables(far_ref, leaves)
    slots = mortars.shape[1]
    face = columns[:, 1:2]
    chosen = pick(columns[:, 0:1] - start, (slots, leaves), 1)
    back = fine_backs(mortars, offset, leaves)
    pick_ref[...] = chosen
    back_ref[...] = back
    far_face_ref[...] = face
    extra = fine_count([back], [face])
    total_ref[...] = diagonal_ref[...] + extra
    lapped = extra * pack_ref[0:leaves, :] - from_blocks(
        [split(far_ref[0:leaves, :])], [two_ref[...]], [two_fine_ref[...]], [chosen], [back],
        [face], face_ref[...], own_back_ref[...], table, False,
    )
    image = partial_ref[...] + placed(lapped)
    image_ref[...] = image
    send_ref[...] = image * scale_ref[...]


def far_rows_kernel(
    place_ref, pack_ref, neighbours_ref, far_ref, table, scale_ref, face_ref, own_pick_ref,
    image_ref, rows_ref, turned_ref, zero_ref, length_ref
):
    leaves = pack_ref.shape[0] - 8
    offset = place_ref[0:1, 0:1]
    far = offset - place_ref[0:1, 1:2]
    rows = pack_ref[0:leaves, :]
    parts = split(rows)
    index = own_index(pad_rows(neighbours_ref[...]), far)
    seen = jnp.concatenate(
        [dot(pick(index[f ^ 1 : (f ^ 1) + 1, :], (leaves, leaves), 0), parts) for f in range(FACES)],
        axis=0,
    )
    face = face_ref[...]
    mortars, _, _ = read_tables(pack_ref, leaves)
    far_mortars, columns, scale = read_tables(far_ref, leaves)
    slots = mortars.shape[1]
    far_face = columns[:, 1:2]
    fine = own_index(columns, offset)
    chosen = [pick(fine[:, 2 + q : 3 + q], (slots, leaves), 1) for q in range(4)]
    chosen = dot(jnp.concatenate(chosen + [own_pick_ref[...]], axis=0), parts)
    trace = side_traces(chosen, [opposite(far_face)] * 4 + [face], table)
    quarters = [trace[slots * q : slots * (q + 1), :] for q in range(4)]
    sent = lift(trace[4 * slots :, :], [face], table)
    sent.append(lower(quarters, far_face, table, STAY_AT))
    back = fine_backs(mortars, far, leaves)
    extra = fine_count([back], [face])
    backs = [back, pick(far_mortars[0:1, :] - far, (leaves, slots), 0)]
    mortars = dot(jnp.concatenate(backs, axis=1), jnp.concatenate(sent, axis=0))
    lapped = extra * far_ref[0:leaves, :] - across_faces(seen) - fold(mortars)
    rows_ref[...] = scale * placed(lapped)
    turned_ref[...] = image_ref[...].T
    length, zero = unit(rows / scale_ref[...])
    zero_ref[...] = zero
    length_ref[...] = jnp.broadcast_to(length, length_ref.shape)


def total(values):
    return jnp.sum(values, keepdims=True)


def unit(values):
    length = jnp.sqrt(total(values * values))
    return length, values * jnp.where(length > 0.0, 1.0 / jnp.where(length > 0.0, length, 1.0), 0.0)


def in_lanes(shape, values):
    lane = lax.broadcasted_iota(jnp.int32, shape, 1)
    row = jnp.zeros(shape, F32)
    for at, value in enumerate(values):
        row = jnp.where(lane == at, value, row)
    return row


def second_kernel(
    table, send_ref, one_ref, two_ref, lacked_ref, image_ref, total_ref, zero_ref, length_ref, faces_two_ref,
    two_fine_ref, two_pick_ref, two_back_ref, two_face_ref, *refs
):
    kept = dict(zip(CHOSEN + MADE[1:], refs))
    stats_ref = refs[len(CHOSEN) + len(MADE) - 1]
    image, zero = image_ref[...], zero_ref[...]
    r01 = total(zero * image)
    rest = image - r01 * zero
    again = total(zero * rest)
    r11, one = unit(rest - again * zero)
    rows = send_ref[...]
    parts = [split(rows), split(one_ref[...]), split(two_ref[...] + lacked_ref[...])]
    face = kept["face"][...]
    lapped = total_ref[...] * rows + fold(dot(parts[0], kept["stiff"][...])) - from_blocks(
        parts,
        [kept["own"][...], kept["one"][...], faces_two_ref[...]],
        [kept["own_fine"][...], kept["one_fine"][...], two_fine_ref[...]],
        [kept["own_pick"][...], kept["one_pick"][...], two_pick_ref[...]],
        [kept["fine_back"][...], kept["one_back"][...], two_back_ref[...]],
        [face, kept["one_face"][...], two_face_ref[...]],
        face,
        kept["own_back"][...],
        table,
        True,
    )
    image = image_of(image, lapped, kept)
    r02 = total(zero * image)
    r12 = total(one * image)
    rest = image - r02 * zero - r12 * one
    r22 = jnp.sqrt(total(rest * rest))
    values = (length_ref[0:1, 0:1], r01 + again, r11, r02, r12, r22)
    stats_ref[...] = in_lanes(stats_ref.shape, values)


def final_kernel(stats_ref, cot_ref, image_ref, out_ref):
    table = stats_ref[...].T
    a0, a1, b1, a2, b2, c2 = [table[at : at + 1, :] for at in range(6)]
    r00_sq = total(a0 * a0)
    r00 = jnp.sqrt(r00_sq)
    f01 = total(a0 * a1) / r00_sq
    f02 = total(a0 * a2) / r00_sq
    a1 = a1 - f01 * a0
    a2 = a2 - f02 * a0
    r11_sq = total(a1 * a1) + total(b1 * b1)
    r11 = jnp.sqrt(r11_sq)
    f12 = (total(a1 * a2) + total(b1 * b2)) / r11_sq
    a2 = a2 - f12 * a1
    b2 = b2 - f12 * b1
    r22 = jnp.sqrt(total(a2 * a2) + total(b2 * b2) + total(c2 * c2))
    rhs_norm = r00
    first_diag = f01
    first_below = r11 / r00
    upper_right = (f02 - first_diag * f01) / first_below
    second_diag = f12 - first_diag
    second_below = r22 / r11
    first_len = jnp.sqrt(first_diag * first_diag + first_below * first_below)
    cos_one = first_diag / first_len
    sin_one = first_below / first_len
    rotated_top = cos_one * upper_right + sin_one * second_diag
    rotated_low = cos_one * second_diag - sin_one * upper_right
    second_len = jnp.sqrt(rotated_low * rotated_low + second_below * second_below)
    cos_two = rotated_low / second_len
    y_two = cos_two * (-sin_one * rhs_norm) / second_len
    y_one = (cos_one * rhs_norm - rotated_top * y_two) / first_len
    on_one = y_two / r11
    on_base = y_one / r00 - on_one * f01
    out_ref[...] = on_base * cot_ref[...] + on_one * image_ref[...]


def on_device(cotangent, nodal_mass, curvature, stiffness, levels, neighbours, mortars):
    fields, nodes, leaves = cotangent.shape
    slots = mortars.shape[1]
    count = lax.axis_size("leaf")
    flat = cotangent.reshape(fields * nodes, leaves)
    levels = levels.reshape(1, leaves)
    me = lax.axis_index("leaf").astype(jnp.int32)
    place = jnp.stack([me * leaves, leaves - 2 * leaves * (me & 1)]).reshape(1, 2)
    table = jnp.asarray(matrices())
    vmem = pl.BlockSpec(memory_space=pltpu.VMEM)
    hbm = pl.BlockSpec(memory_space=pltpu.HBM)

    def call(kernel, outs, specs, operands, scratch=(), flops=0, moved=0, mib=40):
        return pl.pallas_call(
            kernel,
            out_shape=outs,
            in_specs=specs,
            out_specs=jax.tree.map(lambda _: vmem, outs),
            scratch_shapes=scratch,
            compiler_params=pltpu.CompilerParams(vmem_limit_bytes=mib * 1024 * 1024),
            cost_estimate=pl.CostEstimate(flops=flops, bytes_accessed=moved, transcendentals=0),
        )(*operands)

    def shape(*dims, dtype=F32):
        return jax.ShapeDtypeStruct(dims, dtype)

    pairs_one = [(i, i ^ 1) for i in range(count) if i ^ 1 < count]
    pairs_two = [(i, i + 1) for i in range(1, count - 1, 2)]
    pairs_two = pairs_two + [(j, i) for i, j in pairs_two]

    wide = 2 * LANES
    rows = shape(leaves, LANES)
    faces = shape(FACES * leaves, leaves, dtype=BF16)
    fine = shape(4 * slots, leaves, dtype=BF16)
    picks = shape(slots, leaves, dtype=BF16)
    backs = shape(leaves, 4 * slots, dtype=BF16)
    face = shape(slots, 1, dtype=jnp.int32)
    shapes = dict(
        own=faces,
        one=faces,
        own_fine=fine,
        one_fine=fine,
        own_pick=picks,
        own_back=shape(leaves, slots, dtype=BF16),
        fine_back=backs,
        face=face,
        diagonal=rows,
        stiff=shape(wide, wide, dtype=BF16),
        mass=rows,
        curve=rows,
        scale=rows,
        one_pick=picks,
        one_back=backs,
        one_face=face,
    )

    def stay_out(*arrays):
        return tuple(pltpu.with_memory_space_constraint(array, pltpu.HBM) for array in arrays)

    pack = call(
        prep_kernel,
        shape(leaves + 8, LANES),
        [hbm] * 3,
        stay_out(flat, levels, mortars),
        scratch=[
            pltpu.VMEM(flat.shape, F32),
            pltpu.VMEM(levels.shape, jnp.int32),
            pltpu.VMEM(mortars.shape, jnp.int32),
            pltpu.SemaphoreType.DMA((3,)),
        ],
        flops=10_000_000_000,
        moved=4_000_000,
    )
    far = lax.ppermute(pack, "leaf", pairs_two)
    one = lax.ppermute(pack, "leaf", pairs_one)
    chosen = call(
        choose_kernel,
        [shapes[name] for name in CHOSEN],
        [vmem] * 3,
        (place, pack, neighbours),
    )
    *made, partial, scaled = call(
        first_kernel,
        [shapes[name] for name in MADE] + [rows, rows],
        [vmem] * (8 + len(CHOSEN)),
        [place, pack, one, table, nodal_mass, curvature, stiffness, levels, *chosen],
    )
    kept = dict(zip(CHOSEN + MADE, [*chosen, *made]))
    two = lax.ppermute(scaled, "leaf", pairs_two)
    image, send, faces_two, two_fine, two_pick, two_back, two_face, diagonal = call(
        far_kernel,
        [rows, rows, faces, fine, picks, backs, face, rows],
        [vmem] * 10,
        [place, pack, neighbours, far, table, kept["scale"], kept["diagonal"], partial,
         kept["own_back"], kept["face"]],
    )
    one = lax.ppermute(send, "leaf", pairs_one)
    lacked, turned, zero, length = call(
        far_rows_kernel,
        [rows, shape(LANES, leaves), rows, shape(1, LANES)],
        [vmem] * 9,
        [place, pack, neighbours, far, table, kept["scale"], kept["face"], kept["own_pick"],
         image],
        flops=1_000_000_000,
        moved=2_000_000,
    )
    stats = call(
        second_kernel,
        shape(1, LANES),
        [vmem] * (14 + len(CHOSEN) + len(MADE) - 1),
        [table, send, one, two, lacked, image, diagonal, zero, length, faces_two, two_fine, two_pick,
         two_back, two_face] + [kept[name] for name in CHOSEN + MADE[1:]],
    )
    gathered = lax.all_to_all(
        jnp.broadcast_to(stats, (count, LANES)), "leaf", 0, 0, tiled=True
    )
    out = call(final_kernel, shape(*flat.shape), [vmem] * 3, (gathered, flat, turned))
    return out.reshape(cotangent.shape)


def solution(mesh):
    placed = (
        P(None, None, "leaf"),
        P(None, "leaf"),
        P(None, "leaf"),
        P(),
        P("leaf"),
        P(None, "leaf"),
        P(None, "leaf"),
    )
    return jax.shard_map(
        on_device, mesh=mesh, in_specs=placed, out_specs=P(None, None, "leaf"), check_vma=False
    )
```

```python
import jax
import jax.numpy as jnp
import ml_dtypes
import numpy as np
from jax import lax
from jax.experimental import pallas as pl
from jax.experimental.pallas import tpu as pltpu
from jax.sharding import PartitionSpec as P

TAU_WEIGHT = 0.15
EPS_WEIGHT = 0.1
FACES = 6
NODES = 64
LANES = 128
F32 = jnp.float32
BF16 = jnp.bfloat16


def face_tables():
    node_at = np.zeros((6, 16), dtype=np.int64)
    for face_id in range(6):
        for row_pos in range(4):
            for col_pos in range(4):
                coords = [row_pos, col_pos]
                coords.insert(face_id // 2, 3 * (face_id % 2))
                node_at[face_id, 4 * row_pos + col_pos] = (
                    16 * coords[0] + 4 * coords[1] + coords[2]
                )
    points = np.array([-1.0, -1.0 / np.sqrt(5.0), 1.0 / np.sqrt(5.0), 1.0])
    halves = np.zeros((2, 4, 4))
    for half_id in range(2):
        target = (points + 2.0 * half_id - 1.0) / 2.0
        for column in range(4):
            lagrange = np.ones(4)
            for other_id in range(4):
                if other_id != column:
                    lagrange = (
                        lagrange * (target - points[other_id]) / (points[column] - points[other_id])
                    )
            halves[half_id, :, column] = lagrange
    mortar = np.stack([np.kron(halves[quarter // 2], halves[quarter % 2]) for quarter in range(4)])
    return node_at, mortar


def two_parts(table):
    high = table.astype(np.float32).astype(ml_dtypes.bfloat16)
    low = (table - high.astype(np.float64)).astype(np.float32).astype(ml_dtypes.bfloat16)
    return np.concatenate([high, low], axis=-1)


def matrices():
    node_at, mortar = face_tables()
    traces = np.zeros((2 * LANES, 2 * LANES))
    to_fine = np.zeros((4, 2 * LANES, LANES))
    to_coarse = np.zeros((4, 2 * LANES, LANES))
    stay = np.zeros((2 * LANES, LANES))
    square = sum(mortar[quarter].T @ mortar[quarter] for quarter in range(4))
    for face in range(FACES):
        for field in range(2):
            nodes = 64 * field + node_at[face]
            for part in range(2):
                for place in range(16):
                    at = part * LANES + 32 * (face // 2) + 16 * field + place
                    traces[part * LANES + nodes[place], at] = 1.0
                    stay[at, nodes] = -square[:, place]
                    for quarter in range(4):
                        to_fine[quarter, at, nodes] = mortar[quarter][:, place]
                        to_coarse[quarter, at, nodes] = mortar[quarter][place, :]
    return np.concatenate(
        [traces.astype(ml_dtypes.bfloat16)]
        + list(two_parts(to_fine))
        + list(two_parts(to_coarse))
        + [two_parts(stay)],
        axis=0,
    )


TRACES_AT, FINE_AT, COARSE_AT, STAY_AT, TABLE_ROWS = 0, 256, 1280, 2304, 2560


def split(values, axis=1):
    high = values.astype(BF16)
    return jnp.concatenate([high, (values - high.astype(F32)).astype(BF16)], axis=axis)


def dot(left, right):
    return jnp.dot(left, right, preferred_element_type=F32)


def fold(values):
    return values[:, :LANES] + values[:, LANES:]


def pick(index, shape, dim):
    places = lax.broadcasted_iota(jnp.int32, shape, dim).astype(F32).astype(BF16)
    index = jnp.broadcast_to(index.astype(F32), shape).astype(BF16)
    return jnp.where(index == places, jnp.ones(shape, BF16), jnp.zeros(shape, BF16))


def on_axis(face):
    lane = lax.broadcasted_iota(jnp.int32, (1, 2 * LANES), 1)
    axis = jnp.right_shift(face, 1)
    return jnp.where((jnp.right_shift(lane, 5) & 3) == axis, 1.0, 0.0).astype(BF16)


def face_nodes(face):
    lane = lax.broadcasted_iota(jnp.int32, (1, LANES), 1)
    axis = jnp.right_shift(face, 1)
    place = jnp.right_shift(lane, 4 - 2 * axis) & 3
    return jnp.where((place == 3 * (face & 1)) & (face >= 0), 1.0, 0.0)


def opposite(face):
    return jnp.where(face >= 0, face ^ 1, -1)


def fetch(pairs, sems):
    copies = [
        pltpu.make_async_copy(source, target, sems.at[at])
        for at, (source, target) in enumerate(pairs)
    ]
    for copy in copies:
        copy.start()
    return copies


def prep_kernel(cot_hbm, levels_hbm, mortars_hbm, pack_ref, cot_ref, levels_ref, mortars_ref, sems):
    for copy in fetch(
        ((cot_hbm, cot_ref), (levels_hbm, levels_ref), (mortars_hbm, mortars_ref)), sems
    ):
        copy.wait()
    leaves = cot_ref.shape[1]
    scale = jnp.left_shift(jnp.ones_like(levels_ref[...]), levels_ref[...]).astype(F32)
    pack_ref[0:leaves, :] = (cot_ref[...] * scale).T
    table = mortars_ref[...].astype(F32) + 1.0
    halves = [scale[:, k * table.shape[1] : (k + 1) * table.shape[1]] for k in range(2)]
    pack_ref[leaves : leaves + 8, :] = jnp.concatenate([table] + halves, axis=0)


CHOSEN = (
    "own", "one", "own_fine", "one_fine", "own_pick", "own_back", "fine_back", "face",
)
MADE = ("diagonal", "stiff", "mass", "curve", "scale", "one_pick", "one_back", "one_face")


def across_faces(seen):
    leaves = seen.shape[0] // FACES
    result = jnp.zeros((leaves, LANES), F32)
    for f in range(FACES):
        shift = 3 * 4 ** (2 - f // 2)
        part = fold(seen[leaves * f : leaves * (f + 1), :])
        part = pltpu.roll(part, shift if f % 2 else LANES - shift, 1)
        result = result + face_nodes(jnp.int32(f)) * part
    return result


def side_traces(chosen, faces, table):
    nodes = jnp.concatenate([face_nodes(face).astype(BF16) for face in faces], axis=0)
    axes = jnp.concatenate([on_axis(face) for face in faces], axis=0)
    nodes = jnp.concatenate([nodes, nodes], axis=1)
    trace = dot(chosen.astype(BF16) * nodes, table[TRACES_AT : TRACES_AT + 256, :])
    return trace.astype(BF16) * axes


def lift(trace, faces, table):
    mask = jnp.concatenate([face_nodes(opposite(face)) for face in faces], axis=0)
    return [
        split(mask * fold(dot(trace, table[FINE_AT + 256 * q : FINE_AT + 256 * (q + 1), :])))
        for q in range(4)
    ]


def lower(traces, face, table, last):
    back = dot(jnp.concatenate(traces, axis=1), table[COARSE_AT:last, :])
    return split(face_nodes(face) * fold(back))


def from_blocks(parts, faces, fine, picks, backs, coarse_faces, face, own_back, table, own):
    slots = own_back.shape[1]
    rows = jnp.concatenate(parts, axis=0)
    seen = dot(jnp.concatenate(faces, axis=1), rows)
    chosen = [dot(jnp.concatenate(fine, axis=1), rows)]
    chosen += [dot(pick_rows, part) for pick_rows, part in zip(picks, parts)]
    trace = side_traces(
        jnp.concatenate(chosen, axis=0), [opposite(face)] * 4 + coarse_faces, table
    )
    quarters = [trace[slots * q : slots * (q + 1), :] for q in range(4)]
    sent = lift(trace[4 * slots :, :], coarse_faces, table)
    ordered = [
        sent[q][slots * k : slots * (k + 1), :] for k in range(len(parts)) for q in range(4)
    ]
    if own:
        quarters.append(trace[4 * slots : 5 * slots, :])
    ordered.append(lower(quarters, face, table, TABLE_ROWS if own else STAY_AT))
    mortars = dot(jnp.concatenate(backs + [own_back], axis=1), jnp.concatenate(ordered, axis=0))
    return fold(mortars) + across_faces(seen)


def placed(lapped):
    first = lax.broadcasted_iota(jnp.int32, lapped.shape, 1) < NODES
    return jnp.where(first, -EPS_WEIGHT, TAU_WEIGHT) * pltpu.roll(lapped, NODES, 1)


def fine_count(backs, faces):
    weights = [face_nodes(opposite(face)).astype(BF16) for face in faces for _ in range(4)]
    return dot(jnp.concatenate(backs, axis=1), jnp.concatenate(weights, axis=0))


def own_index(index, offset):
    return jnp.where(index < 0, -1, index - offset)


def to_columns(table):
    return table.astype(F32).T.astype(jnp.int32)


def fine_backs(table, offset, leaves):
    index = own_index(table, offset)
    return jnp.concatenate(
        [pick(index[2 + q : 3 + q, :], (leaves, table.shape[1]), 0) for q in range(4)], axis=1
    )


def choose(refs, kinds, columns, neighbours, leaves):
    slots = columns.shape[0]
    for faces_ref, fine_ref, start, own in kinds:
        index = own_index(neighbours, start)
        across = index if own else to_columns(index)
        for f in range(FACES):
            refs[faces_ref][leaves * f : leaves * (f + 1), :] = (
                pick(across[f ^ 1 : (f ^ 1) + 1, :], (leaves, leaves), 0)
                if own
                else pick(across[:, f : f + 1], (leaves, leaves), 1)
            )
        fine = own_index(columns, start)
        for q in range(4):
            refs[fine_ref][slots * q : slots * (q + 1), :] = pick(
                fine[:, 2 + q : 3 + q], (slots, leaves), 1
            )


def read_tables(pack_ref, leaves):
    table = pack_ref[leaves : leaves + 8, :]
    columns = table.T
    scale = jnp.concatenate([columns[:, 6:7], columns[:, 7:8]], axis=0)
    return table.astype(jnp.int32) - 1, columns.astype(jnp.int32) - 1, scale


def pad_rows(neighbours):
    return jnp.concatenate(
        [neighbours, jnp.full((2, neighbours.shape[1]), -1, jnp.int32)], axis=0
    )


def choose_kernel(place_ref, pack_ref, neighbours_ref, *refs):
    made = dict(zip(CHOSEN, refs))
    leaves = pack_ref.shape[0] - 8
    offset, first = place_ref[0:1, 0:1], place_ref[0:1, 1:2]
    mortars, columns, _ = read_tables(pack_ref, leaves)
    slots = mortars.shape[1]
    made["face"][...] = columns[:, 1:2]
    made["fine_back"][...] = fine_backs(mortars, offset, leaves)
    made["own_back"][...] = pick(mortars[0:1, :] - offset, (leaves, slots), 0)
    made["own_pick"][...] = pick(columns[:, 0:1] - offset, (slots, leaves), 1)
    kinds = (("own", "own_fine", offset, True), ("one", "one_fine", offset + first, False))
    choose(made, kinds, columns, pad_rows(neighbours_ref[...]), leaves)


def image_of(vector, lapped, kept):
    swapped = pltpu.roll(vector, NODES, 1)
    return kept["mass"][...] * vector + kept["curve"][...] * swapped + placed(lapped)


def first_kernel(
    place_ref, pack_ref, other_ref, table, mass_ref, curve_ref, stiffness_ref, *refs
):
    kept = dict(zip(CHOSEN + MADE, refs))
    image_ref, far_ref = refs[len(CHOSEN) + len(MADE) :]
    leaves = pack_ref.shape[0] - 8
    offset, first = place_ref[0:1, 0:1], place_ref[0:1, 1:2]
    mortars, columns, _ = read_tables(other_ref, leaves)
    slots = mortars.shape[1]
    face, other_face = kept["face"][...], columns[:, 1:2]
    other_pick = pick(columns[:, 0:1] - (offset + first), (slots, leaves), 1)
    other_back = fine_backs(mortars, offset, leaves)
    kept["one_pick"][...] = other_pick
    kept["one_back"][...] = other_back
    kept["one_face"][...] = other_face
    back = kept["fine_back"][...]
    diagonal = (
        fine_count([back, other_back], [face, other_face])
        + sum(face_nodes(jnp.int32(f)) for f in range(FACES))
    )
    kept["diagonal"][...] = diagonal
    wide = jnp.concatenate([stiffness_ref[...]] * 2, axis=1)
    wide = jnp.concatenate([wide, wide], axis=0)
    same = (lax.broadcasted_iota(jnp.int32, wide.shape, 0) < NODES) == (
        lax.broadcasted_iota(jnp.int32, wide.shape, 1) < NODES
    )
    wide = split(jnp.where(same, wide, 0.0))
    wide = jnp.concatenate([wide, wide], axis=0)
    kept["stiff"][...] = wide
    both = jnp.concatenate([mass_ref[...], curve_ref[...]], axis=0).T
    turned = pltpu.roll(both, NODES, 1)
    low = lax.broadcasted_iota(jnp.int32, (1, LANES), 1) < NODES
    kept["mass"][...] = jnp.where(low, both, turned)
    kept["curve"][...] = jnp.where(low, -turned, 0.0)
    scale = jnp.broadcast_to(read_tables(pack_ref, leaves)[2], both.shape)
    kept["scale"][...] = scale
    rows = pack_ref[0:leaves, :]
    parts = [split(rows), split(other_ref[0:leaves, :])]
    lapped = diagonal * rows + fold(dot(parts[0], wide)) - from_blocks(
        parts,
        [kept["own"][...], kept["one"][...]],
        [kept["own_fine"][...], kept["one_fine"][...]],
        [kept["own_pick"][...], other_pick],
        [back, other_back],
        [face, other_face],
        face,
        kept["own_back"][...],
        table,
        True,
    )
    image = image_of(rows / scale, lapped, kept)
    image_ref[...] = image
    far_ref[...] = image * scale


def far_kernel(
    place_ref, pack_ref, neighbours_ref, far_ref, table, scale_ref, diagonal_ref, partial_ref,
    own_back_ref, face_ref, image_ref, send_ref, two_ref, two_fine_ref, pick_ref, back_ref,
    far_face_ref, total_ref
):
    leaves = pack_ref.shape[0] - 8
    offset = place_ref[0:1, 0:1]
    start = offset - place_ref[0:1, 1:2]
    _, columns, _ = read_tables(pack_ref, leaves)
    neighbours = pad_rows(neighbours_ref[...])
    choose((two_ref, two_fine_ref), ((0, 1, start, False),), columns, neighbours, leaves)
    mortars, columns, _ = read_tables(far_ref, leaves)
    slots = mortars.shape[1]
    face = columns[:, 1:2]
    chosen = pick(columns[:, 0:1] - start, (slots, leaves), 1)
    back = fine_backs(mortars, offset, leaves)
    pick_ref[...] = chosen
    back_ref[...] = back
    far_face_ref[...] = face
    extra = fine_count([back], [face])
    total_ref[...] = diagonal_ref[...] + extra
    lapped = extra * pack_ref[0:leaves, :] - from_blocks(
        [split(far_ref[0:leaves, :])], [two_ref[...]], [two_fine_ref[...]], [chosen], [back],
        [face], face_ref[...], own_back_ref[...], table, False,
    )
    image = partial_ref[...] + placed(lapped)
    image_ref[...] = image
    send_ref[...] = image * scale_ref[...]


def far_rows_kernel(
    place_ref, pack_ref, neighbours_ref, far_ref, table, scale_ref, face_ref, own_pick_ref,
    image_ref, rows_ref, turned_ref, zero_ref, length_ref
):
    leaves = pack_ref.shape[0] - 8
    offset = place_ref[0:1, 0:1]
    far = offset - place_ref[0:1, 1:2]
    rows = pack_ref[0:leaves, :]
    parts = split(rows)
    index = own_index(pad_rows(neighbours_ref[...]), far)
    seen = jnp.concatenate(
        [dot(pick(index[f ^ 1 : (f ^ 1) + 1, :], (leaves, leaves), 0), parts) for f in range(FACES)],
        axis=0,
    )
    face = face_ref[...]
    mortars, _, _ = read_tables(pack_ref, leaves)
    far_mortars, columns, scale = read_tables(far_ref, leaves)
    slots = mortars.shape[1]
    far_face = columns[:, 1:2]
    fine = own_index(columns, offset)
    chosen = [pick(fine[:, 2 + q : 3 + q], (slots, leaves), 1) for q in range(4)]
    chosen = dot(jnp.concatenate(chosen + [own_pick_ref[...]], axis=0), parts)
    trace = side_traces(chosen, [opposite(far_face)] * 4 + [face], table)
    quarters = [trace[slots * q : slots * (q + 1), :] for q in range(4)]
    sent = lift(trace[4 * slots :, :], [face], table)
    sent.append(lower(quarters, far_face, table, STAY_AT))
    back = fine_backs(mortars, far, leaves)
    extra = fine_count([back], [face])
    backs = [back, pick(far_mortars[0:1, :] - far, (leaves, slots), 0)]
    mortars = dot(jnp.concatenate(backs, axis=1), jnp.concatenate(sent, axis=0))
    lapped = extra * far_ref[0:leaves, :] - across_faces(seen) - fold(mortars)
    rows_ref[...] = scale * placed(lapped)
    turned_ref[...] = image_ref[...].T
    length, zero = unit(rows / scale_ref[...])
    zero_ref[...] = zero
    length_ref[...] = jnp.broadcast_to(length, length_ref.shape)


def total(values):
    return jnp.sum(values, keepdims=True)


def unit(values):
    length = jnp.sqrt(total(values * values))
    return length, values * jnp.where(length > 0.0, 1.0 / jnp.where(length > 0.0, length, 1.0), 0.0)


def in_lanes(shape, values):
    lane = lax.broadcasted_iota(jnp.int32, shape, 1)
    row = jnp.zeros(shape, F32)
    for at, value in enumerate(values):
        row = jnp.where(lane == at, value, row)
    return row


def second_kernel(
    table, send_ref, one_ref, two_ref, lacked_ref, image_ref, total_ref, zero_ref, length_ref, faces_two_ref,
    two_fine_ref, two_pick_ref, two_back_ref, two_face_ref, *refs
):
    kept = dict(zip(CHOSEN + MADE[1:], refs))
    stats_ref = refs[len(CHOSEN) + len(MADE) - 1]
    image, zero = image_ref[...], zero_ref[...]
    r01 = total(zero * image)
    rest = image - r01 * zero
    again = total(zero * rest)
    r11, one = unit(rest - again * zero)
    rows = send_ref[...]
    parts = [split(rows), split(one_ref[...]), split(two_ref[...] + lacked_ref[...])]
    face = kept["face"][...]
    lapped = total_ref[...] * rows + fold(dot(parts[0], kept["stiff"][...])) - from_blocks(
        parts,
        [kept["own"][...], kept["one"][...], faces_two_ref[...]],
        [kept["own_fine"][...], kept["one_fine"][...], two_fine_ref[...]],
        [kept["own_pick"][...], kept["one_pick"][...], two_pick_ref[...]],
        [kept["fine_back"][...], kept["one_back"][...], two_back_ref[...]],
        [face, kept["one_face"][...], two_face_ref[...]],
        face,
        kept["own_back"][...],
        table,
        True,
    )
    image = image_of(image, lapped, kept)
    r02 = total(zero * image)
    r12 = total(one * image)
    rest = image - r02 * zero - r12 * one
    r22 = jnp.sqrt(total(rest * rest))
    values = (length_ref[0:1, 0:1], r01 + again, r11, r02, r12, r22)
    stats_ref[...] = in_lanes(stats_ref.shape, values)


def final_kernel(stats_ref, cot_ref, image_ref, out_ref):
    table = stats_ref[...].T
    a0, a1, b1, a2, b2, c2 = [table[at : at + 1, :] for at in range(6)]
    r00_sq = total(a0 * a0)
    r00 = jnp.sqrt(r00_sq)
    f01 = total(a0 * a1) / r00_sq
    f02 = total(a0 * a2) / r00_sq
    a1 = a1 - f01 * a0
    a2 = a2 - f02 * a0
    r11_sq = total(a1 * a1) + total(b1 * b1)
    r11 = jnp.sqrt(r11_sq)
    f12 = (total(a1 * a2) + total(b1 * b2)) / r11_sq
    a2 = a2 - f12 * a1
    b2 = b2 - f12 * b1
    r22 = jnp.sqrt(total(a2 * a2) + total(b2 * b2) + total(c2 * c2))
    rhs_norm = r00
    first_diag = f01
    first_below = r11 / r00
    upper_right = (f02 - first_diag * f01) / first_below
    second_diag = f12 - first_diag
    second_below = r22 / r11
    first_len = jnp.sqrt(first_diag * first_diag + first_below * first_below)
    cos_one = first_diag / first_len
    sin_one = first_below / first_len
    rotated_top = cos_one * upper_right + sin_one * second_diag
    rotated_low = cos_one * second_diag - sin_one * upper_right
    second_len = jnp.sqrt(rotated_low * rotated_low + second_below * second_below)
    cos_two = rotated_low / second_len
    y_two = cos_two * (-sin_one * rhs_norm) / second_len
    y_one = (cos_one * rhs_norm - rotated_top * y_two) / first_len
    on_one = y_two / r11
    on_base = y_one / r00 - on_one * f01
    out_ref[...] = on_base * cot_ref[...] + on_one * image_ref[...]


def on_device(cotangent, nodal_mass, curvature, stiffness, levels, neighbours, mortars):
    fields, nodes, leaves = cotangent.shape
    slots = mortars.shape[1]
    count = lax.axis_size("leaf")
    flat = cotangent.reshape(fields * nodes, leaves)
    levels = levels.reshape(1, leaves)
    me = lax.axis_index("leaf").astype(jnp.int32)
    place = jnp.stack([me * leaves, leaves - 2 * leaves * (me & 1)]).reshape(1, 2)
    table = jnp.asarray(matrices())
    vmem = pl.BlockSpec(memory_space=pltpu.VMEM)
    hbm = pl.BlockSpec(memory_space=pltpu.HBM)

    def call(kernel, outs, specs, operands, scratch=(), flops=0, moved=0, mib=40):
        return pl.pallas_call(
            kernel,
            out_shape=outs,
            in_specs=specs,
            out_specs=jax.tree.map(lambda _: vmem, outs),
            scratch_shapes=scratch,
            compiler_params=pltpu.CompilerParams(vmem_limit_bytes=mib * 1024 * 1024),
            cost_estimate=pl.CostEstimate(flops=flops, bytes_accessed=moved, transcendentals=0),
        )(*operands)

    def shape(*dims, dtype=F32):
        return jax.ShapeDtypeStruct(dims, dtype)

    pairs_one = [(i, i ^ 1) for i in range(count) if i ^ 1 < count]
    pairs_two = [(i, i + 1) for i in range(1, count - 1, 2)]
    pairs_two = pairs_two + [(j, i) for i, j in pairs_two]

    wide = 2 * LANES
    rows = shape(leaves, LANES)
    faces = shape(FACES * leaves, leaves, dtype=BF16)
    fine = shape(4 * slots, leaves, dtype=BF16)
    picks = shape(slots, leaves, dtype=BF16)
    backs = shape(leaves, 4 * slots, dtype=BF16)
    face = shape(slots, 1, dtype=jnp.int32)
    shapes = dict(
        own=faces,
        one=faces,
        own_fine=fine,
        one_fine=fine,
        own_pick=picks,
        own_back=shape(leaves, slots, dtype=BF16),
        fine_back=backs,
        face=face,
        diagonal=rows,
        stiff=shape(wide, wide, dtype=BF16),
        mass=rows,
        curve=rows,
        scale=rows,
        one_pick=picks,
        one_back=backs,
        one_face=face,
    )

    def stay_out(*arrays):
        return tuple(pltpu.with_memory_space_constraint(array, pltpu.HBM) for array in arrays)

    pack = call(
        prep_kernel,
        shape(leaves + 8, LANES),
        [hbm] * 3,
        stay_out(flat, levels, mortars),
        scratch=[
            pltpu.VMEM(flat.shape, F32),
            pltpu.VMEM(levels.shape, jnp.int32),
            pltpu.VMEM(mortars.shape, jnp.int32),
            pltpu.SemaphoreType.DMA((3,)),
        ],
        flops=10_000_000_000,
        moved=4_000_000,
    )
    far = lax.ppermute(pack, "leaf", pairs_two)
    one = lax.ppermute(pack, "leaf", pairs_one)
    chosen = call(
        choose_kernel,
        [shapes[name] for name in CHOSEN],
        [vmem] * 3,
        (place, pack, neighbours),
    )
    *made, partial, scaled = call(
        first_kernel,
        [shapes[name] for name in MADE] + [rows, rows],
        [vmem] * (7 + len(CHOSEN)),
        [place, pack, one, table, nodal_mass, curvature, stiffness, *chosen],
    )
    kept = dict(zip(CHOSEN + MADE, [*chosen, *made]))
    two = lax.ppermute(scaled, "leaf", pairs_two)
    image, send, faces_two, two_fine, two_pick, two_back, two_face, diagonal = call(
        far_kernel,
        [rows, rows, faces, fine, picks, backs, face, rows],
        [vmem] * 10,
        [place, pack, neighbours, far, table, kept["scale"], kept["diagonal"], partial,
         kept["own_back"], kept["face"]],
    )
    one = lax.ppermute(send, "leaf", pairs_one)
    lacked, turned, zero, length = call(
        far_rows_kernel,
        [rows, shape(LANES, leaves), rows, shape(1, LANES)],
        [vmem] * 9,
        [place, pack, neighbours, far, table, kept["scale"], kept["face"], kept["own_pick"],
         image],
        flops=1_000_000_000,
        moved=2_000_000,
    )
    stats = call(
        second_kernel,
        shape(1, LANES),
        [vmem] * (14 + len(CHOSEN) + len(MADE) - 1),
        [table, send, one, two, lacked, image, diagonal, zero, length, faces_two, two_fine, two_pick,
         two_back, two_face] + [kept[name] for name in CHOSEN + MADE[1:]],
    )
    gathered = lax.all_to_all(
        jnp.broadcast_to(stats, (count, LANES)), "leaf", 0, 0, tiled=True
    )
    out = call(final_kernel, shape(*flat.shape), [vmem] * 3, (gathered, flat, turned))
    return out.reshape(cotangent.shape)


def solution(mesh):
    placed = (
        P(None, None, "leaf"),
        P(None, "leaf"),
        P(None, "leaf"),
        P(),
        P("leaf"),
        P(None, "leaf"),
        P(None, "leaf"),
    )
    return jax.shard_map(
        on_device, mesh=mesh, in_specs=placed, out_specs=P(None, None, "leaf"), check_vma=False
    )
```

```python
import jax
import jax.numpy as jnp
import ml_dtypes
import numpy as np
from jax import lax
from jax.experimental import pallas as pl
from jax.experimental.pallas import tpu as pltpu
from jax.sharding import PartitionSpec as P

TAU_WEIGHT = 0.15
EPS_WEIGHT = 0.1
FACES = 6
NODES = 64
LANES = 128
F32 = jnp.float32
BF16 = jnp.bfloat16


def face_tables():
    node_at = np.zeros((6, 16), dtype=np.int64)
    for face_id in range(6):
        for row_pos in range(4):
            for col_pos in range(4):
                coords = [row_pos, col_pos]
                coords.insert(face_id // 2, 3 * (face_id % 2))
                node_at[face_id, 4 * row_pos + col_pos] = (
                    16 * coords[0] + 4 * coords[1] + coords[2]
                )
    points = np.array([-1.0, -1.0 / np.sqrt(5.0), 1.0 / np.sqrt(5.0), 1.0])
    halves = np.zeros((2, 4, 4))
    for half_id in range(2):
        target = (points + 2.0 * half_id - 1.0) / 2.0
        for column in range(4):
            lagrange = np.ones(4)
            for other_id in range(4):
                if other_id != column:
                    lagrange = (
                        lagrange * (target - points[other_id]) / (points[column] - points[other_id])
                    )
            halves[half_id, :, column] = lagrange
    mortar = np.stack([np.kron(halves[quarter // 2], halves[quarter % 2]) for quarter in range(4)])
    return node_at, mortar


def two_parts(table):
    high = table.astype(np.float32).astype(ml_dtypes.bfloat16)
    low = (table - high.astype(np.float64)).astype(np.float32).astype(ml_dtypes.bfloat16)
    return np.concatenate([high, low], axis=-1)


def matrices():
    node_at, mortar = face_tables()
    traces = np.zeros((2 * LANES, 2 * LANES))
    to_fine = np.zeros((4, 2 * LANES, LANES))
    to_coarse = np.zeros((4, 2 * LANES, LANES))
    stay = np.zeros((2 * LANES, LANES))
    square = sum(mortar[quarter].T @ mortar[quarter] for quarter in range(4))
    for face in range(FACES):
        for field in range(2):
            nodes = 64 * field + node_at[face]
            for part in range(2):
                for place in range(16):
                    at = part * LANES + 32 * (face // 2) + 16 * field + place
                    traces[part * LANES + nodes[place], at] = 1.0
                    stay[at, nodes] = -square[:, place]
                    for quarter in range(4):
                        to_fine[quarter, at, nodes] = mortar[quarter][:, place]
                        to_coarse[quarter, at, nodes] = mortar[quarter][place, :]
    return np.concatenate(
        [traces.astype(ml_dtypes.bfloat16)]
        + list(two_parts(to_fine))
        + list(two_parts(to_coarse))
        + [two_parts(stay)],
        axis=0,
    )


TRACES_AT, FINE_AT, COARSE_AT, STAY_AT, TABLE_ROWS = 0, 256, 1280, 2304, 2560


def split(values, axis=1):
    high = values.astype(BF16)
    return jnp.concatenate([high, (values - high.astype(F32)).astype(BF16)], axis=axis)


def dot(left, right):
    return jnp.dot(left, right, preferred_element_type=F32)


def fold(values):
    return values[:, :LANES] + values[:, LANES:]


def pick(index, shape, dim):
    places = lax.broadcasted_iota(jnp.int32, shape, dim).astype(F32).astype(BF16)
    index = jnp.broadcast_to(index.astype(F32), shape).astype(BF16)
    return jnp.where(index == places, jnp.ones(shape, BF16), jnp.zeros(shape, BF16))


def on_axis(face):
    lane = lax.broadcasted_iota(jnp.int32, (1, 2 * LANES), 1)
    axis = jnp.right_shift(face, 1)
    return jnp.where((jnp.right_shift(lane, 5) & 3) == axis, 1.0, 0.0).astype(BF16)


def face_nodes(face):
    lane = lax.broadcasted_iota(jnp.int32, (1, LANES), 1)
    axis = jnp.right_shift(face, 1)
    place = jnp.right_shift(lane, 4 - 2 * axis) & 3
    return jnp.where((place == 3 * (face & 1)) & (face >= 0), 1.0, 0.0)


def opposite(face):
    return jnp.where(face >= 0, face ^ 1, -1)


def fetch(pairs, sems):
    copies = [
        pltpu.make_async_copy(source, target, sems.at[at])
        for at, (source, target) in enumerate(pairs)
    ]
    for copy in copies:
        copy.start()
    return copies


def prep_kernel(cot_hbm, levels_hbm, mortars_hbm, pack_ref, cot_ref, levels_ref, mortars_ref, sems):
    for copy in fetch(
        ((cot_hbm, cot_ref), (levels_hbm, levels_ref), (mortars_hbm, mortars_ref)), sems
    ):
        copy.wait()
    leaves = cot_ref.shape[1]
    scale = jnp.left_shift(jnp.ones_like(levels_ref[...]), levels_ref[...]).astype(F32)
    pack_ref[0:leaves, :] = (cot_ref[...] * scale).T
    table = mortars_ref[...].astype(F32) + 1.0
    halves = [scale[:, k * table.shape[1] : (k + 1) * table.shape[1]] for k in range(2)]
    pack_ref[leaves : leaves + 8, :] = jnp.concatenate([table] + halves, axis=0)


CHOSEN = (
    "own", "one", "own_fine", "one_fine", "own_pick", "own_back", "fine_back", "face",
)
MADE = ("diagonal", "stiff", "mass", "curve", "scale", "one_pick", "one_back", "one_face")


def across_faces(seen):
    leaves = seen.shape[0] // FACES
    result = jnp.zeros((leaves, LANES), F32)
    for f in range(FACES):
        shift = 3 * 4 ** (2 - f // 2)
        part = fold(seen[leaves * f : leaves * (f + 1), :])
        part = pltpu.roll(part, shift if f % 2 else LANES - shift, 1)
        result = result + face_nodes(jnp.int32(f)) * part
    return result


def side_traces(chosen, faces, table):
    nodes = jnp.concatenate([face_nodes(face).astype(BF16) for face in faces], axis=0)
    axes = jnp.concatenate([on_axis(face) for face in faces], axis=0)
    nodes = jnp.concatenate([nodes, nodes], axis=1)
    trace = dot(chosen.astype(BF16) * nodes, table[TRACES_AT : TRACES_AT + 256, :])
    return trace.astype(BF16) * axes


def lift(trace, faces, table):
    mask = jnp.concatenate([face_nodes(opposite(face)) for face in faces], axis=0)
    return [
        split(mask * fold(dot(trace, table[FINE_AT + 256 * q : FINE_AT + 256 * (q + 1), :])))
        for q in range(4)
    ]


def lower(traces, face, table, last):
    back = dot(jnp.concatenate(traces, axis=1), table[COARSE_AT:last, :])
    return split(face_nodes(face) * fold(back))


def from_blocks(parts, faces, fine, picks, backs, coarse_faces, face, own_back, table, own):
    slots = own_back.shape[1]
    rows = jnp.concatenate(parts, axis=0)
    seen = dot(jnp.concatenate(faces, axis=1), rows)
    chosen = [dot(jnp.concatenate(fine, axis=1), rows)]
    chosen += [dot(pick_rows, part) for pick_rows, part in zip(picks, parts)]
    trace = side_traces(
        jnp.concatenate(chosen, axis=0), [opposite(face)] * 4 + coarse_faces, table
    )
    quarters = [trace[slots * q : slots * (q + 1), :] for q in range(4)]
    sent = lift(trace[4 * slots :, :], coarse_faces, table)
    ordered = [
        sent[q][slots * k : slots * (k + 1), :] for k in range(len(parts)) for q in range(4)
    ]
    if own:
        quarters.append(trace[4 * slots : 5 * slots, :])
    ordered.append(lower(quarters, face, table, TABLE_ROWS if own else STAY_AT))
    mortars = dot(jnp.concatenate(backs + [own_back], axis=1), jnp.concatenate(ordered, axis=0))
    return fold(mortars) + across_faces(seen)


def placed(lapped):
    first = lax.broadcasted_iota(jnp.int32, lapped.shape, 1) < NODES
    return jnp.where(first, -EPS_WEIGHT, TAU_WEIGHT) * pltpu.roll(lapped, NODES, 1)


def fine_count(backs, faces):
    weights = [face_nodes(opposite(face)).astype(BF16) for face in faces for _ in range(4)]
    return dot(jnp.concatenate(backs, axis=1), jnp.concatenate(weights, axis=0))


def own_index(index, offset):
    return jnp.where(index < 0, -1, index - offset)


def to_columns(table):
    return table.astype(F32).T.astype(jnp.int32)


def fine_backs(table, offset, leaves):
    index = own_index(table, offset)
    return jnp.concatenate(
        [pick(index[2 + q : 3 + q, :], (leaves, table.shape[1]), 0) for q in range(4)], axis=1
    )


def choose(refs, kinds, columns, neighbours, leaves):
    slots = columns.shape[0]
    for faces_ref, fine_ref, start, own in kinds:
        index = own_index(neighbours, start)
        across = index if own else to_columns(index)
        for f in range(FACES):
            refs[faces_ref][leaves * f : leaves * (f + 1), :] = (
                pick(across[f ^ 1 : (f ^ 1) + 1, :], (leaves, leaves), 0)
                if own
                else pick(across[:, f : f + 1], (leaves, leaves), 1)
            )
        fine = own_index(columns, start)
        for q in range(4):
            refs[fine_ref][slots * q : slots * (q + 1), :] = pick(
                fine[:, 2 + q : 3 + q], (slots, leaves), 1
            )


def read_tables(pack_ref, leaves):
    table = pack_ref[leaves : leaves + 8, :]
    columns = table.T
    scale = jnp.concatenate([columns[:, 6:7], columns[:, 7:8]], axis=0)
    return table.astype(jnp.int32) - 1, columns.astype(jnp.int32) - 1, scale


def pad_rows(neighbours):
    return jnp.concatenate(
        [neighbours, jnp.full((2, neighbours.shape[1]), -1, jnp.int32)], axis=0
    )


def choose_kernel(place_ref, pack_ref, neighbours_ref, *refs):
    made = dict(zip(CHOSEN, refs))
    leaves = pack_ref.shape[0] - 8
    offset, first = place_ref[0:1, 0:1], place_ref[0:1, 1:2]
    mortars, columns, _ = read_tables(pack_ref, leaves)
    slots = mortars.shape[1]
    made["face"][...] = columns[:, 1:2]
    made["fine_back"][...] = fine_backs(mortars, offset, leaves)
    made["own_back"][...] = pick(mortars[0:1, :] - offset, (leaves, slots), 0)
    made["own_pick"][...] = pick(columns[:, 0:1] - offset, (slots, leaves), 1)
    kinds = (("own", "own_fine", offset, True), ("one", "one_fine", offset + first, False))
    choose(made, kinds, columns, pad_rows(neighbours_ref[...]), leaves)


def image_of(vector, lapped, kept):
    swapped = pltpu.roll(vector, NODES, 1)
    return kept["mass"][...] * vector + kept["curve"][...] * swapped + placed(lapped)


def first_kernel(
    place_ref, pack_ref, other_ref, table, mass_ref, curve_ref, stiffness_ref, *refs
):
    kept = dict(zip(CHOSEN + MADE, refs))
    image_ref, far_ref = refs[len(CHOSEN) + len(MADE) :]
    leaves = pack_ref.shape[0] - 8
    offset, first = place_ref[0:1, 0:1], place_ref[0:1, 1:2]
    mortars, columns, _ = read_tables(other_ref, leaves)
    slots = mortars.shape[1]
    face, other_face = kept["face"][...], columns[:, 1:2]
    other_pick = pick(columns[:, 0:1] - (offset + first), (slots, leaves), 1)
    other_back = fine_backs(mortars, offset, leaves)
    kept["one_pick"][...] = other_pick
    kept["one_back"][...] = other_back
    kept["one_face"][...] = other_face
    back = kept["fine_back"][...]
    diagonal = (
        fine_count([back, other_back], [face, other_face])
        + sum(face_nodes(jnp.int32(f)) for f in range(FACES))
    )
    kept["diagonal"][...] = diagonal
    wide = jnp.concatenate([stiffness_ref[...]] * 2, axis=1)
    wide = jnp.concatenate([wide, wide], axis=0)
    same = (lax.broadcasted_iota(jnp.int32, wide.shape, 0) < NODES) == (
        lax.broadcasted_iota(jnp.int32, wide.shape, 1) < NODES
    )
    wide = split(jnp.where(same, wide, 0.0))
    wide = jnp.concatenate([wide, wide], axis=0)
    kept["stiff"][...] = wide
    both = jnp.concatenate([mass_ref[...], curve_ref[...]], axis=0).T
    turned = pltpu.roll(both, NODES, 1)
    low = lax.broadcasted_iota(jnp.int32, (1, LANES), 1) < NODES
    kept["mass"][...] = jnp.where(low, both, turned)
    kept["curve"][...] = jnp.where(low, -turned, 0.0)
    scale = jnp.broadcast_to(read_tables(pack_ref, leaves)[2], both.shape)
    kept["scale"][...] = scale
    rows = pack_ref[0:leaves, :]
    parts = [split(rows), split(other_ref[0:leaves, :])]
    lapped = diagonal * rows + fold(dot(parts[0], wide)) - from_blocks(
        parts,
        [kept["own"][...], kept["one"][...]],
        [kept["own_fine"][...], kept["one_fine"][...]],
        [kept["own_pick"][...], other_pick],
        [back, other_back],
        [face, other_face],
        face,
        kept["own_back"][...],
        table,
        True,
    )
    image = image_of(rows / scale, lapped, kept)
    image_ref[...] = image
    far_ref[...] = image * scale


def far_kernel(
    place_ref, pack_ref, neighbours_ref, far_ref, table, scale_ref, diagonal_ref, partial_ref,
    own_back_ref, face_ref, image_ref, send_ref, two_ref, two_fine_ref, pick_ref, back_ref,
    far_face_ref, total_ref
):
    leaves = pack_ref.shape[0] - 8
    offset = place_ref[0:1, 0:1]
    start = offset - place_ref[0:1, 1:2]
    _, columns, _ = read_tables(pack_ref, leaves)
    neighbours = pad_rows(neighbours_ref[...])
    choose((two_ref, two_fine_ref), ((0, 1, start, False),), columns, neighbours, leaves)
    mortars, columns, _ = read_tables(far_ref, leaves)
    slots = mortars.shape[1]
    face = columns[:, 1:2]
    chosen = pick(columns[:, 0:1] - start, (slots, leaves), 1)
    back = fine_backs(mortars, offset, leaves)
    pick_ref[...] = chosen
    back_ref[...] = back
    far_face_ref[...] = face
    extra = fine_count([back], [face])
    total_ref[...] = diagonal_ref[...] + extra
    lapped = extra * pack_ref[0:leaves, :] - from_blocks(
        [split(far_ref[0:leaves, :])], [two_ref[...]], [two_fine_ref[...]], [chosen], [back],
        [face], face_ref[...], own_back_ref[...], table, False,
    )
    image = partial_ref[...] + placed(lapped)
    image_ref[...] = image
    send_ref[...] = image * scale_ref[...]


def far_rows_kernel(
    place_ref, pack_ref, neighbours_ref, far_ref, table, scale_ref, face_ref, own_pick_ref,
    image_ref, rows_ref, turned_ref, zero_ref, length_ref
):
    leaves = pack_ref.shape[0] - 8
    offset = place_ref[0:1, 0:1]
    far = offset - place_ref[0:1, 1:2]
    rows = pack_ref[0:leaves, :]
    parts = split(rows)
    index = own_index(pad_rows(neighbours_ref[...]), far)
    seen = jnp.concatenate(
        [dot(pick(index[f ^ 1 : (f ^ 1) + 1, :], (leaves, leaves), 0), parts) for f in range(FACES)],
        axis=0,
    )
    face = face_ref[...]
    mortars, _, _ = read_tables(pack_ref, leaves)
    far_mortars, columns, scale = read_tables(far_ref, leaves)
    slots = mortars.shape[1]
    far_face = columns[:, 1:2]
    fine = own_index(columns, offset)
    chosen = [pick(fine[:, 2 + q : 3 + q], (slots, leaves), 1) for q in range(4)]
    chosen = dot(jnp.concatenate(chosen + [own_pick_ref[...]], axis=0), parts)
    trace = side_traces(chosen, [opposite(far_face)] * 4 + [face], table)
    quarters = [trace[slots * q : slots * (q + 1), :] for q in range(4)]
    sent = lift(trace[4 * slots :, :], [face], table)
    sent.append(lower(quarters, far_face, table, STAY_AT))
    back = fine_backs(mortars, far, leaves)
    extra = fine_count([back], [face])
    backs = [back, pick(far_mortars[0:1, :] - far, (leaves, slots), 0)]
    mortars = dot(jnp.concatenate(backs, axis=1), jnp.concatenate(sent, axis=0))
    lapped = extra * far_ref[0:leaves, :] - across_faces(seen) - fold(mortars)
    rows_ref[...] = scale * placed(lapped)
    turned_ref[...] = image_ref[...].T
    length, zero = unit(rows / scale_ref[...])
    zero_ref[...] = zero
    length_ref[...] = jnp.broadcast_to(length, length_ref.shape)


def total(values):
    return jnp.sum(values, keepdims=True)


def unit(values):
    length = jnp.sqrt(total(values * values))
    return length, values * jnp.where(length > 0.0, 1.0 / jnp.where(length > 0.0, length, 1.0), 0.0)


def in_lanes(shape, values, first):
    lane = lax.broadcasted_iota(jnp.int32, shape, 1) - first
    row = jnp.zeros(shape, F32)
    for at, value in enumerate(values):
        row = jnp.where(lane == at, value, row)
    return row


def second_kernel(
    table, send_ref, one_ref, two_ref, lacked_ref, image_ref, total_ref, zero_ref, length_ref, faces_two_ref,
    two_fine_ref, two_pick_ref, two_back_ref, two_face_ref, *refs
):
    kept = dict(zip(CHOSEN + MADE[1:], refs))
    stats_ref = refs[len(CHOSEN) + len(MADE) - 1]
    image, zero = image_ref[...], zero_ref[...]
    r01 = total(zero * image)
    rest = image - r01 * zero
    again = total(zero * rest)
    r11, one = unit(rest - again * zero)
    rows = send_ref[...]
    parts = [split(rows), split(one_ref[...]), split(two_ref[...] + lacked_ref[...])]
    face = kept["face"][...]
    lapped = total_ref[...] * rows + fold(dot(parts[0], kept["stiff"][...])) - from_blocks(
        parts,
        [kept["own"][...], kept["one"][...], faces_two_ref[...]],
        [kept["own_fine"][...], kept["one_fine"][...], two_fine_ref[...]],
        [kept["own_pick"][...], kept["one_pick"][...], two_pick_ref[...]],
        [kept["fine_back"][...], kept["one_back"][...], two_back_ref[...]],
        [face, kept["one_face"][...], two_face_ref[...]],
        face,
        kept["own_back"][...],
        table,
        True,
    )
    image = image_of(image, lapped, kept)
    r02 = total(zero * image)
    r12 = total(one * image)
    rest = image - r02 * zero - r12 * one
    r22 = jnp.sqrt(total(rest * rest))
    values = (length_ref[0:1, 0:1], r01 + again, r11, r02, r12, r22)
    first = len(values) * (lax.axis_index("leaf") % 2)
    stats_ref[...] = in_lanes(stats_ref.shape, values, first)


def final_kernel(stats_ref, cot_ref, image_ref, out_ref):
    table = stats_ref[...].T
    a0, a1, b1, a2, b2, c2 = [
        jnp.concatenate([table[at : at + 1, :], table[at + 6 : at + 7, :]], axis=1)
        for at in range(6)
    ]
    r00_sq = total(a0 * a0)
    r00 = jnp.sqrt(r00_sq)
    f01 = total(a0 * a1) / r00_sq
    f02 = total(a0 * a2) / r00_sq
    a1 = a1 - f01 * a0
    a2 = a2 - f02 * a0
    r11_sq = total(a1 * a1) + total(b1 * b1)
    r11 = jnp.sqrt(r11_sq)
    f12 = (total(a1 * a2) + total(b1 * b2)) / r11_sq
    a2 = a2 - f12 * a1
    b2 = b2 - f12 * b1
    r22 = jnp.sqrt(total(a2 * a2) + total(b2 * b2) + total(c2 * c2))
    rhs_norm = r00
    first_diag = f01
    first_below = r11 / r00
    upper_right = (f02 - first_diag * f01) / first_below
    second_diag = f12 - first_diag
    second_below = r22 / r11
    first_len = jnp.sqrt(first_diag * first_diag + first_below * first_below)
    cos_one = first_diag / first_len
    sin_one = first_below / first_len
    rotated_top = cos_one * upper_right + sin_one * second_diag
    rotated_low = cos_one * second_diag - sin_one * upper_right
    second_len = jnp.sqrt(rotated_low * rotated_low + second_below * second_below)
    cos_two = rotated_low / second_len
    y_two = cos_two * (-sin_one * rhs_norm) / second_len
    y_one = (cos_one * rhs_norm - rotated_top * y_two) / first_len
    on_one = y_two / r11
    on_base = y_one / r00 - on_one * f01
    out_ref[...] = on_base * cot_ref[...] + on_one * image_ref[...]


def on_device(cotangent, nodal_mass, curvature, stiffness, levels, neighbours, mortars):
    fields, nodes, leaves = cotangent.shape
    slots = mortars.shape[1]
    count = lax.axis_size("leaf")
    flat = cotangent.reshape(fields * nodes, leaves)
    levels = levels.reshape(1, leaves)
    me = lax.axis_index("leaf").astype(jnp.int32)
    place = jnp.stack([me * leaves, leaves - 2 * leaves * (me & 1)]).reshape(1, 2)
    table = jnp.asarray(matrices())
    vmem = pl.BlockSpec(memory_space=pltpu.VMEM)
    hbm = pl.BlockSpec(memory_space=pltpu.HBM)

    def call(kernel, outs, specs, operands, scratch=(), flops=0, moved=0, mib=40):
        return pl.pallas_call(
            kernel,
            out_shape=outs,
            in_specs=specs,
            out_specs=jax.tree.map(lambda _: vmem, outs),
            scratch_shapes=scratch,
            compiler_params=pltpu.CompilerParams(vmem_limit_bytes=mib * 1024 * 1024),
            cost_estimate=pl.CostEstimate(flops=flops, bytes_accessed=moved, transcendentals=0),
        )(*operands)

    def shape(*dims, dtype=F32):
        return jax.ShapeDtypeStruct(dims, dtype)

    pairs_one = [(i, i ^ 1) for i in range(count) if i ^ 1 < count]
    pairs_two = [(i, i + 1) for i in range(1, count - 1, 2)]
    pairs_two = pairs_two + [(j, i) for i, j in pairs_two]

    wide = 2 * LANES
    rows = shape(leaves, LANES)
    faces = shape(FACES * leaves, leaves, dtype=BF16)
    fine = shape(4 * slots, leaves, dtype=BF16)
    picks = shape(slots, leaves, dtype=BF16)
    backs = shape(leaves, 4 * slots, dtype=BF16)
    face = shape(slots, 1, dtype=jnp.int32)
    shapes = dict(
        own=faces,
        one=faces,
        own_fine=fine,
        one_fine=fine,
        own_pick=picks,
        own_back=shape(leaves, slots, dtype=BF16),
        fine_back=backs,
        face=face,
        diagonal=rows,
        stiff=shape(wide, wide, dtype=BF16),
        mass=rows,
        curve=rows,
        scale=rows,
        one_pick=picks,
        one_back=backs,
        one_face=face,
    )

    def stay_out(*arrays):
        return tuple(pltpu.with_memory_space_constraint(array, pltpu.HBM) for array in arrays)

    pack = call(
        prep_kernel,
        shape(leaves + 8, LANES),
        [hbm] * 3,
        stay_out(flat, levels, mortars),
        scratch=[
            pltpu.VMEM(flat.shape, F32),
            pltpu.VMEM(levels.shape, jnp.int32),
            pltpu.VMEM(mortars.shape, jnp.int32),
            pltpu.SemaphoreType.DMA((3,)),
        ],
        flops=10_000_000_000,
        moved=4_000_000,
    )
    far = lax.ppermute(pack, "leaf", pairs_two)
    one = lax.ppermute(pack, "leaf", pairs_one)
    chosen = call(
        choose_kernel,
        [shapes[name] for name in CHOSEN],
        [vmem] * 3,
        (place, pack, neighbours),
    )
    *made, partial, scaled = call(
        first_kernel,
        [shapes[name] for name in MADE] + [rows, rows],
        [vmem] * (7 + len(CHOSEN)),
        [place, pack, one, table, nodal_mass, curvature, stiffness, *chosen],
    )
    kept = dict(zip(CHOSEN + MADE, [*chosen, *made]))
    two = lax.ppermute(scaled, "leaf", pairs_two)
    image, send, faces_two, two_fine, two_pick, two_back, two_face, diagonal = call(
        far_kernel,
        [rows, rows, faces, fine, picks, backs, face, rows],
        [vmem] * 10,
        [place, pack, neighbours, far, table, kept["scale"], kept["diagonal"], partial,
         kept["own_back"], kept["face"]],
    )
    one = lax.ppermute(send, "leaf", pairs_one)
    lacked, turned, zero, length = call(
        far_rows_kernel,
        [rows, shape(LANES, leaves), rows, shape(1, LANES)],
        [vmem] * 9,
        [place, pack, neighbours, far, table, kept["scale"], kept["face"], kept["own_pick"],
         image],
        flops=1_000_000_000,
        moved=2_000_000,
    )
    stats = call(
        second_kernel,
        shape(1, LANES),
        [vmem] * (14 + len(CHOSEN) + len(MADE) - 1),
        [table, send, one, two, lacked, image, diagonal, zero, length, faces_two, two_fine, two_pick,
         two_back, two_face] + [kept[name] for name in CHOSEN + MADE[1:]],
    )
    stats = stats + lax.ppermute(stats, "leaf", pairs_one)
    gathered = lax.all_to_all(
        jnp.broadcast_to(stats, (count // 2, LANES)),
        "leaf",
        0,
        0,
        axis_index_groups=[list(range(0, count, 2)), list(range(1, count, 2))],
        tiled=True,
    )
    out = call(final_kernel, shape(*flat.shape), [vmem] * 3, (gathered, flat, turned))
    return out.reshape(cotangent.shape)


def solution(mesh):
    placed = (
        P(None, None, "leaf"),
        P(None, "leaf"),
        P(None, "leaf"),
        P(),
        P("leaf"),
        P(None, "leaf"),
        P(None, "leaf"),
    )
    return jax.shard_map(
        on_device, mesh=mesh, in_specs=placed, out_specs=P(None, None, "leaf"), check_vma=False
    )
```

```python
import jax
import jax.numpy as jnp
import ml_dtypes
import numpy as np
from jax import lax
from jax.experimental import pallas as pl
from jax.experimental.pallas import tpu as pltpu
from jax.sharding import PartitionSpec as P

TAU_WEIGHT = 0.15
EPS_WEIGHT = 0.1
FACES = 6
NODES = 64
LANES = 128
F32 = jnp.float32
BF16 = jnp.bfloat16


def face_tables():
    node_at = np.zeros((6, 16), dtype=np.int64)
    for face_id in range(6):
        for row_pos in range(4):
            for col_pos in range(4):
                coords = [row_pos, col_pos]
                coords.insert(face_id // 2, 3 * (face_id % 2))
                node_at[face_id, 4 * row_pos + col_pos] = (
                    16 * coords[0] + 4 * coords[1] + coords[2]
                )
    points = np.array([-1.0, -1.0 / np.sqrt(5.0), 1.0 / np.sqrt(5.0), 1.0])
    halves = np.zeros((2, 4, 4))
    for half_id in range(2):
        target = (points + 2.0 * half_id - 1.0) / 2.0
        for column in range(4):
            lagrange = np.ones(4)
            for other_id in range(4):
                if other_id != column:
                    lagrange = (
                        lagrange * (target - points[other_id]) / (points[column] - points[other_id])
                    )
            halves[half_id, :, column] = lagrange
    mortar = np.stack([np.kron(halves[quarter // 2], halves[quarter % 2]) for quarter in range(4)])
    return node_at, mortar


def two_parts(table):
    high = table.astype(np.float32).astype(ml_dtypes.bfloat16)
    low = (table - high.astype(np.float64)).astype(np.float32).astype(ml_dtypes.bfloat16)
    return np.concatenate([high, low], axis=-1)


def matrices():
    node_at, mortar = face_tables()
    traces = np.zeros((2 * LANES, 2 * LANES))
    to_fine = np.zeros((4, 2 * LANES, LANES))
    to_coarse = np.zeros((4, 2 * LANES, LANES))
    stay = np.zeros((2 * LANES, LANES))
    square = sum(mortar[quarter].T @ mortar[quarter] for quarter in range(4))
    for face in range(FACES):
        for field in range(2):
            nodes = 64 * field + node_at[face]
            for part in range(2):
                for place in range(16):
                    at = part * LANES + 32 * (face // 2) + 16 * field + place
                    traces[part * LANES + nodes[place], at] = 1.0
                    stay[at, nodes] = -square[:, place]
                    for quarter in range(4):
                        to_fine[quarter, at, nodes] = mortar[quarter][:, place]
                        to_coarse[quarter, at, nodes] = mortar[quarter][place, :]
    return np.concatenate(
        [traces.astype(ml_dtypes.bfloat16)]
        + list(two_parts(to_fine))
        + list(two_parts(to_coarse))
        + [two_parts(stay)],
        axis=0,
    )


TRACES_AT, FINE_AT, COARSE_AT, STAY_AT, TABLE_ROWS = 0, 256, 1280, 2304, 2560


def split(values, axis=1):
    high = values.astype(BF16)
    return jnp.concatenate([high, (values - high.astype(F32)).astype(BF16)], axis=axis)


def dot(left, right):
    return jnp.dot(left, right, preferred_element_type=F32)


def fold(values):
    return values[:, :LANES] + values[:, LANES:]


def pick(index, shape, dim):
    places = lax.broadcasted_iota(jnp.int32, shape, dim).astype(F32).astype(BF16)
    index = jnp.broadcast_to(index.astype(F32), shape).astype(BF16)
    return jnp.where(index == places, jnp.ones(shape, BF16), jnp.zeros(shape, BF16))


def on_axis(face):
    lane = lax.broadcasted_iota(jnp.int32, (1, 2 * LANES), 1)
    axis = jnp.right_shift(face, 1)
    return jnp.where((jnp.right_shift(lane, 5) & 3) == axis, 1.0, 0.0).astype(BF16)


def face_nodes(face):
    lane = lax.broadcasted_iota(jnp.int32, (1, LANES), 1)
    axis = jnp.right_shift(face, 1)
    place = jnp.right_shift(lane, 4 - 2 * axis) & 3
    return jnp.where((place == 3 * (face & 1)) & (face >= 0), 1.0, 0.0)


def opposite(face):
    return jnp.where(face >= 0, face ^ 1, -1)


def fetch(pairs, sems):
    copies = [
        pltpu.make_async_copy(source, target, sems.at[at])
        for at, (source, target) in enumerate(pairs)
    ]
    for copy in copies:
        copy.start()
    return copies


def prep_kernel(cot_hbm, levels_hbm, mortars_hbm, pack_ref, cot_ref, levels_ref, mortars_ref, sems):
    quarters = [pl.ds(32 * at, 32) for at in range(4)]
    pairs = [(cot_hbm.at[rows, :], cot_ref.at[rows, :]) for rows in quarters]
    for copy in fetch(
        pairs + [(levels_hbm, levels_ref), (mortars_hbm, mortars_ref)], sems
    ):
        copy.wait()
    leaves = cot_ref.shape[1]
    scale = jnp.left_shift(jnp.ones_like(levels_ref[...]), levels_ref[...]).astype(F32)
    pack_ref[0:leaves, :] = (cot_ref[...] * scale).T
    table = mortars_ref[...].astype(F32) + 1.0
    halves = [scale[:, k * table.shape[1] : (k + 1) * table.shape[1]] for k in range(2)]
    pack_ref[leaves : leaves + 8, :] = jnp.concatenate([table] + halves, axis=0)


CHOSEN = (
    "own", "one", "own_fine", "one_fine", "own_pick", "own_back", "fine_back", "face",
)
MADE = ("diagonal", "stiff", "mass", "curve", "scale", "one_pick", "one_back", "one_face")


def across_faces(seen):
    leaves = seen.shape[0] // FACES
    result = jnp.zeros((leaves, LANES), F32)
    for f in range(FACES):
        shift = 3 * 4 ** (2 - f // 2)
        part = fold(seen[leaves * f : leaves * (f + 1), :])
        part = pltpu.roll(part, shift if f % 2 else LANES - shift, 1)
        result = result + face_nodes(jnp.int32(f)) * part
    return result


def side_traces(chosen, faces, table):
    nodes = jnp.concatenate([face_nodes(face).astype(BF16) for face in faces], axis=0)
    axes = jnp.concatenate([on_axis(face) for face in faces], axis=0)
    nodes = jnp.concatenate([nodes, nodes], axis=1)
    trace = dot(chosen.astype(BF16) * nodes, table[TRACES_AT : TRACES_AT + 256, :])
    return trace.astype(BF16) * axes


def lift(trace, faces, table):
    mask = jnp.concatenate([face_nodes(opposite(face)) for face in faces], axis=0)
    return [
        split(mask * fold(dot(trace, table[FINE_AT + 256 * q : FINE_AT + 256 * (q + 1), :])))
        for q in range(4)
    ]


def lower(traces, face, table, last):
    back = dot(jnp.concatenate(traces, axis=1), table[COARSE_AT:last, :])
    return split(face_nodes(face) * fold(back))


def from_blocks(parts, faces, fine, picks, backs, coarse_faces, face, own_back, table, own):
    slots = own_back.shape[1]
    rows = jnp.concatenate(parts, axis=0)
    chosen = [dot(jnp.concatenate(fine, axis=1), rows)]
    chosen += [dot(pick_rows, part) for pick_rows, part in zip(picks, parts)]
    trace = side_traces(
        jnp.concatenate(chosen, axis=0), [opposite(face)] * 4 + coarse_faces, table
    )
    quarters = [trace[slots * q : slots * (q + 1), :] for q in range(4)]
    if own:
        quarters.append(trace[4 * slots : 5 * slots, :])
    back = lower(quarters, face, table, TABLE_ROWS if own else STAY_AT)
    seen = dot(jnp.concatenate(faces, axis=1), rows)
    sent = lift(trace[4 * slots :, :], coarse_faces, table)
    ordered = [
        sent[q][slots * k : slots * (k + 1), :] for k in range(len(parts)) for q in range(4)
    ]
    mortars = dot(
        jnp.concatenate(backs + [own_back], axis=1), jnp.concatenate(ordered + [back], axis=0)
    )
    mortars = fold(mortars)
    seen = across_faces(seen)
    return mortars + seen


def placed(lapped):
    first = lax.broadcasted_iota(jnp.int32, lapped.shape, 1) < NODES
    return jnp.where(first, -EPS_WEIGHT, TAU_WEIGHT) * pltpu.roll(lapped, NODES, 1)


def fine_count(backs, faces):
    weights = [face_nodes(opposite(face)).astype(BF16) for face in faces for _ in range(4)]
    return dot(jnp.concatenate(backs, axis=1), jnp.concatenate(weights, axis=0))


def own_index(index, offset):
    return jnp.where(index < 0, -1, index - offset)


def to_columns(table):
    return table.astype(F32).T.astype(jnp.int32)


def fine_backs(table, offset, leaves):
    index = own_index(table, offset)
    return jnp.concatenate(
        [pick(index[2 + q : 3 + q, :], (leaves, table.shape[1]), 0) for q in range(4)], axis=1
    )


def choose(refs, kinds, columns, neighbours, leaves):
    slots = columns.shape[0]
    for faces_ref, fine_ref, start, own in kinds:
        index = own_index(neighbours, start)
        across = index if own else to_columns(index)
        for f in range(FACES):
            refs[faces_ref][leaves * f : leaves * (f + 1), :] = (
                pick(across[f ^ 1 : (f ^ 1) + 1, :], (leaves, leaves), 0)
                if own
                else pick(across[:, f : f + 1], (leaves, leaves), 1)
            )
        fine = own_index(columns, start)
        for q in range(4):
            refs[fine_ref][slots * q : slots * (q + 1), :] = pick(
                fine[:, 2 + q : 3 + q], (slots, leaves), 1
            )


def read_tables(pack_ref, leaves):
    table = pack_ref[leaves : leaves + 8, :]
    columns = table.T
    scale = jnp.concatenate([columns[:, 6:7], columns[:, 7:8]], axis=0)
    return table.astype(jnp.int32) - 1, columns.astype(jnp.int32) - 1, scale


def pad_rows(neighbours):
    return jnp.concatenate(
        [neighbours, jnp.full((2, neighbours.shape[1]), -1, jnp.int32)], axis=0
    )


def choose_kernel(place_ref, pack_ref, neighbours_ref, *refs):
    made = dict(zip(CHOSEN, refs))
    leaves = pack_ref.shape[0] - 8
    offset, first = place_ref[0:1, 0:1], place_ref[0:1, 1:2]
    mortars, columns, _ = read_tables(pack_ref, leaves)
    slots = mortars.shape[1]
    made["face"][...] = columns[:, 1:2]
    made["fine_back"][...] = fine_backs(mortars, offset, leaves)
    made["own_back"][...] = pick(mortars[0:1, :] - offset, (leaves, slots), 0)
    made["own_pick"][...] = pick(columns[:, 0:1] - offset, (slots, leaves), 1)
    kinds = (("own", "own_fine", offset, True), ("one", "one_fine", offset + first, False))
    choose(made, kinds, columns, pad_rows(neighbours_ref[...]), leaves)


def image_of(vector, lapped, kept):
    swapped = pltpu.roll(vector, NODES, 1)
    return kept["mass"][...] * vector + kept["curve"][...] * swapped + placed(lapped)


def first_kernel(
    place_ref, pack_ref, other_ref, table, mass_ref, curve_ref, stiffness_ref, *refs
):
    kept = dict(zip(CHOSEN + MADE, refs))
    image_ref, far_ref = refs[len(CHOSEN) + len(MADE) :]
    leaves = pack_ref.shape[0] - 8
    offset, first = place_ref[0:1, 0:1], place_ref[0:1, 1:2]
    mortars, columns, _ = read_tables(other_ref, leaves)
    slots = mortars.shape[1]
    face, other_face = kept["face"][...], columns[:, 1:2]
    other_pick = pick(columns[:, 0:1] - (offset + first), (slots, leaves), 1)
    other_back = fine_backs(mortars, offset, leaves)
    kept["one_pick"][...] = other_pick
    kept["one_back"][...] = other_back
    kept["one_face"][...] = other_face
    back = kept["fine_back"][...]
    diagonal = (
        fine_count([back, other_back], [face, other_face])
        + sum(face_nodes(jnp.int32(f)) for f in range(FACES))
    )
    kept["diagonal"][...] = diagonal
    wide = jnp.concatenate([stiffness_ref[...]] * 2, axis=1)
    wide = jnp.concatenate([wide, wide], axis=0)
    same = (lax.broadcasted_iota(jnp.int32, wide.shape, 0) < NODES) == (
        lax.broadcasted_iota(jnp.int32, wide.shape, 1) < NODES
    )
    wide = split(jnp.where(same, wide, 0.0))
    wide = jnp.concatenate([wide, wide], axis=0)
    kept["stiff"][...] = wide
    both = jnp.concatenate([mass_ref[...], curve_ref[...]], axis=0).T
    turned = pltpu.roll(both, NODES, 1)
    low = lax.broadcasted_iota(jnp.int32, (1, LANES), 1) < NODES
    kept["mass"][...] = jnp.where(low, both, turned)
    kept["curve"][...] = jnp.where(low, -turned, 0.0)
    scale = jnp.broadcast_to(read_tables(pack_ref, leaves)[2], both.shape)
    kept["scale"][...] = scale
    rows = pack_ref[0:leaves, :]
    parts = [split(rows), split(other_ref[0:leaves, :])]
    lapped = diagonal * rows + fold(dot(parts[0], wide)) - from_blocks(
        parts,
        [kept["own"][...], kept["one"][...]],
        [kept["own_fine"][...], kept["one_fine"][...]],
        [kept["own_pick"][...], other_pick],
        [back, other_back],
        [face, other_face],
        face,
        kept["own_back"][...],
        table,
        True,
    )
    image = image_of(rows / scale, lapped, kept)
    image_ref[...] = image
    far_ref[...] = image * scale


def far_kernel(
    place_ref, pack_ref, neighbours_ref, far_ref, table, scale_ref, diagonal_ref, partial_ref,
    own_back_ref, face_ref, image_ref, send_ref, two_ref, two_fine_ref, pick_ref, back_ref,
    far_face_ref, total_ref
):
    leaves = pack_ref.shape[0] - 8
    offset = place_ref[0:1, 0:1]
    start = offset - place_ref[0:1, 1:2]
    _, columns, _ = read_tables(pack_ref, leaves)
    neighbours = pad_rows(neighbours_ref[...])
    choose((two_ref, two_fine_ref), ((0, 1, start, False),), columns, neighbours, leaves)
    mortars, columns, _ = read_tables(far_ref, leaves)
    slots = mortars.shape[1]
    face = columns[:, 1:2]
    chosen = pick(columns[:, 0:1] - start, (slots, leaves), 1)
    back = fine_backs(mortars, offset, leaves)
    pick_ref[...] = chosen
    back_ref[...] = back
    far_face_ref[...] = face
    extra = fine_count([back], [face])
    total_ref[...] = diagonal_ref[...] + extra
    lapped = extra * pack_ref[0:leaves, :] - from_blocks(
        [split(far_ref[0:leaves, :])], [two_ref[...]], [two_fine_ref[...]], [chosen], [back],
        [face], face_ref[...], own_back_ref[...], table, False,
    )
    image = partial_ref[...] + placed(lapped)
    image_ref[...] = image
    send_ref[...] = image * scale_ref[...]


def far_rows_kernel(
    place_ref, pack_ref, neighbours_ref, far_ref, table, scale_ref, face_ref, own_pick_ref,
    image_ref, rows_ref, turned_ref, zero_ref, length_ref
):
    leaves = pack_ref.shape[0] - 8
    offset = place_ref[0:1, 0:1]
    far = offset - place_ref[0:1, 1:2]
    rows = pack_ref[0:leaves, :]
    parts = split(rows)
    index = own_index(pad_rows(neighbours_ref[...]), far)
    face = face_ref[...]
    mortars, _, _ = read_tables(pack_ref, leaves)
    far_mortars, columns, scale = read_tables(far_ref, leaves)
    slots = mortars.shape[1]
    far_face = columns[:, 1:2]
    fine = own_index(columns, offset)
    chosen = [pick(fine[:, 2 + q : 3 + q], (slots, leaves), 1) for q in range(4)]
    chosen = dot(jnp.concatenate(chosen + [own_pick_ref[...]], axis=0), parts)
    trace = side_traces(chosen, [opposite(far_face)] * 4 + [face], table)
    quarters = [trace[slots * q : slots * (q + 1), :] for q in range(4)]
    lowered = lower(quarters, far_face, table, STAY_AT)
    seen = jnp.concatenate(
        [dot(pick(index[f ^ 1 : (f ^ 1) + 1, :], (leaves, leaves), 0), parts) for f in range(FACES)],
        axis=0,
    )
    sent = lift(trace[4 * slots :, :], [face], table) + [lowered]
    back = fine_backs(mortars, far, leaves)
    extra = fine_count([back], [face])
    backs = [back, pick(far_mortars[0:1, :] - far, (leaves, slots), 0)]
    mortars = dot(jnp.concatenate(backs, axis=1), jnp.concatenate(sent, axis=0))
    lapped = extra * far_ref[0:leaves, :] - across_faces(seen) - fold(mortars)
    rows_ref[...] = scale * placed(lapped)
    turned_ref[...] = image_ref[...].T
    length, zero = unit(rows / scale_ref[...])
    zero_ref[...] = zero
    length_ref[...] = jnp.broadcast_to(length, length_ref.shape)


def total(values):
    return jnp.sum(values, keepdims=True)


def unit(values):
    length = jnp.sqrt(total(values * values))
    return length, values * jnp.where(length > 0.0, 1.0 / jnp.where(length > 0.0, length, 1.0), 0.0)


def in_lanes(shape, values):
    lane = lax.broadcasted_iota(jnp.int32, shape, 1)
    row = jnp.zeros(shape, F32)
    for at, value in enumerate(values):
        row = jnp.where(lane == at, value, row)
    return row


def second_kernel(
    table, send_ref, one_ref, two_ref, lacked_ref, image_ref, total_ref, zero_ref, length_ref, faces_two_ref,
    two_fine_ref, two_pick_ref, two_back_ref, two_face_ref, *refs
):
    kept = dict(zip(CHOSEN + MADE[1:], refs))
    stats_ref = refs[len(CHOSEN) + len(MADE) - 1]
    image, zero = image_ref[...], zero_ref[...]
    r01 = total(zero * image)
    rest = image - r01 * zero
    again = total(zero * rest)
    r11, one = unit(rest - again * zero)
    rows = send_ref[...]
    parts = [split(rows), split(one_ref[...]), split(two_ref[...] + lacked_ref[...])]
    face = kept["face"][...]
    lapped = total_ref[...] * rows + fold(dot(parts[0], kept["stiff"][...])) - from_blocks(
        parts,
        [kept["own"][...], kept["one"][...], faces_two_ref[...]],
        [kept["own_fine"][...], kept["one_fine"][...], two_fine_ref[...]],
        [kept["own_pick"][...], kept["one_pick"][...], two_pick_ref[...]],
        [kept["fine_back"][...], kept["one_back"][...], two_back_ref[...]],
        [face, kept["one_face"][...], two_face_ref[...]],
        face,
        kept["own_back"][...],
        table,
        True,
    )
    image = image_of(image, lapped, kept)
    r02 = total(zero * image)
    r12 = total(one * image)
    rest = image - r02 * zero - r12 * one
    r22 = jnp.sqrt(total(rest * rest))
    values = (length_ref[0:1, 0:1], r01 + again, r11, r02, r12, r22)
    stats_ref[...] = in_lanes(stats_ref.shape, values)


def final_kernel(stats_ref, cot_ref, image_ref, out_ref):
    table = stats_ref[...].T
    a0, a1, b1, a2, b2, c2 = [table[at : at + 1, :] for at in range(6)]
    r00_sq = total(a0 * a0)
    r00 = jnp.sqrt(r00_sq)
    f01 = total(a0 * a1) / r00_sq
    f02 = total(a0 * a2) / r00_sq
    a1 = a1 - f01 * a0
    a2 = a2 - f02 * a0
    r11_sq = total(a1 * a1) + total(b1 * b1)
    r11 = jnp.sqrt(r11_sq)
    f12 = (total(a1 * a2) + total(b1 * b2)) / r11_sq
    a2 = a2 - f12 * a1
    b2 = b2 - f12 * b1
    r22 = jnp.sqrt(total(a2 * a2) + total(b2 * b2) + total(c2 * c2))
    rhs_norm = r00
    first_diag = f01
    first_below = r11 / r00
    upper_right = (f02 - first_diag * f01) / first_below
    second_diag = f12 - first_diag
    second_below = r22 / r11
    first_len = jnp.sqrt(first_diag * first_diag + first_below * first_below)
    cos_one = first_diag / first_len
    sin_one = first_below / first_len
    rotated_top = cos_one * upper_right + sin_one * second_diag
    rotated_low = cos_one * second_diag - sin_one * upper_right
    second_len = jnp.sqrt(rotated_low * rotated_low + second_below * second_below)
    cos_two = rotated_low / second_len
    y_two = cos_two * (-sin_one * rhs_norm) / second_len
    y_one = (cos_one * rhs_norm - rotated_top * y_two) / first_len
    on_one = y_two / r11
    on_base = y_one / r00 - on_one * f01
    out_ref[...] = on_base * cot_ref[...] + on_one * image_ref[...]


def on_device(cotangent, nodal_mass, curvature, stiffness, levels, neighbours, mortars):
    fields, nodes, leaves = cotangent.shape
    slots = mortars.shape[1]
    count = lax.axis_size("leaf")
    flat = cotangent.reshape(fields * nodes, leaves)
    levels = levels.reshape(1, leaves)
    me = lax.axis_index("leaf").astype(jnp.int32)
    place = jnp.stack([me * leaves, leaves - 2 * leaves * (me & 1)]).reshape(1, 2)
    table = jnp.asarray(matrices())
    vmem = pl.BlockSpec(memory_space=pltpu.VMEM)
    hbm = pl.BlockSpec(memory_space=pltpu.HBM)

    def call(kernel, outs, specs, operands, scratch=(), flops=0, moved=0, mib=40):
        return pl.pallas_call(
            kernel,
            out_shape=outs,
            in_specs=specs,
            out_specs=jax.tree.map(lambda _: vmem, outs),
            scratch_shapes=scratch,
            compiler_params=pltpu.CompilerParams(vmem_limit_bytes=mib * 1024 * 1024),
            cost_estimate=pl.CostEstimate(flops=flops, bytes_accessed=moved, transcendentals=0),
        )(*operands)

    def shape(*dims, dtype=F32):
        return jax.ShapeDtypeStruct(dims, dtype)

    pairs_one = [(i, i ^ 1) for i in range(count) if i ^ 1 < count]
    pairs_two = [(i, i + 1) for i in range(1, count - 1, 2)]
    pairs_two = pairs_two + [(j, i) for i, j in pairs_two]

    wide = 2 * LANES
    rows = shape(leaves, LANES)
    faces = shape(FACES * leaves, leaves, dtype=BF16)
    fine = shape(4 * slots, leaves, dtype=BF16)
    picks = shape(slots, leaves, dtype=BF16)
    backs = shape(leaves, 4 * slots, dtype=BF16)
    face = shape(slots, 1, dtype=jnp.int32)
    shapes = dict(
        own=faces,
        one=faces,
        own_fine=fine,
        one_fine=fine,
        own_pick=picks,
        own_back=shape(leaves, slots, dtype=BF16),
        fine_back=backs,
        face=face,
        diagonal=rows,
        stiff=shape(wide, wide, dtype=BF16),
        mass=rows,
        curve=rows,
        scale=rows,
        one_pick=picks,
        one_back=backs,
        one_face=face,
    )

    def stay_out(*arrays):
        return tuple(pltpu.with_memory_space_constraint(array, pltpu.HBM) for array in arrays)

    pack = call(
        prep_kernel,
        shape(leaves + 8, LANES),
        [hbm] * 3,
        stay_out(flat, levels, mortars),
        scratch=[
            pltpu.VMEM(flat.shape, F32),
            pltpu.VMEM(levels.shape, jnp.int32),
            pltpu.VMEM(mortars.shape, jnp.int32),
            pltpu.SemaphoreType.DMA((6,)),
        ],
        flops=10_000_000_000,
        moved=4_000_000,
    )
    far = lax.ppermute(pack, "leaf", pairs_two)
    one = lax.ppermute(pack, "leaf", pairs_one)
    chosen = call(
        choose_kernel,
        [shapes[name] for name in CHOSEN],
        [vmem] * 3,
        (place, pack, neighbours),
    )
    *made, partial, scaled = call(
        first_kernel,
        [shapes[name] for name in MADE] + [rows, rows],
        [vmem] * (7 + len(CHOSEN)),
        [place, pack, one, table, nodal_mass, curvature, stiffness, *chosen],
    )
    kept = dict(zip(CHOSEN + MADE, [*chosen, *made]))
    two = lax.ppermute(scaled, "leaf", pairs_two)
    image, send, faces_two, two_fine, two_pick, two_back, two_face, diagonal = call(
        far_kernel,
        [rows, rows, faces, fine, picks, backs, face, rows],
        [vmem] * 10,
        [place, pack, neighbours, far, table, kept["scale"], kept["diagonal"], partial,
         kept["own_back"], kept["face"]],
    )
    one = lax.ppermute(send, "leaf", pairs_one)
    lacked, turned, zero, length = call(
        far_rows_kernel,
        [rows, shape(LANES, leaves), rows, shape(1, LANES)],
        [vmem] * 9,
        [place, pack, neighbours, far, table, kept["scale"], kept["face"], kept["own_pick"],
         image],
        flops=1_000_000_000,
        moved=2_000_000,
    )
    stats = call(
        second_kernel,
        shape(1, LANES),
        [vmem] * (14 + len(CHOSEN) + len(MADE) - 1),
        [table, send, one, two, lacked, image, diagonal, zero, length, faces_two, two_fine, two_pick,
         two_back, two_face] + [kept[name] for name in CHOSEN + MADE[1:]],
    )
    gathered = lax.all_to_all(
        jnp.broadcast_to(stats, (count, LANES)), "leaf", 0, 0, tiled=True
    )
    out = call(final_kernel, shape(*flat.shape), [vmem] * 3, (gathered, flat, turned))
    return out.reshape(cotangent.shape)


def solution(mesh):
    placed = (
        P(None, None, "leaf"),
        P(None, "leaf"),
        P(None, "leaf"),
        P(),
        P("leaf"),
        P(None, "leaf"),
        P(None, "leaf"),
    )
    return jax.shard_map(
        on_device, mesh=mesh, in_specs=placed, out_specs=P(None, None, "leaf"), check_vma=False
    )
```

```python
import jax
import jax.numpy as jnp
import ml_dtypes
import numpy as np
from jax import lax
from jax.experimental import pallas as pl
from jax.experimental.pallas import tpu as pltpu
from jax.sharding import PartitionSpec as P

TAU_WEIGHT = 0.15
EPS_WEIGHT = 0.1
FACES = 6
NODES = 64
LANES = 128
F32 = jnp.float32
BF16 = jnp.bfloat16


def face_tables():
    node_at = np.zeros((6, 16), dtype=np.int64)
    for face_id in range(6):
        for row_pos in range(4):
            for col_pos in range(4):
                coords = [row_pos, col_pos]
                coords.insert(face_id // 2, 3 * (face_id % 2))
                node_at[face_id, 4 * row_pos + col_pos] = (
                    16 * coords[0] + 4 * coords[1] + coords[2]
                )
    points = np.array([-1.0, -1.0 / np.sqrt(5.0), 1.0 / np.sqrt(5.0), 1.0])
    halves = np.zeros((2, 4, 4))
    for half_id in range(2):
        target = (points + 2.0 * half_id - 1.0) / 2.0
        for column in range(4):
            lagrange = np.ones(4)
            for other_id in range(4):
                if other_id != column:
                    lagrange = (
                        lagrange * (target - points[other_id]) / (points[column] - points[other_id])
                    )
            halves[half_id, :, column] = lagrange
    mortar = np.stack([np.kron(halves[quarter // 2], halves[quarter % 2]) for quarter in range(4)])
    return node_at, mortar


def two_parts(table):
    high = table.astype(np.float32).astype(ml_dtypes.bfloat16)
    low = (table - high.astype(np.float64)).astype(np.float32).astype(ml_dtypes.bfloat16)
    return np.concatenate([high, low], axis=-1)


def matrices():
    node_at, mortar = face_tables()
    traces = np.zeros((2 * LANES, 2 * LANES))
    to_fine = np.zeros((4, 2 * LANES, LANES))
    to_coarse = np.zeros((4, 2 * LANES, LANES))
    stay = np.zeros((2 * LANES, LANES))
    square = sum(mortar[quarter].T @ mortar[quarter] for quarter in range(4))
    for face in range(FACES):
        for field in range(2):
            nodes = 64 * field + node_at[face]
            for part in range(2):
                for place in range(16):
                    at = part * LANES + 32 * (face // 2) + 16 * field + place
                    traces[part * LANES + nodes[place], at] = 1.0
                    stay[at, nodes] = -square[:, place]
                    for quarter in range(4):
                        to_fine[quarter, at, nodes] = mortar[quarter][:, place]
                        to_coarse[quarter, at, nodes] = mortar[quarter][place, :]
    return np.concatenate(
        [traces.astype(ml_dtypes.bfloat16)]
        + list(two_parts(to_fine))
        + list(two_parts(to_coarse))
        + [two_parts(stay)],
        axis=0,
    )


TRACES_AT, FINE_AT, COARSE_AT, STAY_AT, TABLE_ROWS = 0, 256, 1280, 2304, 2560


def split(values, axis=1):
    high = values.astype(BF16)
    return jnp.concatenate([high, (values - high.astype(F32)).astype(BF16)], axis=axis)


def dot(left, right):
    return jnp.dot(left, right, preferred_element_type=F32)


def fold(values):
    return values[:, :LANES] + values[:, LANES:]


def pick(index, shape, dim):
    places = lax.broadcasted_iota(jnp.int32, shape, dim).astype(F32).astype(BF16)
    index = jnp.broadcast_to(index.astype(F32), shape).astype(BF16)
    return jnp.where(index == places, jnp.ones(shape, BF16), jnp.zeros(shape, BF16))


def on_axis(face):
    lane = lax.broadcasted_iota(jnp.int32, (1, 2 * LANES), 1)
    axis = jnp.right_shift(face, 1)
    return jnp.where((jnp.right_shift(lane, 5) & 3) == axis, 1.0, 0.0).astype(BF16)


def face_nodes(face):
    lane = lax.broadcasted_iota(jnp.int32, (1, LANES), 1)
    axis = jnp.right_shift(face, 1)
    place = jnp.right_shift(lane, 4 - 2 * axis) & 3
    return jnp.where((place == 3 * (face & 1)) & (face >= 0), 1.0, 0.0)


def opposite(face):
    return jnp.where(face >= 0, face ^ 1, -1)


def fetch(pairs, sems):
    copies = [
        pltpu.make_async_copy(source, target, sems.at[at])
        for at, (source, target) in enumerate(pairs)
    ]
    for copy in copies:
        copy.start()
    return copies


def prep_kernel(
    cot_hbm, levels_hbm, mortars_hbm, pack_ref, wide_ref, cot_ref, levels_ref, mortars_ref, sems
):
    quarters = [pl.ds(32 * at, 32) for at in range(4)]
    pairs = [(cot_hbm.at[rows, :], cot_ref.at[rows, :]) for rows in quarters]
    for copy in fetch(
        pairs + [(levels_hbm, levels_ref), (mortars_hbm, mortars_ref)], sems
    ):
        copy.wait()
    leaves = cot_ref.shape[1]
    scale = jnp.left_shift(jnp.ones_like(levels_ref[...]), levels_ref[...]).astype(F32)
    pack_ref[0:leaves, :] = (cot_ref[...] * scale).T
    table = mortars_ref[...].astype(F32) + 1.0
    halves = [scale[:, k * table.shape[1] : (k + 1) * table.shape[1]] for k in range(2)]
    pack_ref[leaves : leaves + 8, :] = jnp.concatenate([table] + halves, axis=0)
    wide_ref[0 : leaves + 8, :] = pack_ref[...]
    wide_ref[leaves + 8 :, :] = jnp.zeros((8, LANES), F32)


CHOSEN = (
    "own", "one", "own_fine", "one_fine", "own_pick", "own_back", "fine_back", "face",
)
MADE = ("diagonal", "stiff", "mass", "curve", "scale", "one_pick", "one_back", "one_face")


def across_faces(seen):
    leaves = seen.shape[0] // FACES
    result = jnp.zeros((leaves, LANES), F32)
    for f in range(FACES):
        shift = 3 * 4 ** (2 - f // 2)
        part = fold(seen[leaves * f : leaves * (f + 1), :])
        part = pltpu.roll(part, shift if f % 2 else LANES - shift, 1)
        result = result + face_nodes(jnp.int32(f)) * part
    return result


def side_traces(chosen, faces, table):
    nodes = jnp.concatenate([face_nodes(face).astype(BF16) for face in faces], axis=0)
    axes = jnp.concatenate([on_axis(face) for face in faces], axis=0)
    nodes = jnp.concatenate([nodes, nodes], axis=1)
    trace = dot(chosen.astype(BF16) * nodes, table[TRACES_AT : TRACES_AT + 256, :])
    return trace.astype(BF16) * axes


def lift(trace, faces, table):
    mask = jnp.concatenate([face_nodes(opposite(face)) for face in faces], axis=0)
    return [
        split(mask * fold(dot(trace, table[FINE_AT + 256 * q : FINE_AT + 256 * (q + 1), :])))
        for q in range(4)
    ]


def lower(traces, face, table, last):
    back = dot(jnp.concatenate(traces, axis=1), table[COARSE_AT:last, :])
    return split(face_nodes(face) * fold(back))


def from_blocks(parts, faces, fine, picks, backs, coarse_faces, face, own_back, table, own):
    slots = own_back.shape[1]
    rows = jnp.concatenate(parts, axis=0)
    chosen = [dot(jnp.concatenate(fine, axis=1), rows)]
    chosen += [dot(pick_rows, part) for pick_rows, part in zip(picks, parts)]
    trace = side_traces(
        jnp.concatenate(chosen, axis=0), [opposite(face)] * 4 + coarse_faces, table
    )
    quarters = [trace[slots * q : slots * (q + 1), :] for q in range(4)]
    if own:
        quarters.append(trace[4 * slots : 5 * slots, :])
    back = lower(quarters, face, table, TABLE_ROWS if own else STAY_AT)
    seen = dot(jnp.concatenate(faces, axis=1), rows)
    sent = lift(trace[4 * slots :, :], coarse_faces, table)
    ordered = [
        sent[q][slots * k : slots * (k + 1), :] for k in range(len(parts)) for q in range(4)
    ]
    mortars = dot(
        jnp.concatenate(backs + [own_back], axis=1), jnp.concatenate(ordered + [back], axis=0)
    )
    mortars = fold(mortars)
    seen = across_faces(seen)
    return mortars + seen


def placed(lapped):
    first = lax.broadcasted_iota(jnp.int32, lapped.shape, 1) < NODES
    return jnp.where(first, -EPS_WEIGHT, TAU_WEIGHT) * pltpu.roll(lapped, NODES, 1)


def fine_count(backs, faces):
    weights = [face_nodes(opposite(face)).astype(BF16) for face in faces for _ in range(4)]
    return dot(jnp.concatenate(backs, axis=1), jnp.concatenate(weights, axis=0))


def own_index(index, offset):
    return jnp.where(index < 0, -1, index - offset)


def to_columns(table):
    return table.astype(F32).T.astype(jnp.int32)


def fine_backs(table, offset, leaves):
    index = own_index(table, offset)
    return jnp.concatenate(
        [pick(index[2 + q : 3 + q, :], (leaves, table.shape[1]), 0) for q in range(4)], axis=1
    )


def choose(refs, kinds, columns, neighbours, leaves):
    slots = columns.shape[0]
    for faces_ref, fine_ref, start, own in kinds:
        index = own_index(neighbours, start)
        across = index if own else to_columns(index)
        for f in range(FACES):
            refs[faces_ref][leaves * f : leaves * (f + 1), :] = (
                pick(across[f ^ 1 : (f ^ 1) + 1, :], (leaves, leaves), 0)
                if own
                else pick(across[:, f : f + 1], (leaves, leaves), 1)
            )
        fine = own_index(columns, start)
        for q in range(4):
            refs[fine_ref][slots * q : slots * (q + 1), :] = pick(
                fine[:, 2 + q : 3 + q], (slots, leaves), 1
            )


def read_tables(pack_ref, leaves):
    table = pack_ref[leaves : leaves + 8, :]
    columns = table.T
    scale = jnp.concatenate([columns[:, 6:7], columns[:, 7:8]], axis=0)
    return table.astype(jnp.int32) - 1, columns.astype(jnp.int32) - 1, scale


def pad_rows(neighbours):
    return jnp.concatenate(
        [neighbours, jnp.full((2, neighbours.shape[1]), -1, jnp.int32)], axis=0
    )


def choose_kernel(place_ref, pack_ref, neighbours_ref, *refs):
    made = dict(zip(CHOSEN, refs))
    leaves = pack_ref.shape[0] - 8
    offset, first = place_ref[0:1, 0:1], place_ref[0:1, 1:2]
    mortars, columns, _ = read_tables(pack_ref, leaves)
    slots = mortars.shape[1]
    made["face"][...] = columns[:, 1:2]
    made["fine_back"][...] = fine_backs(mortars, offset, leaves)
    made["own_back"][...] = pick(mortars[0:1, :] - offset, (leaves, slots), 0)
    made["own_pick"][...] = pick(columns[:, 0:1] - offset, (slots, leaves), 1)
    kinds = (("own", "own_fine", offset, True), ("one", "one_fine", offset + first, False))
    choose(made, kinds, columns, pad_rows(neighbours_ref[...]), leaves)


def image_of(vector, lapped, kept):
    swapped = pltpu.roll(vector, NODES, 1)
    return kept["mass"][...] * vector + kept["curve"][...] * swapped + placed(lapped)


def first_kernel(
    place_ref, pack_ref, other_ref, table, mass_ref, curve_ref, stiffness_ref, *refs
):
    kept = dict(zip(CHOSEN + MADE, refs))
    image_ref, far_ref = refs[len(CHOSEN) + len(MADE) :]
    leaves = pack_ref.shape[0] - 8
    offset, first = place_ref[0:1, 0:1], place_ref[0:1, 1:2]
    mortars, columns, _ = read_tables(other_ref, leaves)
    slots = mortars.shape[1]
    face, other_face = kept["face"][...], columns[:, 1:2]
    other_pick = pick(columns[:, 0:1] - (offset + first), (slots, leaves), 1)
    other_back = fine_backs(mortars, offset, leaves)
    kept["one_pick"][...] = other_pick
    kept["one_back"][...] = other_back
    kept["one_face"][...] = other_face
    back = kept["fine_back"][...]
    diagonal = (
        fine_count([back, other_back], [face, other_face])
        + sum(face_nodes(jnp.int32(f)) for f in range(FACES))
    )
    kept["diagonal"][...] = diagonal
    wide = jnp.concatenate([stiffness_ref[...]] * 2, axis=1)
    wide = jnp.concatenate([wide, wide], axis=0)
    same = (lax.broadcasted_iota(jnp.int32, wide.shape, 0) < NODES) == (
        lax.broadcasted_iota(jnp.int32, wide.shape, 1) < NODES
    )
    wide = split(jnp.where(same, wide, 0.0))
    wide = jnp.concatenate([wide, wide], axis=0)
    kept["stiff"][...] = wide
    both = jnp.concatenate([mass_ref[...], curve_ref[...]], axis=0).T
    turned = pltpu.roll(both, NODES, 1)
    low = lax.broadcasted_iota(jnp.int32, (1, LANES), 1) < NODES
    kept["mass"][...] = jnp.where(low, both, turned)
    kept["curve"][...] = jnp.where(low, -turned, 0.0)
    scale = jnp.broadcast_to(read_tables(pack_ref, leaves)[2], both.shape)
    kept["scale"][...] = scale
    rows = pack_ref[0:leaves, :]
    parts = [split(rows), split(other_ref[0:leaves, :])]
    lapped = diagonal * rows + fold(dot(parts[0], wide)) - from_blocks(
        parts,
        [kept["own"][...], kept["one"][...]],
        [kept["own_fine"][...], kept["one_fine"][...]],
        [kept["own_pick"][...], other_pick],
        [back, other_back],
        [face, other_face],
        face,
        kept["own_back"][...],
        table,
        True,
    )
    image = image_of(rows / scale, lapped, kept)
    image_ref[...] = image
    far_ref[...] = image * scale


def far_kernel(
    place_ref, pack_ref, neighbours_ref, far_ref, table, scale_ref, diagonal_ref, partial_ref,
    own_back_ref, face_ref, image_ref, send_ref, two_ref, two_fine_ref, pick_ref, back_ref,
    far_face_ref, total_ref
):
    leaves = pack_ref.shape[0] - 8
    offset = place_ref[0:1, 0:1]
    start = offset - place_ref[0:1, 1:2]
    _, columns, _ = read_tables(pack_ref, leaves)
    neighbours = pad_rows(neighbours_ref[...])
    choose((two_ref, two_fine_ref), ((0, 1, start, False),), columns, neighbours, leaves)
    mortars, columns, _ = read_tables(far_ref, leaves)
    slots = mortars.shape[1]
    face = columns[:, 1:2]
    chosen = pick(columns[:, 0:1] - start, (slots, leaves), 1)
    back = fine_backs(mortars, offset, leaves)
    pick_ref[...] = chosen
    back_ref[...] = back
    far_face_ref[...] = face
    extra = fine_count([back], [face])
    total_ref[...] = diagonal_ref[...] + extra
    lapped = extra * pack_ref[0:leaves, :] - from_blocks(
        [split(far_ref[0:leaves, :])], [two_ref[...]], [two_fine_ref[...]], [chosen], [back],
        [face], face_ref[...], own_back_ref[...], table, False,
    )
    image = partial_ref[...] + placed(lapped)
    image_ref[...] = image
    send_ref[...] = image * scale_ref[...]


def far_rows_kernel(
    place_ref, pack_ref, neighbours_ref, far_ref, table, scale_ref, face_ref, own_pick_ref,
    image_ref, rows_ref, turned_ref, zero_ref, length_ref
):
    leaves = pack_ref.shape[0] - 8
    offset = place_ref[0:1, 0:1]
    far = offset - place_ref[0:1, 1:2]
    rows = pack_ref[0:leaves, :]
    parts = split(rows)
    index = own_index(pad_rows(neighbours_ref[...]), far)
    face = face_ref[...]
    mortars, _, _ = read_tables(pack_ref, leaves)
    far_mortars, columns, scale = read_tables(far_ref, leaves)
    slots = mortars.shape[1]
    far_face = columns[:, 1:2]
    fine = own_index(columns, offset)
    chosen = [pick(fine[:, 2 + q : 3 + q], (slots, leaves), 1) for q in range(4)]
    chosen = dot(jnp.concatenate(chosen + [own_pick_ref[...]], axis=0), parts)
    trace = side_traces(chosen, [opposite(far_face)] * 4 + [face], table)
    quarters = [trace[slots * q : slots * (q + 1), :] for q in range(4)]
    lowered = lower(quarters, far_face, table, STAY_AT)
    seen = jnp.concatenate(
        [dot(pick(index[f ^ 1 : (f ^ 1) + 1, :], (leaves, leaves), 0), parts) for f in range(FACES)],
        axis=0,
    )
    sent = lift(trace[4 * slots :, :], [face], table) + [lowered]
    back = fine_backs(mortars, far, leaves)
    extra = fine_count([back], [face])
    backs = [back, pick(far_mortars[0:1, :] - far, (leaves, slots), 0)]
    mortars = dot(jnp.concatenate(backs, axis=1), jnp.concatenate(sent, axis=0))
    lapped = extra * far_ref[0:leaves, :] - across_faces(seen) - fold(mortars)
    rows_ref[...] = scale * placed(lapped)
    turned_ref[...] = image_ref[...].T
    length, zero = unit(rows / scale_ref[...])
    zero_ref[...] = zero
    length_ref[...] = jnp.broadcast_to(length, length_ref.shape)


def total(values):
    return jnp.sum(values, keepdims=True)


def unit(values):
    length = jnp.sqrt(total(values * values))
    return length, values * jnp.where(length > 0.0, 1.0 / jnp.where(length > 0.0, length, 1.0), 0.0)


def in_lanes(shape, values):
    lane = lax.broadcasted_iota(jnp.int32, shape, 1)
    row = jnp.zeros(shape, F32)
    for at, value in enumerate(values):
        row = jnp.where(lane == at, value, row)
    return row


def second_kernel(
    table, send_ref, one_ref, two_ref, lacked_ref, image_ref, total_ref, zero_ref, length_ref, faces_two_ref,
    two_fine_ref, two_pick_ref, two_back_ref, two_face_ref, *refs
):
    kept = dict(zip(CHOSEN + MADE[1:], refs))
    stats_ref = refs[len(CHOSEN) + len(MADE) - 1]
    image, zero = image_ref[...], zero_ref[...]
    r01 = total(zero * image)
    rest = image - r01 * zero
    again = total(zero * rest)
    r11, one = unit(rest - again * zero)
    rows = send_ref[...]
    parts = [split(rows), split(one_ref[...]), split(two_ref[...] + lacked_ref[...])]
    face = kept["face"][...]
    lapped = total_ref[...] * rows + fold(dot(parts[0], kept["stiff"][...])) - from_blocks(
        parts,
        [kept["own"][...], kept["one"][...], faces_two_ref[...]],
        [kept["own_fine"][...], kept["one_fine"][...], two_fine_ref[...]],
        [kept["own_pick"][...], kept["one_pick"][...], two_pick_ref[...]],
        [kept["fine_back"][...], kept["one_back"][...], two_back_ref[...]],
        [face, kept["one_face"][...], two_face_ref[...]],
        face,
        kept["own_back"][...],
        table,
        True,
    )
    image = image_of(image, lapped, kept)
    r02 = total(zero * image)
    r12 = total(one * image)
    rest = image - r02 * zero - r12 * one
    r22 = jnp.sqrt(total(rest * rest))
    values = (length_ref[0:1, 0:1], r01 + again, r11, r02, r12, r22)
    stats_ref[...] = in_lanes(stats_ref.shape, values)


def final_kernel(stats_ref, cot_ref, image_ref, out_ref):
    table = stats_ref[...].T
    a0, a1, b1, a2, b2, c2 = [table[at : at + 1, :] for at in range(6)]
    r00_sq = total(a0 * a0)
    r00 = jnp.sqrt(r00_sq)
    f01 = total(a0 * a1) / r00_sq
    f02 = total(a0 * a2) / r00_sq
    a1 = a1 - f01 * a0
    a2 = a2 - f02 * a0
    r11_sq = total(a1 * a1) + total(b1 * b1)
    r11 = jnp.sqrt(r11_sq)
    f12 = (total(a1 * a2) + total(b1 * b2)) / r11_sq
    a2 = a2 - f12 * a1
    b2 = b2 - f12 * b1
    r22 = jnp.sqrt(total(a2 * a2) + total(b2 * b2) + total(c2 * c2))
    rhs_norm = r00
    first_diag = f01
    first_below = r11 / r00
    upper_right = (f02 - first_diag * f01) / first_below
    second_diag = f12 - first_diag
    second_below = r22 / r11
    first_len = jnp.sqrt(first_diag * first_diag + first_below * first_below)
    cos_one = first_diag / first_len
    sin_one = first_below / first_len
    rotated_top = cos_one * upper_right + sin_one * second_diag
    rotated_low = cos_one * second_diag - sin_one * upper_right
    second_len = jnp.sqrt(rotated_low * rotated_low + second_below * second_below)
    cos_two = rotated_low / second_len
    y_two = cos_two * (-sin_one * rhs_norm) / second_len
    y_one = (cos_one * rhs_norm - rotated_top * y_two) / first_len
    on_one = y_two / r11
    on_base = y_one / r00 - on_one * f01
    out_ref[...] = on_base * cot_ref[...] + on_one * image_ref[...]


def on_device(cotangent, nodal_mass, curvature, stiffness, levels, neighbours, mortars):
    fields, nodes, leaves = cotangent.shape
    slots = mortars.shape[1]
    count = lax.axis_size("leaf")
    flat = cotangent.reshape(fields * nodes, leaves)
    levels = levels.reshape(1, leaves)
    me = lax.axis_index("leaf").astype(jnp.int32)
    place = jnp.stack([me * leaves, leaves - 2 * leaves * (me & 1)]).reshape(1, 2)
    table = jnp.asarray(matrices())
    vmem = pl.BlockSpec(memory_space=pltpu.VMEM)
    hbm = pl.BlockSpec(memory_space=pltpu.HBM)

    def call(kernel, outs, specs, operands, scratch=(), flops=0, moved=0, mib=40):
        return pl.pallas_call(
            kernel,
            out_shape=outs,
            in_specs=specs,
            out_specs=jax.tree.map(lambda _: vmem, outs),
            scratch_shapes=scratch,
            compiler_params=pltpu.CompilerParams(vmem_limit_bytes=mib * 1024 * 1024),
            cost_estimate=pl.CostEstimate(flops=flops, bytes_accessed=moved, transcendentals=0),
        )(*operands)

    def shape(*dims, dtype=F32):
        return jax.ShapeDtypeStruct(dims, dtype)

    pairs_one = [(i, i ^ 1) for i in range(count) if i ^ 1 < count]
    pairs_two = [(i, i + 1) for i in range(1, count - 1, 2)]
    pairs_two = pairs_two + [(j, i) for i, j in pairs_two]

    wide = 2 * LANES
    rows = shape(leaves, LANES)
    faces = shape(FACES * leaves, leaves, dtype=BF16)
    fine = shape(4 * slots, leaves, dtype=BF16)
    picks = shape(slots, leaves, dtype=BF16)
    backs = shape(leaves, 4 * slots, dtype=BF16)
    face = shape(slots, 1, dtype=jnp.int32)
    shapes = dict(
        own=faces,
        one=faces,
        own_fine=fine,
        one_fine=fine,
        own_pick=picks,
        own_back=shape(leaves, slots, dtype=BF16),
        fine_back=backs,
        face=face,
        diagonal=rows,
        stiff=shape(wide, wide, dtype=BF16),
        mass=rows,
        curve=rows,
        scale=rows,
        one_pick=picks,
        one_back=backs,
        one_face=face,
    )

    def stay_out(*arrays):
        return tuple(pltpu.with_memory_space_constraint(array, pltpu.HBM) for array in arrays)

    pack, wide = call(
        prep_kernel,
        [shape(leaves + 8, LANES), shape(leaves + 16, LANES)],
        [hbm] * 3,
        stay_out(flat, levels, mortars),
        scratch=[
            pltpu.VMEM(flat.shape, F32),
            pltpu.VMEM(levels.shape, jnp.int32),
            pltpu.VMEM(mortars.shape, jnp.int32),
            pltpu.SemaphoreType.DMA((6,)),
        ],
        flops=10_000_000_000,
        moved=4_000_000,
    )
    far = lax.ppermute(wide, "leaf", pairs_two)
    one = lax.ppermute(pack, "leaf", pairs_one)
    chosen = call(
        choose_kernel,
        [shapes[name] for name in CHOSEN],
        [vmem] * 3,
        (place, pack, neighbours),
    )
    *made, partial, scaled = call(
        first_kernel,
        [shapes[name] for name in MADE] + [rows, rows],
        [vmem] * (7 + len(CHOSEN)),
        [place, pack, one, table, nodal_mass, curvature, stiffness, *chosen],
    )
    kept = dict(zip(CHOSEN + MADE, [*chosen, *made]))
    two = lax.ppermute(scaled, "leaf", pairs_two)
    image, send, faces_two, two_fine, two_pick, two_back, two_face, diagonal = call(
        far_kernel,
        [rows, rows, faces, fine, picks, backs, face, rows],
        [vmem] * 10,
        [place, pack, neighbours, far, table, kept["scale"], kept["diagonal"], partial,
         kept["own_back"], kept["face"]],
    )
    one = lax.ppermute(send, "leaf", pairs_one)
    lacked, turned, zero, length = call(
        far_rows_kernel,
        [rows, shape(LANES, leaves), rows, shape(1, LANES)],
        [vmem] * 9,
        [place, pack, neighbours, far, table, kept["scale"], kept["face"], kept["own_pick"],
         image],
        flops=1_000_000_000,
        moved=2_000_000,
    )
    stats = call(
        second_kernel,
        shape(1, LANES),
        [vmem] * (14 + len(CHOSEN) + len(MADE) - 1),
        [table, send, one, two, lacked, image, diagonal, zero, length, faces_two, two_fine, two_pick,
         two_back, two_face] + [kept[name] for name in CHOSEN + MADE[1:]],
    )
    gathered = lax.all_to_all(
        jnp.broadcast_to(stats, (count, LANES)), "leaf", 0, 0, tiled=True
    )
    out = call(final_kernel, shape(*flat.shape), [vmem] * 3, (gathered, flat, turned))
    return out.reshape(cotangent.shape)


def solution(mesh):
    placed = (
        P(None, None, "leaf"),
        P(None, "leaf"),
        P(None, "leaf"),
        P(),
        P("leaf"),
        P(None, "leaf"),
        P(None, "leaf"),
    )
    return jax.shard_map(
        on_device, mesh=mesh, in_specs=placed, out_specs=P(None, None, "leaf"), check_vma=False
    )
```

```python
import jax
import jax.numpy as jnp
import ml_dtypes
import numpy as np
from jax import lax
from jax.experimental import pallas as pl
from jax.experimental.pallas import tpu as pltpu
from jax.sharding import PartitionSpec as P

TAU_WEIGHT = 0.15
EPS_WEIGHT = 0.1
FACES = 6
NODES = 64
LANES = 128
F32 = jnp.float32
BF16 = jnp.bfloat16


def face_tables():
    node_at = np.zeros((6, 16), dtype=np.int64)
    for face_id in range(6):
        for row_pos in range(4):
            for col_pos in range(4):
                coords = [row_pos, col_pos]
                coords.insert(face_id // 2, 3 * (face_id % 2))
                node_at[face_id, 4 * row_pos + col_pos] = (
                    16 * coords[0] + 4 * coords[1] + coords[2]
                )
    points = np.array([-1.0, -1.0 / np.sqrt(5.0), 1.0 / np.sqrt(5.0), 1.0])
    halves = np.zeros((2, 4, 4))
    for half_id in range(2):
        target = (points + 2.0 * half_id - 1.0) / 2.0
        for column in range(4):
            lagrange = np.ones(4)
            for other_id in range(4):
                if other_id != column:
                    lagrange = (
                        lagrange * (target - points[other_id]) / (points[column] - points[other_id])
                    )
            halves[half_id, :, column] = lagrange
    mortar = np.stack([np.kron(halves[quarter // 2], halves[quarter % 2]) for quarter in range(4)])
    return node_at, mortar


def two_parts(table):
    high = table.astype(np.float32).astype(ml_dtypes.bfloat16)
    low = (table - high.astype(np.float64)).astype(np.float32).astype(ml_dtypes.bfloat16)
    return np.concatenate([high, low], axis=-1)


def matrices():
    node_at, mortar = face_tables()
    traces = np.zeros((2 * LANES, 2 * LANES))
    to_fine = np.zeros((4, 2 * LANES, LANES))
    to_coarse = np.zeros((4, 2 * LANES, LANES))
    stay = np.zeros((2 * LANES, LANES))
    square = sum(mortar[quarter].T @ mortar[quarter] for quarter in range(4))
    for face in range(FACES):
        for field in range(2):
            nodes = 64 * field + node_at[face]
            for part in range(2):
                for place in range(16):
                    at = part * LANES + 32 * (face // 2) + 16 * field + place
                    traces[part * LANES + nodes[place], at] = 1.0
                    stay[at, nodes] = -square[:, place]
                    for quarter in range(4):
                        to_fine[quarter, at, nodes] = mortar[quarter][:, place]
                        to_coarse[quarter, at, nodes] = mortar[quarter][place, :]
    return np.concatenate(
        [traces.astype(ml_dtypes.bfloat16)]
        + list(two_parts(to_fine))
        + list(two_parts(to_coarse))
        + [two_parts(stay)],
        axis=0,
    )


TRACES_AT, FINE_AT, COARSE_AT, STAY_AT, TABLE_ROWS = 0, 256, 1280, 2304, 2560


def split(values, axis=1):
    high = values.astype(BF16)
    return jnp.concatenate([high, (values - high.astype(F32)).astype(BF16)], axis=axis)


def dot(left, right):
    return jnp.dot(left, right, preferred_element_type=F32)


def fold(values):
    return values[:, :LANES] + values[:, LANES:]


def pick(index, shape, dim):
    places = lax.broadcasted_iota(jnp.int32, shape, dim).astype(F32).astype(BF16)
    index = jnp.broadcast_to(index.astype(F32), shape).astype(BF16)
    return jnp.where(index == places, jnp.ones(shape, BF16), jnp.zeros(shape, BF16))


def on_axis(face):
    lane = lax.broadcasted_iota(jnp.int32, (1, 2 * LANES), 1)
    axis = jnp.right_shift(face, 1)
    return jnp.where((jnp.right_shift(lane, 5) & 3) == axis, 1.0, 0.0).astype(BF16)


def face_nodes(face):
    lane = lax.broadcasted_iota(jnp.int32, (1, LANES), 1)
    axis = jnp.right_shift(face, 1)
    place = jnp.right_shift(lane, 4 - 2 * axis) & 3
    return jnp.where((place == 3 * (face & 1)) & (face >= 0), 1.0, 0.0)


def opposite(face):
    return jnp.where(face >= 0, face ^ 1, -1)


def fetch(pairs, sems):
    copies = [
        pltpu.make_async_copy(source, target, sems.at[at])
        for at, (source, target) in enumerate(pairs)
    ]
    for copy in copies:
        copy.start()
    return copies


def prep_kernel(
    cot_hbm, levels_hbm, mortars_hbm, pack_ref, wide_ref, cot_ref, levels_ref, mortars_ref, sems
):
    quarters = [pl.ds(32 * at, 32) for at in range(4)]
    pairs = [(cot_hbm.at[rows, :], cot_ref.at[rows, :]) for rows in quarters]
    for copy in fetch(
        pairs + [(levels_hbm, levels_ref), (mortars_hbm, mortars_ref)], sems
    ):
        copy.wait()
    leaves = cot_ref.shape[1]
    scale = jnp.left_shift(jnp.ones_like(levels_ref[...]), levels_ref[...]).astype(F32)
    pack_ref[0:leaves, :] = (cot_ref[...] * scale).T
    table = mortars_ref[...].astype(F32) + 1.0
    halves = [scale[:, k * table.shape[1] : (k + 1) * table.shape[1]] for k in range(2)]
    pack_ref[leaves : leaves + 8, :] = jnp.concatenate([table] + halves, axis=0)
    wide_ref[0 : leaves + 8, :] = pack_ref[...]
    wide_ref[leaves + 8 :, :] = jnp.zeros((8, LANES), F32)


CHOSEN = (
    "own", "one", "own_fine", "one_fine", "own_pick", "own_back", "fine_back", "face",
    "stiff", "mass", "curve", "scale",
)
AHEAD = ("two", "two_fine", "count")
MADE = ("diagonal", "one_pick", "one_back", "one_face")


def across_faces(seen):
    leaves = seen.shape[0] // FACES
    result = jnp.zeros((leaves, LANES), F32)
    for f in range(FACES):
        shift = 3 * 4 ** (2 - f // 2)
        part = fold(seen[leaves * f : leaves * (f + 1), :])
        part = pltpu.roll(part, shift if f % 2 else LANES - shift, 1)
        result = result + face_nodes(jnp.int32(f)) * part
    return result


def side_traces(chosen, faces, table):
    nodes = jnp.concatenate([face_nodes(face).astype(BF16) for face in faces], axis=0)
    axes = jnp.concatenate([on_axis(face) for face in faces], axis=0)
    nodes = jnp.concatenate([nodes, nodes], axis=1)
    trace = dot(chosen.astype(BF16) * nodes, table[TRACES_AT : TRACES_AT + 256, :])
    return trace.astype(BF16) * axes


def lift(trace, faces, table):
    mask = jnp.concatenate([face_nodes(opposite(face)) for face in faces], axis=0)
    return [
        split(mask * fold(dot(trace, table[FINE_AT + 256 * q : FINE_AT + 256 * (q + 1), :])))
        for q in range(4)
    ]


def lower(traces, face, table, last):
    back = dot(jnp.concatenate(traces, axis=1), table[COARSE_AT:last, :])
    return split(face_nodes(face) * fold(back))


def from_blocks(parts, faces, fine, picks, backs, coarse_faces, face, own_back, table, own):
    slots = own_back.shape[1]
    rows = jnp.concatenate(parts, axis=0)
    chosen = [dot(jnp.concatenate(fine, axis=1), rows)]
    chosen += [dot(pick_rows, part) for pick_rows, part in zip(picks, parts)]
    trace = side_traces(
        jnp.concatenate(chosen, axis=0), [opposite(face)] * 4 + coarse_faces, table
    )
    quarters = [trace[slots * q : slots * (q + 1), :] for q in range(4)]
    if own:
        quarters.append(trace[4 * slots : 5 * slots, :])
    back = lower(quarters, face, table, TABLE_ROWS if own else STAY_AT)
    seen = dot(jnp.concatenate(faces, axis=1), rows)
    sent = lift(trace[4 * slots :, :], coarse_faces, table)
    ordered = [
        sent[q][slots * k : slots * (k + 1), :] for k in range(len(parts)) for q in range(4)
    ]
    mortars = dot(
        jnp.concatenate(backs + [own_back], axis=1), jnp.concatenate(ordered + [back], axis=0)
    )
    mortars = fold(mortars)
    seen = across_faces(seen)
    return mortars + seen


def placed(lapped):
    first = lax.broadcasted_iota(jnp.int32, lapped.shape, 1) < NODES
    return jnp.where(first, -EPS_WEIGHT, TAU_WEIGHT) * pltpu.roll(lapped, NODES, 1)


def fine_count(backs, faces):
    weights = [face_nodes(opposite(face)).astype(BF16) for face in faces for _ in range(4)]
    return dot(jnp.concatenate(backs, axis=1), jnp.concatenate(weights, axis=0))


def own_index(index, offset):
    return jnp.where(index < 0, -1, index - offset)


def to_columns(table):
    return table.astype(F32).T.astype(jnp.int32)


def fine_backs(table, offset, leaves):
    index = own_index(table, offset)
    return jnp.concatenate(
        [pick(index[2 + q : 3 + q, :], (leaves, table.shape[1]), 0) for q in range(4)], axis=1
    )


def choose(refs, kinds, columns, neighbours, leaves):
    slots = columns.shape[0]
    for faces_ref, fine_ref, start, own in kinds:
        index = own_index(neighbours, start)
        across = index if own else to_columns(index)
        for f in range(FACES):
            refs[faces_ref][leaves * f : leaves * (f + 1), :] = (
                pick(across[f ^ 1 : (f ^ 1) + 1, :], (leaves, leaves), 0)
                if own
                else pick(across[:, f : f + 1], (leaves, leaves), 1)
            )
        fine = own_index(columns, start)
        for q in range(4):
            refs[fine_ref][slots * q : slots * (q + 1), :] = pick(
                fine[:, 2 + q : 3 + q], (slots, leaves), 1
            )


def read_tables(pack_ref, leaves):
    table = pack_ref[leaves : leaves + 8, :]
    columns = table.T
    scale = jnp.concatenate([columns[:, 6:7], columns[:, 7:8]], axis=0)
    return table.astype(jnp.int32) - 1, columns.astype(jnp.int32) - 1, scale


def pad_rows(neighbours):
    return jnp.concatenate(
        [neighbours, jnp.full((2, neighbours.shape[1]), -1, jnp.int32)], axis=0
    )


def choose_kernel(
    place_ref, pack_ref, neighbours_ref, mass_ref, curve_ref, stiffness_ref, *refs
):
    made = dict(zip(CHOSEN + AHEAD, refs))
    leaves = pack_ref.shape[0] - 8
    offset, first = place_ref[0:1, 0:1], place_ref[0:1, 1:2]
    mortars, columns, _ = read_tables(pack_ref, leaves)
    slots = mortars.shape[1]
    made["face"][...] = columns[:, 1:2]
    made["fine_back"][...] = fine_backs(mortars, offset, leaves)
    made["own_back"][...] = pick(mortars[0:1, :] - offset, (leaves, slots), 0)
    made["own_pick"][...] = pick(columns[:, 0:1] - offset, (slots, leaves), 1)
    kinds = (
        ("own", "own_fine", offset, True),
        ("one", "one_fine", offset + first, False),
        ("two", "two_fine", offset - first, False),
    )
    choose(made, kinds, columns, pad_rows(neighbours_ref[...]), leaves)
    made["count"][...] = fine_count([made["fine_back"][...]], [columns[:, 1:2]]) + sum(
        face_nodes(jnp.int32(f)) for f in range(FACES)
    )
    wide = jnp.concatenate([stiffness_ref[...]] * 2, axis=1)
    wide = jnp.concatenate([wide, wide], axis=0)
    same = (lax.broadcasted_iota(jnp.int32, wide.shape, 0) < NODES) == (
        lax.broadcasted_iota(jnp.int32, wide.shape, 1) < NODES
    )
    wide = split(jnp.where(same, wide, 0.0))
    wide = jnp.concatenate([wide, wide], axis=0)
    made["stiff"][...] = wide
    both = jnp.concatenate([mass_ref[...], curve_ref[...]], axis=0).T
    turned = pltpu.roll(both, NODES, 1)
    low = lax.broadcasted_iota(jnp.int32, (1, LANES), 1) < NODES
    made["mass"][...] = jnp.where(low, both, turned)
    made["curve"][...] = jnp.where(low, -turned, 0.0)
    scale = jnp.broadcast_to(read_tables(pack_ref, leaves)[2], both.shape)
    made["scale"][...] = scale


def image_of(vector, lapped, kept):
    swapped = pltpu.roll(vector, NODES, 1)
    return kept["mass"][...] * vector + kept["curve"][...] * swapped + placed(lapped)


def first_kernel(
    place_ref, pack_ref, other_ref, table, count_ref, *refs
):
    kept = dict(zip(CHOSEN + MADE, refs))
    image_ref, far_ref = refs[len(CHOSEN) + len(MADE) :]
    leaves = pack_ref.shape[0] - 8
    offset, first = place_ref[0:1, 0:1], place_ref[0:1, 1:2]
    mortars, columns, _ = read_tables(other_ref, leaves)
    slots = mortars.shape[1]
    face, other_face = kept["face"][...], columns[:, 1:2]
    other_pick = pick(columns[:, 0:1] - (offset + first), (slots, leaves), 1)
    other_back = fine_backs(mortars, offset, leaves)
    kept["one_pick"][...] = other_pick
    kept["one_back"][...] = other_back
    kept["one_face"][...] = other_face
    back = kept["fine_back"][...]
    diagonal = count_ref[...] + fine_count([other_back], [other_face])
    kept["diagonal"][...] = diagonal
    scale = kept["scale"][...]
    rows = pack_ref[0:leaves, :]
    parts = [split(rows), split(other_ref[0:leaves, :])]
    lapped = diagonal * rows + fold(dot(parts[0], kept["stiff"][...])) - from_blocks(
        parts,
        [kept["own"][...], kept["one"][...]],
        [kept["own_fine"][...], kept["one_fine"][...]],
        [kept["own_pick"][...], other_pick],
        [back, other_back],
        [face, other_face],
        face,
        kept["own_back"][...],
        table,
        True,
    )
    image = image_of(rows / scale, lapped, kept)
    image_ref[...] = image
    far_ref[...] = image * scale


def far_kernel(
    place_ref, pack_ref, far_ref, table, scale_ref, diagonal_ref, partial_ref, own_back_ref,
    face_ref, two_ref, two_fine_ref, image_ref, send_ref, pick_ref, back_ref, far_face_ref,
    total_ref
):
    leaves = pack_ref.shape[0] - 8
    offset = place_ref[0:1, 0:1]
    start = offset - place_ref[0:1, 1:2]
    mortars, columns, _ = read_tables(far_ref, leaves)
    slots = mortars.shape[1]
    face = columns[:, 1:2]
    chosen = pick(columns[:, 0:1] - start, (slots, leaves), 1)
    back = fine_backs(mortars, offset, leaves)
    pick_ref[...] = chosen
    back_ref[...] = back
    far_face_ref[...] = face
    extra = fine_count([back], [face])
    total_ref[...] = diagonal_ref[...] + extra
    lapped = extra * pack_ref[0:leaves, :] - from_blocks(
        [split(far_ref[0:leaves, :])], [two_ref[...]], [two_fine_ref[...]], [chosen], [back],
        [face], face_ref[...], own_back_ref[...], table, False,
    )
    image = partial_ref[...] + placed(lapped)
    image_ref[...] = image
    send_ref[...] = image * scale_ref[...]


def far_rows_kernel(
    place_ref, pack_ref, neighbours_ref, far_ref, table, scale_ref, face_ref, own_pick_ref,
    image_ref, rows_ref, turned_ref, zero_ref, length_ref
):
    leaves = pack_ref.shape[0] - 8
    offset = place_ref[0:1, 0:1]
    far = offset - place_ref[0:1, 1:2]
    rows = pack_ref[0:leaves, :]
    parts = split(rows)
    index = own_index(pad_rows(neighbours_ref[...]), far)
    face = face_ref[...]
    mortars, _, _ = read_tables(pack_ref, leaves)
    far_mortars, columns, scale = read_tables(far_ref, leaves)
    slots = mortars.shape[1]
    far_face = columns[:, 1:2]
    fine = own_index(columns, offset)
    chosen = [pick(fine[:, 2 + q : 3 + q], (slots, leaves), 1) for q in range(4)]
    chosen = dot(jnp.concatenate(chosen + [own_pick_ref[...]], axis=0), parts)
    trace = side_traces(chosen, [opposite(far_face)] * 4 + [face], table)
    quarters = [trace[slots * q : slots * (q + 1), :] for q in range(4)]
    lowered = lower(quarters, far_face, table, STAY_AT)
    seen = jnp.concatenate(
        [dot(pick(index[f ^ 1 : (f ^ 1) + 1, :], (leaves, leaves), 0), parts) for f in range(FACES)],
        axis=0,
    )
    sent = lift(trace[4 * slots :, :], [face], table) + [lowered]
    back = fine_backs(mortars, far, leaves)
    extra = fine_count([back], [face])
    backs = [back, pick(far_mortars[0:1, :] - far, (leaves, slots), 0)]
    mortars = dot(jnp.concatenate(backs, axis=1), jnp.concatenate(sent, axis=0))
    lapped = extra * far_ref[0:leaves, :] - across_faces(seen) - fold(mortars)
    rows_ref[...] = scale * placed(lapped)
    turned_ref[...] = image_ref[...].T
    length, zero = unit(rows / scale_ref[...])
    zero_ref[...] = zero
    length_ref[...] = jnp.broadcast_to(length, length_ref.shape)


def total(values):
    return jnp.sum(values, keepdims=True)


def unit(values):
    length = jnp.sqrt(total(values * values))
    return length, values * jnp.where(length > 0.0, 1.0 / jnp.where(length > 0.0, length, 1.0), 0.0)


def in_lanes(shape, values):
    lane = lax.broadcasted_iota(jnp.int32, shape, 1)
    row = jnp.zeros(shape, F32)
    for at, value in enumerate(values):
        row = jnp.where(lane == at, value, row)
    return row


def second_kernel(
    table, send_ref, one_ref, two_ref, lacked_ref, image_ref, total_ref, zero_ref, length_ref, faces_two_ref,
    two_fine_ref, two_pick_ref, two_back_ref, two_face_ref, *refs
):
    kept = dict(zip(CHOSEN + MADE[1:], refs))
    stats_ref = refs[len(CHOSEN) + len(MADE) - 1]
    image, zero = image_ref[...], zero_ref[...]
    r01 = total(zero * image)
    rest = image - r01 * zero
    again = total(zero * rest)
    r11, one = unit(rest - again * zero)
    rows = send_ref[...]
    parts = [split(rows), split(one_ref[...]), split(two_ref[...] + lacked_ref[...])]
    face = kept["face"][...]
    lapped = total_ref[...] * rows + fold(dot(parts[0], kept["stiff"][...])) - from_blocks(
        parts,
        [kept["own"][...], kept["one"][...], faces_two_ref[...]],
        [kept["own_fine"][...], kept["one_fine"][...], two_fine_ref[...]],
        [kept["own_pick"][...], kept["one_pick"][...], two_pick_ref[...]],
        [kept["fine_back"][...], kept["one_back"][...], two_back_ref[...]],
        [face, kept["one_face"][...], two_face_ref[...]],
        face,
        kept["own_back"][...],
        table,
        True,
    )
    image = image_of(image, lapped, kept)
    r02 = total(zero * image)
    r12 = total(one * image)
    rest = image - r02 * zero - r12 * one
    r22 = jnp.sqrt(total(rest * rest))
    values = (length_ref[0:1, 0:1], r01 + again, r11, r02, r12, r22)
    stats_ref[...] = in_lanes(stats_ref.shape, values)


def final_kernel(stats_ref, cot_ref, image_ref, out_ref):
    table = stats_ref[...].T
    a0, a1, b1, a2, b2, c2 = [table[at : at + 1, :] for at in range(6)]
    r00_sq = total(a0 * a0)
    r00 = jnp.sqrt(r00_sq)
    f01 = total(a0 * a1) / r00_sq
    f02 = total(a0 * a2) / r00_sq
    a1 = a1 - f01 * a0
    a2 = a2 - f02 * a0
    r11_sq = total(a1 * a1) + total(b1 * b1)
    r11 = jnp.sqrt(r11_sq)
    f12 = (total(a1 * a2) + total(b1 * b2)) / r11_sq
    a2 = a2 - f12 * a1
    b2 = b2 - f12 * b1
    r22 = jnp.sqrt(total(a2 * a2) + total(b2 * b2) + total(c2 * c2))
    rhs_norm = r00
    first_diag = f01
    first_below = r11 / r00
    upper_right = (f02 - first_diag * f01) / first_below
    second_diag = f12 - first_diag
    second_below = r22 / r11
    first_len = jnp.sqrt(first_diag * first_diag + first_below * first_below)
    cos_one = first_diag / first_len
    sin_one = first_below / first_len
    rotated_top = cos_one * upper_right + sin_one * second_diag
    rotated_low = cos_one * second_diag - sin_one * upper_right
    second_len = jnp.sqrt(rotated_low * rotated_low + second_below * second_below)
    cos_two = rotated_low / second_len
    y_two = cos_two * (-sin_one * rhs_norm) / second_len
    y_one = (cos_one * rhs_norm - rotated_top * y_two) / first_len
    on_one = y_two / r11
    on_base = y_one / r00 - on_one * f01
    out_ref[...] = on_base * cot_ref[...] + on_one * image_ref[...]


def on_device(cotangent, nodal_mass, curvature, stiffness, levels, neighbours, mortars):
    fields, nodes, leaves = cotangent.shape
    slots = mortars.shape[1]
    count = lax.axis_size("leaf")
    flat = cotangent.reshape(fields * nodes, leaves)
    levels = levels.reshape(1, leaves)
    me = lax.axis_index("leaf").astype(jnp.int32)
    place = jnp.stack([me * leaves, leaves - 2 * leaves * (me & 1)]).reshape(1, 2)
    table = jnp.asarray(matrices())
    vmem = pl.BlockSpec(memory_space=pltpu.VMEM)
    hbm = pl.BlockSpec(memory_space=pltpu.HBM)

    def call(kernel, outs, specs, operands, scratch=(), flops=0, moved=0, mib=40):
        return pl.pallas_call(
            kernel,
            out_shape=outs,
            in_specs=specs,
            out_specs=jax.tree.map(lambda _: vmem, outs),
            scratch_shapes=scratch,
            compiler_params=pltpu.CompilerParams(vmem_limit_bytes=mib * 1024 * 1024),
            cost_estimate=pl.CostEstimate(flops=flops, bytes_accessed=moved, transcendentals=0),
        )(*operands)

    def shape(*dims, dtype=F32):
        return jax.ShapeDtypeStruct(dims, dtype)

    pairs_one = [(i, i ^ 1) for i in range(count) if i ^ 1 < count]
    pairs_two = [(i, i + 1) for i in range(1, count - 1, 2)]
    pairs_two = pairs_two + [(j, i) for i, j in pairs_two]

    wide = 2 * LANES
    rows = shape(leaves, LANES)
    faces = shape(FACES * leaves, leaves, dtype=BF16)
    fine = shape(4 * slots, leaves, dtype=BF16)
    picks = shape(slots, leaves, dtype=BF16)
    backs = shape(leaves, 4 * slots, dtype=BF16)
    face = shape(slots, 1, dtype=jnp.int32)
    shapes = dict(
        own=faces,
        one=faces,
        own_fine=fine,
        one_fine=fine,
        own_pick=picks,
        own_back=shape(leaves, slots, dtype=BF16),
        fine_back=backs,
        face=face,
        diagonal=rows,
        stiff=shape(wide, wide, dtype=BF16),
        mass=rows,
        curve=rows,
        scale=rows,
        one_pick=picks,
        one_back=backs,
        one_face=face,
    )

    def stay_out(*arrays):
        return tuple(pltpu.with_memory_space_constraint(array, pltpu.HBM) for array in arrays)

    pack, wide = call(
        prep_kernel,
        [shape(leaves + 8, LANES), shape(leaves + 16, LANES)],
        [hbm] * 3,
        stay_out(flat, levels, mortars),
        scratch=[
            pltpu.VMEM(flat.shape, F32),
            pltpu.VMEM(levels.shape, jnp.int32),
            pltpu.VMEM(mortars.shape, jnp.int32),
            pltpu.SemaphoreType.DMA((6,)),
        ],
        flops=10_000_000_000,
        moved=4_000_000,
    )
    far = lax.ppermute(wide, "leaf", pairs_two)
    one = lax.ppermute(pack, "leaf", pairs_one)
    *chosen, faces_two, two_fine, count_own = call(
        choose_kernel,
        [shapes[name] for name in CHOSEN] + [faces, fine, rows],
        [vmem] * 6,
        (place, pack, neighbours, nodal_mass, curvature, stiffness),
    )
    *made, partial, scaled = call(
        first_kernel,
        [shapes[name] for name in MADE] + [rows, rows],
        [vmem] * (5 + len(CHOSEN)),
        [place, pack, one, table, count_own, *chosen],
    )
    kept = dict(zip(CHOSEN + MADE, [*chosen, *made]))
    two = lax.ppermute(scaled, "leaf", pairs_two)
    image, send, two_pick, two_back, two_face, diagonal = call(
        far_kernel,
        [rows, rows, picks, backs, face, rows],
        [vmem] * 11,
        [place, pack, far, table, kept["scale"], kept["diagonal"], partial, kept["own_back"],
         kept["face"], faces_two, two_fine],
    )
    one = lax.ppermute(send, "leaf", pairs_one)
    lacked, turned, zero, length = call(
        far_rows_kernel,
        [rows, shape(LANES, leaves), rows, shape(1, LANES)],
        [vmem] * 9,
        [place, pack, neighbours, far, table, kept["scale"], kept["face"], kept["own_pick"],
         image],
        flops=1_000_000_000,
        moved=2_000_000,
    )
    stats = call(
        second_kernel,
        shape(1, LANES),
        [vmem] * (14 + len(CHOSEN) + len(MADE) - 1),
        [table, send, one, two, lacked, image, diagonal, zero, length, faces_two, two_fine, two_pick,
         two_back, two_face] + [kept[name] for name in CHOSEN + MADE[1:]],
    )
    gathered = lax.all_to_all(
        jnp.broadcast_to(stats, (count, LANES)), "leaf", 0, 0, tiled=True
    )
    out = call(final_kernel, shape(*flat.shape), [vmem] * 3, (gathered, flat, turned))
    return out.reshape(cotangent.shape)


def solution(mesh):
    placed = (
        P(None, None, "leaf"),
        P(None, "leaf"),
        P(None, "leaf"),
        P(),
        P("leaf"),
        P(None, "leaf"),
        P(None, "leaf"),
    )
    return jax.shard_map(
        on_device, mesh=mesh, in_specs=placed, out_specs=P(None, None, "leaf"), check_vma=False
    )
```
